32 devices in a mesh: chain: 16 (over z, y, x), block: 2 (over core).
Axes of the slice: x: 2, y: 2, z: 4, core: 2. Of those that a mesh axis runs over, the one named last changes fastest.
Arguments:
- site_tensors: bfloat16 [16, 32, 2, 256, 256], P('chain', 'block'), may hold values from -4.5 to 7.5
- sketch: bfloat16 [512, 256], replicated, may hold values from -6 to 6
- bond_sizes: int32 [16, 2, 32], P('chain'), may hold values from 32 to 256, as said below
- kept_ranks: int32 [16, 2, 32], P('chain'), may hold values from 0 to 256, as said below
- couplings: float32 [16, 2, 3], P('chain'), may hold values from -1 to 2.5, as said below
Outputs:
- updated_sites: bfloat16 [16, 32, 2, 256, 256], P('chain', 'block')
The draws below stay inside these ranges and needn't reach their ends.
Inputs may be any that keep to these rules, and one draw needn't show every extreme that they name: bond_sizes[i, 1] are the block sizes of the bond right of site i and bond_sizes[i, 0] equals bond_sizes[i - 1 mod 16, 1]; every bond has a block of exactly 256. kept_ranks[i, 1] belongs to the bond right of site i and kept_ranks[i, 0] equals kept_ranks[i - 1 mod 16, 1]; a count never exceeds that block's size; some block keeps exactly 256. couplings[i, 0] equals couplings[i - 1 mod 16, 1]; hopping lies in 0.5 to 2.5, the other two in -1 to 1.
All inputs are finite; a program needn't handle non-finite values.
Results may differ from the reference program's by a relative error of at most 0.035.
Values may be sent and summed in bfloat16 or wider, within the bound.
No kernel may reach another device: no remote copies, remote signals or barrier semaphores. Data moves between devices by JAX's collectives and lax.ppermute only.
A program may use at most 128 MiB of HBM per device.

```python
import jax
import jax.numpy as jnp
from jax import lax

P_SIZE = 256
SECTORS = 32
RMAX = 256
SITES = 16


def pair_sum_down(values):
    return values + jnp.concatenate([jnp.zeros((values.shape[0], 1), jnp.int32), values[:, :-1]], axis=1)


def pair_sum_up(values):
    return values + jnp.concatenate([values[:, 1:], jnp.zeros((values.shape[0], 1), jnp.int32)], axis=1)


def bond_layout(key):
    base_key = jax.random.fold_in(key, 7)
    key_center, key_slope, key_cap = jax.random.split(base_key, 3)
    center = jax.random.randint(key_center, (), 1, SECTORS - 1)
    slope_step = jax.random.randint(key_slope, (SITES, 1), 1 + P_SIZE // 64, 2 + P_SIZE // 10)
    sector = jnp.arange(SECTORS, dtype=jnp.int32)[None, :]
    distance = jnp.maximum(jnp.abs(sector - center) - 1, 0)
    block_sizes = jnp.maximum(max(1, P_SIZE // 8), P_SIZE - slope_step * distance).astype(jnp.int32)
    rank_cap = jax.random.randint(key_cap, (SITES, SECTORS), RMAX // 2, RMAX + 1)
    rank_cap = jnp.where(sector == center, RMAX, rank_cap).astype(jnp.int32)
    previous = jnp.roll(block_sizes, 1, axis=0)
    following = jnp.roll(block_sizes, -1, axis=0)
    rank_bound = jnp.minimum(block_sizes, jnp.minimum(pair_sum_down(previous), pair_sum_up(following)) // 2)
    even_rank = jnp.minimum(rank_cap, rank_bound)
    rank_prev = jnp.roll(even_rank, 1, axis=0)
    rank_next = jnp.roll(even_rank, -1, axis=0)
    odd_bound = jnp.minimum(block_sizes, jnp.minimum(pair_sum_down(rank_prev), pair_sum_up(rank_next)) // 2)
    odd_rank = jnp.minimum(rank_cap, odd_bound)
    is_even = jnp.arange(SITES, dtype=jnp.int32)[:, None] % 2 == 0
    bond_rank = jnp.where(is_even, even_rank, odd_rank).astype(jnp.int32)
    return (block_sizes, bond_rank)


def draw_bond_sizes(key, part):
    block_sizes, bond_rank = bond_layout(key)
    return jnp.stack([jnp.roll(block_sizes, 1, axis=0), block_sizes], axis=1)


def draw_kept_ranks(key, part):
    block_sizes, bond_rank = bond_layout(key)
    return jnp.stack([jnp.roll(bond_rank, 1, axis=0), bond_rank], axis=1)


def draw_couplings(key, part):
    uniform_draw = jax.random.uniform(jax.random.fold_in(key, 11), (SITES, 3), jnp.float32)
    lower_end = jnp.array([0.5, -1.0, -1.0], jnp.float32)
    upper_end = jnp.array([2.5, 1.0, 1.0], jnp.float32)
    bond_terms = lower_end + (upper_end - lower_end) * uniform_draw
    return jnp.stack([jnp.roll(bond_terms, 1, axis=0), bond_terms], axis=1)


def draw_site_tensors(key, part):
    block_sizes, bond_rank = bond_layout(key)
    left_sizes = jnp.roll(block_sizes, 1, axis=0)
    right_next = jnp.concatenate([block_sizes[:, 1:], jnp.zeros((SITES, 1), jnp.int32)], axis=1)
    noise_draw = jax.random.normal(jax.random.fold_in(key, 13), (SITES, SECTORS, 2, P_SIZE, P_SIZE), jnp.float32)
    noise_draw = jnp.clip(noise_draw, -5.0, 5.0)
    extent_zero = jnp.maximum(jnp.maximum(left_sizes, block_sizes), 1).astype(jnp.float32)
    extent_one = jnp.maximum(jnp.maximum(left_sizes, right_next), 1).astype(jnp.float32)
    extent = jnp.stack([extent_zero, extent_one], axis=2)
    spread = 0.9 / jnp.sqrt(extent)
    diagonal = 3.0 * jnp.eye(P_SIZE, dtype=jnp.float32)
    return (diagonal + spread[..., None, None] * noise_draw).astype(jnp.bfloat16)


def scatter_about(key, shape, scale, bound, held_as=jnp.bfloat16):
    drawn = scale * jax.random.normal(key, shape, jnp.float32)
    return jnp.clip(drawn, min=-bound, max=bound).astype(held_as)


def setup_inputs(seed: int = 0) -> dict:
    key_of = jax.random.split(jax.random.key(seed), 6)
    return {
        "site_tensors": draw_site_tensors(jax.random.fold_in(key_of[5], 71), 0),
        "sketch": scatter_about(key_of[1], (2 * P_SIZE, RMAX), 1.0, 6.0),
        "bond_sizes": draw_bond_sizes(jax.random.fold_in(key_of[5], 71), 0),
        "kept_ranks": draw_kept_ranks(jax.random.fold_in(key_of[5], 71), 0),
        "couplings": draw_couplings(jax.random.fold_in(key_of[5], 71), 0),
    }


tau_step = 0.5

def gate_terms(coupling):
    hopping = coupling[0]
    ising_term = coupling[1]
    field_term = coupling[2]
    rotation = 0.5 * tau_step * hopping
    middle_scale = jnp.exp(0.25 * tau_step * ising_term)
    weight_empty = jnp.exp(-tau_step * (0.25 * ising_term - 0.5 * field_term))
    weight_full = jnp.exp(-tau_step * (0.25 * ising_term + 0.5 * field_term))
    weight_stay = middle_scale * jnp.cosh(rotation)
    weight_swap = -middle_scale * jnp.sinh(rotation)
    return (weight_empty, weight_stay, weight_swap, weight_full)

def mask_site(site_block, left_sizes, right_sizes):
    row_index = jnp.arange(P_SIZE, dtype=jnp.int32)
    right_next = jnp.concatenate([right_sizes[1:], jnp.zeros((1,), jnp.int32)])
    row_keep = row_index[None, :] < left_sizes[:, None]
    col_stay = row_index[None, :] < right_sizes[:, None]
    col_next = row_index[None, :] < right_next[:, None]
    keep_zero = row_keep[:, :, None] & col_stay[:, None, :]
    keep_one = row_keep[:, :, None] & col_next[:, None, :]
    keep_both = jnp.stack([keep_zero, keep_one], axis=1)
    return jnp.where(keep_both, site_block, jnp.zeros_like(site_block))

def widen(values):
    return values.astype(jnp.float32)

def round_product(left_part, right_part):
    return jnp.einsum('kij,kjl->kil', widen(left_part), widen(right_part)).astype(jnp.bfloat16)

def pair_update(left_site, right_site, mid_ranks, coupling, sketch):
    zero_block = jnp.zeros((1, P_SIZE, P_SIZE), jnp.bfloat16)
    left_zero = left_site[:, 0]
    left_one = left_site[:, 1]
    right_zero = right_site[:, 0]
    right_one = right_site[:, 1]
    left_below = jnp.concatenate([zero_block, left_one[:-1]], axis=0)
    stay_stay = round_product(left_zero, right_zero)
    stay_up = round_product(left_zero, right_one)
    up_stay = round_product(left_below, right_zero)
    up_up = round_product(left_below, right_one)
    up_stay_next = jnp.concatenate([up_stay[1:], zero_block], axis=0)
    stay_up_prev = jnp.concatenate([zero_block, stay_up[:-1]], axis=0)
    weight_empty, weight_stay, weight_swap, weight_full = gate_terms(coupling)
    top_left = weight_empty * widen(stay_stay)
    top_right = weight_stay * widen(stay_up) + weight_swap * widen(up_stay_next)
    bottom_left = weight_swap * widen(stay_up_prev) + weight_stay * widen(up_stay)
    bottom_right = weight_full * widen(up_up)
    two_site = jnp.concatenate([jnp.concatenate([top_left, top_right], axis=2), jnp.concatenate([bottom_left, bottom_right], axis=2)], axis=1).astype(jnp.bfloat16)
    sample = jnp.einsum('kab,bc->kac', widen(two_site), widen(sketch))
    keep_mask = (jnp.arange(RMAX, dtype=jnp.int32)[None, :] < mid_ranks[:, None]).astype(jnp.float32)
    sample = sample * keep_mask[:, None, :]
    gram_matrix = jnp.einsum('kai,kaj->kij', sample, sample, precision=lax.Precision.HIGHEST)
    gram_matrix = gram_matrix + (1.0 - keep_mask)[:, :, None] * jnp.eye(RMAX, dtype=jnp.float32)[None]
    factor = jnp.linalg.cholesky(gram_matrix)
    solved = lax.linalg.triangular_solve(factor, sample, left_side=False, lower=True, transpose_a=True)
    basis_rows = (solved * jnp.sqrt(jnp.float32(P_SIZE))).astype(jnp.bfloat16)
    coef = jnp.einsum('kar,kab->krb', widen(basis_rows), widen(two_site))
    norm_total = jnp.sum(coef * coef)
    scaled = (coef * jnp.sqrt(jnp.float32(SECTORS * RMAX * P_SIZE) / norm_total)).astype(jnp.bfloat16)
    pad_count = P_SIZE - RMAX
    new_zero = jnp.pad(basis_rows[:, :P_SIZE, :], ((0, 0), (0, 0), (0, pad_count)))
    lower_part = jnp.pad(basis_rows[:, P_SIZE:, :], ((0, 0), (0, 0), (0, pad_count)))
    new_one = jnp.concatenate([lower_part[1:], zero_block], axis=0)
    new_left = jnp.stack([new_zero, new_one], axis=1)
    right_zero_new = jnp.pad(scaled[:, :, :P_SIZE], ((0, 0), (0, pad_count), (0, 0)))
    right_one_new = jnp.pad(scaled[:, :, P_SIZE:], ((0, 0), (0, pad_count), (0, 0)))
    new_right = jnp.stack([right_zero_new, right_one_new], axis=1)
    return (new_left, new_right)

def run_layer(current, left_index, right_index, kept_ranks, couplings, sketch):

    def update_pair(packed):
        left_site, right_site, mid_ranks, coupling = packed
        return pair_update(left_site, right_site, mid_ranks, coupling, sketch)
    new_left, new_right = lax.map(update_pair, (current[left_index], current[right_index], kept_ranks[left_index, 1], couplings[left_index, 1]))
    current = current.at[left_index].set(new_left)
    return current.at[right_index].set(new_right)

def reference(site_tensors, sketch, bond_sizes, kept_ranks, couplings):
    current = jax.vmap(mask_site)(site_tensors, bond_sizes[:, 0], bond_sizes[:, 1])
    even_left = jnp.arange(0, SITES, 2, dtype=jnp.int32)
    current = run_layer(current, even_left, even_left + 1, kept_ranks, couplings, sketch)
    odd_left = jnp.arange(1, SITES, 2, dtype=jnp.int32)
    current = run_layer(current, odd_left, (odd_left + 1) % SITES, kept_ranks, couplings, sketch)
    return current
```

```python
import math

import jax
import jax.numpy as jnp
from jax import lax
from jax.experimental import pallas as pl
from jax.experimental.pallas import tpu as pltpu
from jax.sharding import PartitionSpec as P

tau_step = 0.5
SUB = 8
LANES = 128
PANEL = 16
EXACT = lax.Precision.HIGHEST
LAST = (((1,), (1,)), ((), ()))
PLAIN = (((1,), (0,)), ((), ()))


def gate_terms(coupling):
    hopping = coupling[0]
    ising_term = coupling[1]
    field_term = coupling[2]
    rotation = 0.5 * tau_step * hopping
    middle_scale = jnp.exp(0.25 * tau_step * ising_term)
    weight_empty = jnp.exp(-tau_step * (0.25 * ising_term - 0.5 * field_term))
    weight_full = jnp.exp(-tau_step * (0.25 * ising_term + 0.5 * field_term))
    weight_stay = middle_scale * jnp.cosh(rotation)
    weight_swap = -middle_scale * jnp.sinh(rotation)
    return jnp.stack([weight_empty, weight_stay, weight_swap, weight_full])


def local_mask(site_block, sizes_row, first_sector):
    sector_count = site_block.shape[0]
    block_width = site_block.shape[-1]
    right_ext = jnp.concatenate([sizes_row[1], jnp.zeros((1,), jnp.int32)])
    left_here = lax.dynamic_slice_in_dim(sizes_row[0], first_sector, sector_count)
    right_here = lax.dynamic_slice_in_dim(right_ext, first_sector, sector_count)
    right_next = lax.dynamic_slice_in_dim(right_ext, first_sector + 1, sector_count)
    row_index = jnp.arange(block_width, dtype=jnp.int32)
    row_keep = row_index[None, :] < left_here[:, None]
    col_stay = row_index[None, :] < right_here[:, None]
    col_next = row_index[None, :] < right_next[:, None]
    keep_zero = row_keep[:, :, None] & col_stay[:, None, :]
    keep_one = row_keep[:, :, None] & col_next[:, None, :]
    keep_both = jnp.stack([keep_zero, keep_one], axis=1)
    return jnp.where(keep_both, site_block, jnp.zeros_like(site_block))


def dot(left, right, dims, precision=None):
    return lax.dot_general(
        left, right, dims, precision=precision, preferred_element_type=jnp.float32
    )


def spread(row, lane_index):
    return jnp.broadcast_to(row[:, lane_index : lane_index + 1], row.shape)


def refined_reciprocal(value):
    guess = pltpu.reciprocal(value, approx=True)
    return guess * (2.0 - value * guess)


def factor_tile(gram_rows, inverse_rows):
    lane = lax.broadcasted_iota(jnp.int32, (SUB, LANES), 1)

    def at(index):
        return slice(index * SUB, (index + 1) * SUB)

    for start in range(0, LANES, PANEL):
        stop = start + PANEL
        rows = [gram_rows[at(i), :] for i in range(start, stop)]
        later = []
        for step in range(PANEL):
            k = start + step
            row = rows[step]
            pivot = spread(row, k)
            scaled = jnp.where(lane == k, 1.0, row) * refined_reciprocal(pivot)
            unit = jnp.where(lane < k, row, jnp.where(lane == k, 1.0, 0.0))
            inverse_rows[at(k), :] = unit * lax.rsqrt(pivot)
            for other in range(step + 1, PANEL):
                rows[other] = (
                    jnp.where(lane == k, 0.0, rows[other]) - spread(row, start + other) * scaled
                )
            later.append(jnp.where((lane > k) & (lane < stop), 0.0, scaled))
        for i in range(stop, LANES):
            row = jnp.where((lane >= start) & (lane < stop), 0.0, gram_rows[at(i), :])
            for step in range(PANEL):
                row = row - spread(rows[step], i) * later[step]
            gram_rows[at(i), :] = row


def pair_kernel(
    second,
    weights,
    ranks,
    left_ref,
    right_ref,
    sketch_ref,
    basis_ref,
    coef_ref,
    norm_ref,
    two_ref,
    sample_ref,
    gram_ref,
    inverse_ref,
    rows_ref,
    factor_ref,
):
    count, kept, double = sample_ref.shape
    width = double // 2
    tiles = kept // LANES
    row_index = lax.broadcasted_iota(jnp.int32, (kept, 1), 0)
    eye = (
        lax.broadcasted_iota(jnp.int32, (kept, kept), 0)
        == lax.broadcasted_iota(jnp.int32, (kept, kept), 1)
    )

    def left(m, s):
        if second:
            return left_ref[m, :, s * width : (s + 1) * width]
        return left_ref[m, s]

    def right(m, s):
        if second:
            return right_ref[m, :, s * width : (s + 1) * width]
        return right_ref[m, s]

    def product(a, b):
        rounded = dot(a, b, LAST if second else PLAIN).astype(jnp.bfloat16)
        return rounded.astype(jnp.float32)

    w_empty, w_stay, w_swap, w_full = weights[0], weights[1], weights[2], weights[3]

    @pl.loop(0, count)
    def _(m):
        below_zero, below_one = left(m, 0), left(m, 1)
        here_zero, here_one = left(m + 1, 0), left(m + 1, 1)
        same_zero, same_one = right(m, 0), right(m, 1)
        next_zero, next_one = right(m + 1, 0), right(m + 1, 1)
        low, high = slice(0, width), slice(width, double)
        two_ref[m, low, low] = (w_empty * product(here_zero, same_zero)).astype(jnp.bfloat16)
        two_ref[m, low, high] = (
            w_stay * product(here_zero, next_one) + w_swap * product(here_one, next_zero)
        ).astype(jnp.bfloat16)
        two_ref[m, high, low] = (
            w_swap * product(below_zero, same_one) + w_stay * product(below_one, same_zero)
        ).astype(jnp.bfloat16)
        two_ref[m, high, high] = (w_full * product(below_one, next_one)).astype(jnp.bfloat16)
        sample = dot(sketch_ref[...], two_ref[m], LAST)
        keep = row_index < ranks[m]
        sample = jnp.where(keep, sample, 0.0)
        sample_ref[m] = sample
        gram = dot(sample, sample, LAST, EXACT)
        gram_ref[m] = gram + jnp.where(eye & jnp.logical_not(keep), 1.0, 0.0)

    for tile in range(tiles):
        span = slice(tile * LANES, (tile + 1) * LANES)
        for m in range(count):
            rows_ref[pl.ds(m, LANES, stride=SUB), :] = gram_ref[m, span, span]
        factor_tile(rows_ref, factor_ref)
        for m in range(count):
            inverse_ref[m, span, span] = factor_ref[pl.ds(m, LANES, stride=SUB), :]
            if tile + 1 < tiles:
                inverse_ref[m, span, (tile + 1) * LANES :] = jnp.zeros(
                    (LANES, kept - (tile + 1) * LANES), jnp.float32
                )

        @pl.loop(0, count)
        def _(m):
            block = inverse_ref[m, span, span]
            for lower in range(tile + 1, tiles):
                rest = slice(lower * LANES, (lower + 1) * LANES)
                gram_ref[m, rest, span] = dot(gram_ref[m, rest, span], block, LAST, EXACT)
            for row in range(tile + 1, tiles):
                for column in range(tile + 1, row + 1):
                    across = slice(row * LANES, (row + 1) * LANES)
                    down = slice(column * LANES, (column + 1) * LANES)
                    gram_ref[m, across, down] = gram_ref[m, across, down] - dot(
                        gram_ref[m, across, span], gram_ref[m, down, span], LAST, EXACT
                    )
            if tile > 0:
                done = slice(0, tile * LANES)
                carried = dot(gram_ref[m, span, done], inverse_ref[m, done, done], PLAIN, EXACT)
                inverse_ref[m, span, done] = -dot(block, carried, PLAIN, EXACT)

    norm_ref[...] = jnp.zeros_like(norm_ref)

    @pl.loop(0, count)
    def _(m):
        solved = dot(inverse_ref[m], sample_ref[m], PLAIN, EXACT) * math.sqrt(width)
        basis = solved.astype(jnp.bfloat16)
        if second:
            for s in range(2):
                turned = jnp.transpose(solved[:, s * width : (s + 1) * width])
                basis_ref[m, s] = turned.astype(jnp.bfloat16)
        else:
            basis_ref[m] = basis
        coef = dot(basis, two_ref[m], PLAIN)
        norm_ref[...] += jnp.sum(coef * coef, axis=0, keepdims=True)
        rounded = coef.astype(jnp.bfloat16)
        if second:
            for s in range(2):
                coef_ref[m, s] = rounded[:, s * width : (s + 1) * width]
        else:
            coef_ref[m] = rounded


def pair_update(second, weights, ranks, left, right, sketch_turned):
    count = ranks.shape[0]
    kept, double = sketch_turned.shape
    width = double // 2
    shape = (count, 2, width, kept) if second else (count, kept, double)
    coef_shape = (count, 2, kept, width) if second else (count, kept, double)
    vmem = pl.BlockSpec(memory_space=pltpu.VMEM)
    smem = pl.BlockSpec(memory_space=pltpu.SMEM)

    def kernel(*refs):
        pair_kernel(second, *refs)

    basis, coef, norm = pl.pallas_call(
        kernel,
        out_shape=(
            jax.ShapeDtypeStruct(shape, jnp.bfloat16),
            jax.ShapeDtypeStruct(coef_shape, jnp.bfloat16),
            jax.ShapeDtypeStruct((1, double), jnp.float32),
        ),
        in_specs=[smem, smem, vmem, vmem, vmem],
        out_specs=(vmem, vmem, vmem),
        scratch_shapes=[
            pltpu.VMEM((count, double, double), jnp.bfloat16),
            pltpu.VMEM((count, kept, double), jnp.float32),
            pltpu.VMEM((count, kept, kept), jnp.float32),
            pltpu.VMEM((count, kept, kept), jnp.float32),
            pltpu.VMEM((LANES * SUB, LANES), jnp.float32),
            pltpu.VMEM((LANES * SUB, LANES), jnp.float32),
        ],
        compiler_params=pltpu.CompilerParams(vmem_limit_bytes=40 * 2**20),
        cost_estimate=pl.CostEstimate(
            flops=count * 20 * kept * double * double,
            bytes_accessed=8 * count * kept * double * 2,
            transcendentals=0,
        ),
    )(weights, ranks, left, right, sketch_turned)
    return basis, coef, jnp.sum(norm)


def move(value, pairs_of):
    sites, parts = lax.axis_size("chain"), lax.axis_size("block")
    pairs = []
    for site in range(sites):
        for part in range(parts):
            target = pairs_of(site, part)
            if target is None or not 0 <= target[1] < parts:
                continue
            pairs.append((site * parts + part, (target[0] % sites) * parts + target[1]))
    return lax.ppermute(value, ("chain", "block"), pairs)


def group_sum(value, offset):
    total = lax.psum(value, "block")
    return total + move(
        total[None],
        lambda c, b: (c + 1, b) if (c + offset) % 2 == 0 else (c - 1, b),
    )[0]


def body(site_tensors, sketch, bond_sizes, kept_ranks, couplings):
    sectors = site_tensors.shape[1]
    half = sectors // 2
    width = site_tensors.shape[-1]
    kept = sketch.shape[1]
    parts = lax.axis_size("block")
    first_sector = lax.axis_index("block") * sectors
    is_even = lax.axis_index("chain") % 2 == 0
    own = local_mask(site_tensors[0], bond_sizes[0], first_sector)
    sketch_turned = jnp.transpose(sketch)
    first_here = first_sector + jnp.where(is_even, 0, half)

    partner = move(
        jnp.where(is_even, own[half - 1 :], own[: half + 1]),
        lambda c, b: (c + 1, b) if c % 2 == 0 else (c - 1, b),
    )
    edge = move(
        jnp.where(is_even, own[-1], own[0]),
        lambda c, b: (c, b + 1) if c % 2 == 0 else (c, b - 1),
    )
    corner = move(own[-1, 1], lambda c, b: None if c % 2 == 0 else (c - 1, b + 1))
    left = jnp.where(is_even, jnp.concatenate([edge[None], own[:half]]), partner)
    right_zero = jnp.where(
        is_even, partner[:, 0], jnp.concatenate([own[half:, 0], edge[None, 0]])
    )
    right_one = jnp.where(
        is_even, jnp.concatenate([corner[None], partner[:half, 1]]), own[half - 1 :, 1]
    )
    right = jnp.stack([right_zero, right_one], axis=1)
    pair_row = jnp.where(is_even, 1, 0)
    ranks = lax.dynamic_slice(kept_ranks[0], (pair_row, first_here), (1, half))[0]
    weights = gate_terms(lax.dynamic_index_in_dim(couplings[0], pair_row, 0, keepdims=False))
    basis, coef, norm = pair_update(False, weights, ranks, left, right, sketch_turned)
    target = float(sectors * parts * kept * width)
    scale = jnp.sqrt(target / group_sum(norm, 0))

    carried = move(
        jnp.where(is_even, coef, basis), lambda c, b: (c + 2, b) if c % 2 == 0 else (c - 2, b)
    )
    coef_below = move(coef[-1:], lambda c, b: (c + 1, b) if c % 2 == 0 else (c + 1, b + 1))
    basis_above = move(basis[:1], lambda c, b: (c - 1, b - 1) if c % 2 == 0 else (c - 1, b))
    scale_from_left = move(scale[None], lambda c, b: (c + 1, b) if c % 2 == 1 else None)[0]
    scale = jnp.where(is_even, scale_from_left, scale)
    left = jnp.concatenate([coef_below, jnp.where(is_even, carried, coef)])
    right = jnp.concatenate([jnp.where(is_even, basis, carried), basis_above])
    pair_row = jnp.where(is_even, 0, 1)
    ranks = lax.dynamic_slice(kept_ranks[0], (pair_row, first_here), (1, half))[0]
    weights = gate_terms(lax.dynamic_index_in_dim(couplings[0], pair_row, 0, keepdims=False))
    basis, coef, norm = pair_update(True, weights * scale, ranks, left, right, sketch_turned)
    scale = jnp.sqrt(target / group_sum(norm, 1))

    returned = move(
        jnp.where(is_even, basis, coef), lambda c, b: (c - 1, b) if c % 2 == 0 else (c + 1, b)
    )
    lower_above = move(basis[:1, 1], lambda c, b: (c - 1, b - 1) if c % 2 == 0 else None)
    new_left = jnp.stack(
        [
            jnp.concatenate([returned[:, 0], basis[:, 0]]),
            jnp.concatenate([returned[1:, 1], basis[:, 1], lower_above]),
        ],
        axis=1,
    )
    new_right = jnp.concatenate([coef, returned]).astype(jnp.float32) * scale
    return jnp.where(is_even, new_right.astype(jnp.bfloat16), new_left)[None]


def solution(mesh):
    placed = (
        P("chain", "block", None, None, None),
        P(),
        P("chain", None, None),
        P("chain", None, None),
        P("chain", None, None),
    )
    return jax.shard_map(
        body,
        mesh=mesh,
        in_specs=placed,
        out_specs=P("chain", "block", None, None, None),
        check_vma=False,
    )
```

```python
import math

import jax
import jax.numpy as jnp
from jax import lax
from jax.experimental import pallas as pl
from jax.experimental.pallas import tpu as pltpu
from jax.sharding import PartitionSpec as P

tau_step = 0.5
SUB = 8
LANES = 128
PANEL = 32
PART = 8
UNROLL = 2
FIRST = (((0,), (0,)), ((), ()))
LAST = (((1,), (1,)), ((), ()))
PLAIN = (((1,), (0,)), ((), ()))


def gate_terms(coupling):
    hopping = coupling[0]
    ising_term = coupling[1]
    field_term = coupling[2]
    rotation = 0.5 * tau_step * hopping
    middle_scale = jnp.exp(0.25 * tau_step * ising_term)
    weight_empty = jnp.exp(-tau_step * (0.25 * ising_term - 0.5 * field_term))
    weight_full = jnp.exp(-tau_step * (0.25 * ising_term + 0.5 * field_term))
    weight_stay = middle_scale * jnp.cosh(rotation)
    weight_swap = -middle_scale * jnp.sinh(rotation)
    return jnp.stack([weight_empty, weight_stay, weight_swap, weight_full])


def local_mask(site_block, sizes_row, first_sector):
    sector_count = site_block.shape[0]
    block_width = site_block.shape[-1]
    right_ext = jnp.concatenate([sizes_row[1], jnp.zeros((1,), jnp.int32)])
    left_here = lax.dynamic_slice_in_dim(sizes_row[0], first_sector, sector_count)
    right_here = lax.dynamic_slice_in_dim(right_ext, first_sector, sector_count)
    right_next = lax.dynamic_slice_in_dim(right_ext, first_sector + 1, sector_count)
    row_index = jnp.arange(block_width, dtype=jnp.int32)
    row_keep = row_index[None, :] < left_here[:, None]
    col_stay = row_index[None, :] < right_here[:, None]
    col_next = row_index[None, :] < right_next[:, None]
    keep_zero = row_keep[:, :, None] & col_stay[:, None, :]
    keep_one = row_keep[:, :, None] & col_next[:, None, :]
    keep_both = jnp.stack([keep_zero, keep_one], axis=1)
    return jnp.where(keep_both, site_block, jnp.zeros_like(site_block))


def dot(left, right, dims):
    return lax.dot_general(left, right, dims, preferred_element_type=jnp.float32)


def spread(row, lane_index):
    return jnp.take_along_axis(row, lane_index, axis=1)


def refined_reciprocal(value):
    guess = pltpu.reciprocal(value, approx=True)
    return guess * (2.0 - value * guess)


def factor_panel(rows_ref, first, tile):
    lanes = rows_ref.shape[0] * LANES
    lane = lax.broadcasted_iota(jnp.int32, (SUB, lanes), 1)
    zero = jnp.zeros((SUB, LANES), jnp.int32)
    mine = slice(tile * LANES, (tile + 1) * LANES)
    stop = first + PANEL
    inside = (lane >= first) & (lane < stop)

    def load(index):
        at = slice(index * SUB, (index + 1) * SUB)
        return jnp.concatenate([rows_ref[half, at, :] for half in range(lanes // LANES)], axis=1)

    def wide(value):
        return jnp.concatenate([value] * (lanes // LANES), axis=1)

    def store(index, value):
        at = slice(index * SUB, (index + 1) * SUB)
        for half in range(lanes // LANES):
            rows_ref[half, at, :] = value[:, half * LANES : (half + 1) * LANES]

    for start in range(0, PANEL, PART):
        rows = [load(start + i) for i in range(PART)]
        base = first - tile * LANES + start
        entry = [
            [spread(rows[i][:, mine], base + j + zero) if j >= i else None for j in range(PART)]
            for i in range(PART)
        ]
        later = []
        for step in range(PART):
            k = first + start + step
            inverted = refined_reciprocal(entry[step][step])
            unit = jnp.where(lane == k, 1.0, rows[step])
            for other in range(step + 1, PART):
                ratio = entry[step][other] * inverted
                for column in range(other, PART):
                    entry[other][column] = entry[other][column] - ratio * entry[step][column]
                rows[other] = jnp.where(lane == k, 0.0, rows[other]) - wide(ratio) * unit
            done = jnp.where((lane > k) & (lane < stop), 0.0, unit)
            store(start + step, done * wide(lax.rsqrt(entry[step][step])))
            hidden = jnp.where((lane > k) & (lane < first + start + PART), 0.0, unit)
            later.append(hidden * wide(inverted))
        for i in range(start + PART, PANEL):
            hide = (lane >= first + start) & (lane < first + start + PART)
            row = jnp.where(hide, 0.0, load(i))
            for step in range(PART):
                row = row - wide(spread(rows[step][:, mine], first - tile * LANES + i + zero)) * later[step]
            store(i, row)


def in_parts(value):
    high = value.astype(jnp.bfloat16)
    rest = value - high.astype(jnp.float32)
    middle = rest.astype(jnp.bfloat16)
    return high, middle, (rest - middle.astype(jnp.float32)).astype(jnp.bfloat16)


def pair_kernel(
    second,
    weights,
    ranks,
    left_ref,
    right_ref,
    sketch_ref,
    basis_ref,
    coef_ref,
    norm_ref,
    two_ref,
    sample_ref,
    gram_ref,
    inverse_ref,
    rows_ref,
):
    count, kept, double = sample_ref.shape
    width = double // 2
    row_index = lax.broadcasted_iota(jnp.int32, (kept, 1), 0)
    eye = (
        lax.broadcasted_iota(jnp.int32, (kept, kept), 0)
        == lax.broadcasted_iota(jnp.int32, (kept, kept), 1)
    )

    def left(m, s):
        if second:
            return left_ref[m, :, s * width : (s + 1) * width]
        return left_ref[m, s]

    def right(m, s):
        if second:
            return right_ref[m, :, s * width : (s + 1) * width]
        return right_ref[m, s]

    def product(a, b):
        rounded = dot(a, b, LAST if second else PLAIN).astype(jnp.bfloat16)
        return rounded.astype(jnp.float32)

    w_empty, w_stay, w_swap, w_full = weights[0], weights[1], weights[2], weights[3]

    @pl.loop(0, count, unroll=UNROLL)
    def _(m):
        below_zero, below_one = left(m, 0), left(m, 1)
        here_zero, here_one = left(m + 1, 0), left(m + 1, 1)
        same_zero, same_one = right(m, 0), right(m, 1)
        next_zero, next_one = right(m + 1, 0), right(m + 1, 1)
        low, high = slice(0, width), slice(width, double)
        two_ref[m, low, low] = (w_empty * product(here_zero, same_zero)).astype(jnp.bfloat16)
        two_ref[m, low, high] = (
            w_stay * product(here_zero, next_one) + w_swap * product(here_one, next_zero)
        ).astype(jnp.bfloat16)
        two_ref[m, high, low] = (
            w_swap * product(below_zero, same_one) + w_stay * product(below_one, same_zero)
        ).astype(jnp.bfloat16)
        two_ref[m, high, high] = (w_full * product(below_one, next_one)).astype(jnp.bfloat16)
        sample = dot(sketch_ref[...], two_ref[m], LAST)
        keep = row_index < ranks[m]
        sample = jnp.where(keep, sample, 0.0)
        sample_ref[m] = sample
        high_part, middle_part, low_part = in_parts(sample)
        cross = dot(high_part, middle_part, LAST) + dot(high_part, low_part, LAST)
        gram = dot(high_part, high_part, LAST) + (
            dot(middle_part, middle_part, LAST) + (cross + jnp.transpose(cross))
        )
        gram_ref[m] = gram + jnp.where(eye & jnp.logical_not(keep), 1.0, 0.0)

    lane = lax.broadcasted_iota(jnp.int32, (1, kept), 1)
    for tile in range(kept // LANES):
        @pl.loop(0, LANES // PANEL)
        def _(panel):
            first = pl.multiple_of(tile * LANES + panel * PANEL, PANEL)
            here = pl.ds(first, PANEL)
            stop = first + PANEL
            for m in range(count):
                for half in range(kept // LANES):
                    span = slice(half * LANES, (half + 1) * LANES)
                    rows_ref[half, pl.ds(m, PANEL, stride=SUB), :] = gram_ref[m, here, span]
            factor_panel(rows_ref, first, tile)
            for m in range(count):
                solved = jnp.concatenate(
                    [
                        rows_ref[half, pl.ds(m, PANEL, stride=SUB), :]
                        for half in range(kept // LANES)
                    ],
                    axis=1,
                )
                inverse_ref[m, here, :] = jnp.where(lane < stop, solved, 0.0)
                high, middle, low = in_parts(solved)
                one = jnp.concatenate([high, high, middle, middle, high, low], axis=0)
                two = jnp.concatenate([high, middle, high, middle, low, high], axis=0)
                change = dot(one, two, FIRST)
                kept_part = jnp.where((lane >= first) & (lane < stop), 0.0, gram_ref[m])
                gram_ref[m] = kept_part - change

    norm_ref[...] = jnp.zeros_like(norm_ref)

    @pl.loop(0, count, unroll=UNROLL)
    def _(m):
        inverse_high, inverse_middle, _ = in_parts(inverse_ref[m])
        sample_high, sample_middle, _ = in_parts(sample_ref[m])
        solved = dot(inverse_high, sample_high, PLAIN) + (
            dot(inverse_high, sample_middle, PLAIN) + dot(inverse_middle, sample_high, PLAIN)
        )
        solved = solved * math.sqrt(width)
        basis = solved.astype(jnp.bfloat16)
        if second:
            for s in range(2):
                turned = jnp.transpose(solved[:, s * width : (s + 1) * width])
                basis_ref[m, s] = turned.astype(jnp.bfloat16)
        else:
            basis_ref[m] = basis
        coef = dot(basis, two_ref[m], PLAIN)
        norm_ref[...] += jnp.sum(coef * coef, axis=0, keepdims=True)
        rounded = coef.astype(jnp.bfloat16)
        if second:
            for s in range(2):
                coef_ref[m, s] = rounded[:, s * width : (s + 1) * width]
        else:
            coef_ref[m] = rounded


def pair_update(second, weights, ranks, left, right, sketch_turned):
    count = ranks.shape[0]
    kept, double = sketch_turned.shape
    width = double // 2
    shape = (count, 2, width, kept) if second else (count, kept, double)
    coef_shape = (count, 2, kept, width) if second else (count, kept, double)
    vmem = pl.BlockSpec(memory_space=pltpu.VMEM)
    smem = pl.BlockSpec(memory_space=pltpu.SMEM)

    def kernel(*refs):
        pair_kernel(second, *refs)

    basis, coef, norm = pl.pallas_call(
        kernel,
        out_shape=(
            jax.ShapeDtypeStruct(shape, jnp.bfloat16),
            jax.ShapeDtypeStruct(coef_shape, jnp.bfloat16),
            jax.ShapeDtypeStruct((1, double), jnp.float32),
        ),
        in_specs=[smem, smem, vmem, vmem, vmem],
        out_specs=(vmem, vmem, vmem),
        scratch_shapes=[
            pltpu.VMEM((count, double, double), jnp.bfloat16),
            pltpu.VMEM((count, kept, double), jnp.float32),
            pltpu.VMEM((count, kept, kept), jnp.float32),
            pltpu.VMEM((count, kept, kept), jnp.float32),
            pltpu.VMEM((kept // LANES, PANEL * SUB, LANES), jnp.float32),
        ],
        compiler_params=pltpu.CompilerParams(vmem_limit_bytes=40 * 2**20),
        cost_estimate=pl.CostEstimate(
            flops=count * 20 * kept * double * double,
            bytes_accessed=8 * count * kept * double * 2,
            transcendentals=0,
        ),
    )(weights, ranks, left, right, sketch_turned)
    return basis, coef, jnp.sum(norm)


def move(value, target_of):
    sites, parts = lax.axis_size("chain"), lax.axis_size("block")
    pairs = []
    for site in range(sites):
        for part in range(parts):
            target = target_of(site, part)
            if target is not None and 0 <= target[1] < parts:
                pairs.append((site * parts + part, (target[0] % sites) * parts + target[1]))
    return lax.ppermute(value, ("chain", "block"), pairs)


def by_parity(even_target, odd_target):
    return lambda c, b: even_target(c, b) if c % 2 == 0 else odd_target(c, b)


def nowhere(c, b):
    return None


def joined(*parts):
    return jnp.concatenate(parts, axis=0)


def body(site_tensors, sketch, bond_sizes, kept_ranks, couplings):
    sectors = site_tensors.shape[1]
    half = sectors // 2
    early = half // 2
    width = site_tensors.shape[-1]
    kept = sketch.shape[1]
    parts = lax.axis_size("block")
    first_sector = lax.axis_index("block") * sectors
    is_even = lax.axis_index("chain") % 2 == 0
    first_here = first_sector + jnp.where(is_even, 0, half)

    def pick(even_value, odd_value):
        return jnp.where(is_even, even_value, odd_value)

    def bond(row):
        ranks = lax.dynamic_slice(kept_ranks[0], (row, first_here), (1, half))[0]
        weights = gate_terms(lax.dynamic_index_in_dim(couplings[0], row, 0, keepdims=False))
        return ranks[:early], ranks[early:], weights

    own = local_mask(site_tensors[0], bond_sizes[0], first_sector)
    sketch_turned = jnp.transpose(sketch)

    across = by_parity(lambda c, b: (c + 1, b), lambda c, b: (c - 1, b))
    sent = pick(own[half - 1 : half + early], own[: early + 1])
    got_early = move(sent, across)
    edge = move(
        pick(own[-1], own[0]), by_parity(lambda c, b: (c, b + 1), lambda c, b: (c, b - 1))
    )
    corner = move(own[-1:, 1], by_parity(nowhere, lambda c, b: (c - 1, b + 1)))
    sent = pick(own[half + early :], own[early + 1 : half + 1])
    sent, got_early = lax.optimization_barrier((sent, got_early))
    got_late = move(sent, across)
    ranks_early, ranks_late, weights = bond(pick(1, 0))

    left = pick(joined(edge[None], own[:early]), got_early)
    right_zero = pick(got_early[:, 0], own[half : half + early + 1, 0])
    right_one = pick(joined(corner, got_early[:early, 1]), own[half - 1 : half + early, 1])
    right = jnp.stack([right_zero, right_one], axis=1)
    basis_early, coef_early, norm_early = pair_update(
        False, weights, ranks_early, left, right, sketch_turned
    )

    along = by_parity(lambda c, b: (c + 2, b), lambda c, b: (c - 2, b))
    carried_early = move(pick(coef_early, basis_early), along)
    basis_above = move(
        basis_early[:1], by_parity(lambda c, b: (c - 1, b - 1), lambda c, b: (c - 1, b))
    )

    left = pick(own[early - 1 : half], joined(got_early[early:], got_late))
    right_zero = pick(
        joined(got_early[early:, 0], got_late[:, 0]), joined(own[half + early :, 0], edge[:1])
    )
    right_one = pick(
        joined(got_early[early - 1 :, 1], got_late[: half - early - 1, 1]),
        own[half + early - 1 :, 1],
    )
    right = jnp.stack([right_zero, right_one], axis=1)
    basis_late, coef_late, norm_late = pair_update(
        False, weights, ranks_late, left, right, sketch_turned
    )
    norm_even = norm_early + norm_late

    sent = pick(coef_late, basis_late)
    carried_next = move(sent[:1], along)
    coef_below = move(
        coef_late[-1:], by_parity(lambda c, b: (c + 1, b), lambda c, b: (c + 1, b + 1))
    )
    carried_late = move(sent[1:], along)

    ranks_early, ranks_late, weights = bond(pick(0, 1))
    left = joined(coef_below, pick(carried_early, coef_early))
    right = pick(joined(basis_early, basis_late[:1]), joined(carried_early, carried_next))
    new_basis_early, new_coef_early, norm_early = pair_update(
        True, weights, ranks_early, left, right, sketch_turned
    )
    back = by_parity(lambda c, b: (c - 1, b), lambda c, b: (c + 1, b))
    returned_early = move(pick(new_basis_early, new_coef_early), back)
    lower_above = move(
        new_basis_early[:1, 1], by_parity(lambda c, b: (c - 1, b - 1), nowhere)
    )

    left = pick(
        joined(carried_early[-1:], carried_next, carried_late), joined(coef_early[-1:], coef_late)
    )
    right = joined(pick(basis_late, joined(carried_next, carried_late)), basis_above)
    new_basis_late, new_coef_late, norm_late = pair_update(
        True, weights, ranks_late, left, right, sketch_turned
    )
    returned_late = move(pick(new_basis_late, new_coef_late), back)

    norms = lax.psum(jnp.stack([norm_even, norm_early + norm_late]), "block")
    from_left = move(norms, by_parity(nowhere, lambda c, b: (c + 1, b)))
    from_second = move(norms[:1], by_parity(lambda c, b: (c + 2, b), nowhere))
    target = float(sectors * parts * kept * width)
    scale = jnp.sqrt(target / (from_left[0] + from_second[0]))
    scale = scale * jnp.sqrt(target / (scale * scale * (norms[1] + from_left[1])))

    new_left = jnp.stack(
        [
            joined(returned_early[:, 0], returned_late[:, 0], new_basis_early[:, 0], new_basis_late[:, 0]),
            joined(
                returned_early[1:, 1],
                returned_late[:, 1],
                new_basis_early[:, 1],
                new_basis_late[:, 1],
                lower_above,
            ),
        ],
        axis=1,
    )
    new_right = joined(new_coef_early, new_coef_late, returned_early, returned_late)
    new_right = (new_right.astype(jnp.float32) * scale).astype(jnp.bfloat16)
    return pick(new_right, new_left)[None]


def solution(mesh):
    placed = (
        P("chain", "block", None, None, None),
        P(),
        P("chain", None, None),
        P("chain", None, None),
        P("chain", None, None),
    )
    return jax.shard_map(
        body,
        mesh=mesh,
        in_specs=placed,
        out_specs=P("chain", "block", None, None, None),
        check_vma=False,
    )
```

```python
import math

import jax
import jax.numpy as jnp
from jax import lax
from jax.experimental import pallas as pl
from jax.experimental.pallas import tpu as pltpu
from jax.sharding import PartitionSpec as P

tau_step = 0.5
SUB = 8
LANES = 128
PANEL = 32
PART = 8
UNROLL = 2
FIRST = (((0,), (0,)), ((), ()))
LAST = (((1,), (1,)), ((), ()))
PLAIN = (((1,), (0,)), ((), ()))


def gate_terms(hopping, ising_term, field_term):
    rotation = 0.5 * tau_step * hopping
    middle_scale = jnp.exp(0.25 * tau_step * ising_term)
    weight_empty = jnp.exp(-tau_step * (0.25 * ising_term - 0.5 * field_term))
    weight_full = jnp.exp(-tau_step * (0.25 * ising_term + 0.5 * field_term))
    grown, shrunk = jnp.exp(rotation), jnp.exp(-rotation)
    weight_stay = middle_scale * (0.5 * (grown + shrunk))
    weight_swap = -middle_scale * (0.5 * (grown - shrunk))
    return weight_empty, weight_stay, weight_swap, weight_full


def dot(left, right, dims):
    return lax.dot_general(left, right, dims, preferred_element_type=jnp.float32)


def spread(row, lane_index):
    return jnp.take_along_axis(row, lane_index, axis=1)


def refined_reciprocal(value):
    guess = pltpu.reciprocal(value, approx=True)
    return guess * (2.0 - value * guess)


def factor_panel(rows_ref, first, tile):
    lanes = rows_ref.shape[0] * LANES
    lane = lax.broadcasted_iota(jnp.int32, (SUB, lanes), 1)
    zero = jnp.zeros((SUB, LANES), jnp.int32)
    mine = slice(tile * LANES, (tile + 1) * LANES)
    stop = first + PANEL

    def load(index):
        at = slice(index * SUB, (index + 1) * SUB)
        return jnp.concatenate([rows_ref[half, at, :] for half in range(lanes // LANES)], axis=1)

    def wide(value):
        return jnp.concatenate([value] * (lanes // LANES), axis=1)

    def store(index, value):
        at = slice(index * SUB, (index + 1) * SUB)
        for half in range(lanes // LANES):
            rows_ref[half, at, :] = value[:, half * LANES : (half + 1) * LANES]

    for start in range(0, PANEL, PART):
        rows = [load(start + i) for i in range(PART)]
        base = first - tile * LANES + start
        entry = [
            [spread(rows[i][:, mine], base + j + zero) if j >= i else None for j in range(PART)]
            for i in range(PART)
        ]
        later = []
        for step in range(PART):
            k = first + start + step
            inverted = refined_reciprocal(entry[step][step])
            unit = jnp.where(lane == k, 1.0, rows[step])
            for other in range(step + 1, PART):
                ratio = entry[step][other] * inverted
                for column in range(other, PART):
                    entry[other][column] = entry[other][column] - ratio * entry[step][column]
                rows[other] = jnp.where(lane == k, 0.0, rows[other]) - wide(ratio) * unit
            done = jnp.where((lane > k) & (lane < stop), 0.0, unit)
            store(start + step, done * wide(lax.rsqrt(entry[step][step])))
            hidden = jnp.where((lane > k) & (lane < first + start + PART), 0.0, unit)
            later.append(hidden * wide(inverted))
        for i in range(start + PART, PANEL):
            hide = (lane >= first + start) & (lane < first + start + PART)
            row = jnp.where(hide, 0.0, load(i))
            for step in range(PART):
                row = row - wide(spread(rows[step][:, mine], first - tile * LANES + i + zero)) * later[step]
            store(i, row)


def in_parts(value):
    high = value.astype(jnp.bfloat16)
    rest = value - high.astype(jnp.float32)
    middle = rest.astype(jnp.bfloat16)
    return high, middle, (rest - middle.astype(jnp.float32)).astype(jnp.bfloat16)


def run_copies(plan, semaphores):
    copies = [
        pltpu.make_async_copy(source, place, semaphores.at[index])
        for index, (source, place) in enumerate(plan)
    ]
    for copy in copies:
        copy.start()
    for copy in copies:
        copy.wait()


def run_by_parity(even_plan, odd_plan, semaphores):
    is_even = lax.rem(lax.axis_index("chain"), 2) == 0

    @pl.when(is_even)
    def _():
        run_copies(even_plan, semaphores)

    @pl.when(jnp.logical_not(is_even))
    def _():
        run_copies(odd_plan, semaphores)


def first_plans(late, half, early, operands, left, right):
    own, got_early, got_late, edge, corner = operands
    own = own.at[0]
    if late:
        n = half - early
        even = [
            (own.at[pl.ds(early - 1, n + 1)], left),
            (got_early.at[pl.ds(early, 1), 0], right.at[pl.ds(0, 1), 0]),
            (got_late.at[pl.ds(0, n), 0], right.at[pl.ds(1, n), 0]),
            (got_early.at[pl.ds(early - 1, 2), 1], right.at[pl.ds(0, 2), 1]),
        ]
        if n > 1:
            even.append((got_late.at[pl.ds(0, n - 1), 1], right.at[pl.ds(2, n - 1), 1]))
        odd = [
            (got_early.at[pl.ds(early, 1)], left.at[pl.ds(0, 1)]),
            (got_late.at[pl.ds(0, n)], left.at[pl.ds(1, n)]),
            (own.at[pl.ds(half + early, n), 0], right.at[pl.ds(0, n), 0]),
            (edge.at[pl.ds(0, 1), 0], right.at[pl.ds(n, 1), 0]),
            (own.at[pl.ds(half + early - 1, n + 1), 1], right.at[pl.ds(0, n + 1), 1]),
        ]
    else:
        n = early
        even = [
            (edge, left.at[pl.ds(0, 1)]),
            (own.at[pl.ds(0, n)], left.at[pl.ds(1, n)]),
            (got_early.at[pl.ds(0, n + 1), 0], right.at[pl.ds(0, n + 1), 0]),
            (corner, right.at[pl.ds(0, 1), 1]),
            (got_early.at[pl.ds(0, n), 1], right.at[pl.ds(1, n), 1]),
        ]
        odd = [
            (got_early, left),
            (own.at[pl.ds(half, n + 1), 0], right.at[pl.ds(0, n + 1), 0]),
            (own.at[pl.ds(half - 1, n + 1), 1], right.at[pl.ds(0, n + 1), 1]),
        ]
    return even, odd


def second_plans(late, half, early, operands, left, right):
    keep_early, keep_late, carried_early, carried_next, carried_late, beside = operands
    if late:
        n = half - early
        even = [
            (carried_early.at[pl.ds(early - 1, 1)], left.at[pl.ds(0, 1)]),
            (carried_late, left.at[pl.ds(1, n)]),
            (keep_late, right.at[pl.ds(0, n)]),
            (beside, right.at[pl.ds(n, 1)]),
        ]
        odd = [
            (keep_early.at[pl.ds(early - 1, 1)], left.at[pl.ds(0, 1)]),
            (keep_late, left.at[pl.ds(1, n)]),
            (carried_late, right.at[pl.ds(0, n)]),
            (beside, right.at[pl.ds(n, 1)]),
        ]
    else:
        n = early
        even = [
            (beside, left.at[pl.ds(0, 1)]),
            (carried_early, left.at[pl.ds(1, n)]),
            (keep_early, right.at[pl.ds(0, n)]),
            (keep_late.at[pl.ds(0, 1)], right.at[pl.ds(n, 1)]),
        ]
        odd = [
            (beside, left.at[pl.ds(0, 1)]),
            (keep_early, left.at[pl.ds(1, n)]),
            (carried_early, right.at[pl.ds(0, n)]),
            (carried_next, right.at[pl.ds(n, 1)]),
        ]
    return even, odd


def pair_kernel(second, late, sectors, refs):
    half = sectors // 2
    early = half // 2
    sizes, partner_sizes, ranks, couplings = refs[:4]
    operand_count = 6 if second else 5
    operands = refs[4 : 4 + operand_count]
    sketch_ref = refs[4 + operand_count]
    outputs = refs[5 + operand_count : -11]
    (
        left_ref,
        right_ref,
        basis_ref,
        coef_ref,
        two_ref,
        sample_ref,
        gram_ref,
        inverse_ref,
        rows_ref,
        in_semaphores,
        out_semaphores,
    ) = refs[-11:]
    send, keep, norm_ref, *extras = outputs
    count, kept, double = sample_ref.shape
    width = double // 2
    plans = second_plans if second else first_plans
    run_by_parity(*plans(late, half, early, operands, left_ref, right_ref), in_semaphores)

    parity = lax.rem(lax.axis_index("chain"), 2)
    is_even = parity == 0
    first = lax.axis_index("block") * sectors + parity * half + (early if late else 0)
    bond = parity if second else 1 - parity
    total = sizes.shape[2]

    def left_size(sector):
        at = jnp.clip(sector, 0, total - 1)
        return jnp.where(is_even, sizes[0, 0, at], partner_sizes[0, 0, at])

    def middle_size(sector):
        at = jnp.clip(sector, 0, total - 1)
        size = jnp.where(is_even, sizes[0, 1, at], sizes[0, 0, at])
        return jnp.where(sector < total, size, 0)

    def right_size(sector):
        at = jnp.clip(sector, 0, total - 1)
        size = jnp.where(is_even, partner_sizes[0, 1, at], sizes[0, 1, at])
        return jnp.where(sector < total, size, 0)

    row_index = lax.broadcasted_iota(jnp.int32, (kept, 1), 0)
    eye = (
        lax.broadcasted_iota(jnp.int32, (kept, kept), 0)
        == lax.broadcasted_iota(jnp.int32, (kept, kept), 1)
    )
    block_row = lax.broadcasted_iota(jnp.int32, (width, width), 0)
    block_column = lax.broadcasted_iota(jnp.int32, (width, width), 1)
    column = lax.broadcasted_iota(jnp.int32, (1, width), 1)

    def left(m, s, sector):
        if second:
            return left_ref[m, :, s * width : (s + 1) * width]
        inside = (column < middle_size(sector + s)).astype(jnp.float32).astype(jnp.bfloat16)
        return left_ref[m, s] * inside

    def right(m, s):
        if second:
            return right_ref[m, :, s * width : (s + 1) * width]
        return right_ref[m, s]

    def product(a, b):
        rounded = dot(a, b, LAST if second else PLAIN).astype(jnp.bfloat16)
        return rounded.astype(jnp.float32)

    def put(m, rows, columns, value, row_limit, column_limit):
        if not second:
            value = jnp.where(
                (block_row < row_limit) & (block_column < column_limit), value, 0.0
            )
        two_ref[m, rows, columns] = value.astype(jnp.bfloat16)

    w_empty, w_stay, w_swap, w_full = gate_terms(
        *(jnp.full((1, width), couplings[0, bond, term], jnp.float32) for term in range(3))
    )

    @pl.loop(0, count, unroll=min(UNROLL, count))
    def _(m):
        sector = first + m
        below_zero, below_one = left(m, 0, sector - 1), left(m, 1, sector - 1)
        here_zero, here_one = left(m + 1, 0, sector), left(m + 1, 1, sector)
        same_zero, same_one = right(m, 0), right(m, 1)
        next_zero, next_one = right(m + 1, 0), right(m + 1, 1)
        low, high = slice(0, width), slice(width, double)
        rows_low, rows_high = left_size(sector), left_size(sector - 1)
        columns_low, columns_high = right_size(sector), right_size(sector + 1)
        put(m, low, low, w_empty * product(here_zero, same_zero), rows_low, columns_low)
        put(
            m,
            low,
            high,
            w_stay * product(here_zero, next_one) + w_swap * product(here_one, next_zero),
            rows_low,
            columns_high,
        )
        put(
            m,
            high,
            low,
            w_swap * product(below_zero, same_one) + w_stay * product(below_one, same_zero),
            rows_high,
            columns_low,
        )
        put(m, high, high, w_full * product(below_one, next_one), rows_high, columns_high)
        sample = dot(sketch_ref[...], two_ref[m], LAST)
        keep_rows = row_index < ranks[0, bond, sector]
        sample = jnp.where(keep_rows, sample, 0.0)
        sample_ref[m] = sample
        high_part, middle_part, low_part = in_parts(sample)
        cross = dot(high_part, middle_part, LAST) + dot(high_part, low_part, LAST)
        gram = dot(high_part, high_part, LAST) + (
            dot(middle_part, middle_part, LAST) + (cross + jnp.transpose(cross))
        )
        gram_ref[m] = gram + jnp.where(eye & jnp.logical_not(keep_rows), 1.0, 0.0)

    lane = lax.broadcasted_iota(jnp.int32, (1, kept), 1)
    for tile in range(kept // LANES):
        @pl.loop(0, LANES // PANEL)
        def _(panel):
            first = pl.multiple_of(tile * LANES + panel * PANEL, PANEL)
            here = pl.ds(first, PANEL)
            stop = first + PANEL
            for m in range(count):
                for half in range(kept // LANES):
                    span = slice(half * LANES, (half + 1) * LANES)
                    rows_ref[half, pl.ds(m, PANEL, stride=SUB), :] = gram_ref[m, here, span]
            factor_panel(rows_ref, first, tile)
            for m in range(count):
                solved = jnp.concatenate(
                    [
                        rows_ref[half, pl.ds(m, PANEL, stride=SUB), :]
                        for half in range(kept // LANES)
                    ],
                    axis=1,
                )
                inverse_ref[m, here, :] = jnp.where(lane < stop, solved, 0.0)
                high, middle, low = in_parts(solved)
                one = jnp.concatenate([high, high, middle, middle, high, low], axis=0)
                two = jnp.concatenate([high, middle, high, middle, low, high], axis=0)
                change = dot(one, two, FIRST)
                kept_part = jnp.where((lane >= first) & (lane < stop), 0.0, gram_ref[m])
                gram_ref[m] = kept_part - change

    norm_ref[...] = jnp.zeros_like(norm_ref)

    @pl.loop(0, count, unroll=min(UNROLL, count))
    def _(m):
        inverse_high, inverse_middle, _ = in_parts(inverse_ref[m])
        sample_high, sample_middle, _ = in_parts(sample_ref[m])
        solved = dot(inverse_high, sample_high, PLAIN) + (
            dot(inverse_high, sample_middle, PLAIN) + dot(inverse_middle, sample_high, PLAIN)
        )
        solved = solved * math.sqrt(width)
        basis = solved.astype(jnp.bfloat16)
        if second:
            for s in range(2):
                turned = jnp.transpose(solved[:, s * width : (s + 1) * width])
                basis_ref[m, s] = turned.astype(jnp.bfloat16)
        else:
            basis_ref[m] = basis
        coef = dot(basis, two_ref[m], PLAIN)
        norm_ref[...] += jnp.sum(coef * coef, axis=0, keepdims=True)
        rounded = coef.astype(jnp.bfloat16)
        if second:
            for s in range(2):
                coef_ref[m, s] = rounded[:, s * width : (s + 1) * width]
        else:
            coef_ref[m] = rounded


    if second:
        even, odd = [(basis_ref, send), (coef_ref, keep)], [(coef_ref, send), (basis_ref, keep)]
        if not late:
            both = [(basis_ref.at[pl.ds(0, 1), 1], extras[0])]
    else:
        even, odd = [(coef_ref, send), (basis_ref, keep)], [(basis_ref, send), (coef_ref, keep)]
        if late:
            both = [(coef_ref.at[pl.ds(count - 1, 1)], extras[0])]
            even.append((coef_ref.at[pl.ds(0, 1)], extras[1]))
            odd.append((basis_ref.at[pl.ds(0, 1)], extras[1]))
        else:
            both = [(basis_ref.at[pl.ds(0, 1)], extras[0])]
    if not (second and late):
        even, odd = even + both, odd + both
    run_by_parity(even, odd, out_semaphores)


def pair_update(second, late, sizes, partner_sizes, ranks, couplings, operands, sketch_turned):
    kept, double = sketch_turned.shape
    width = double // 2
    sectors = sizes.shape[2] // lax.axis_size("block")
    half = sectors // 2
    early = half // 2
    count = half - early if late else early
    block = (2, width, kept) if second else (kept, double)
    coef_block = (2, kept, width) if second else (kept, double)
    extra = [(1, width, kept)] if second else [(1, kept, double)]
    if late:
        extra = [] if second else extra * 2
    left_shape = (count + 1, kept, double) if second else (count + 1, 2, width, width)
    vmem = pl.BlockSpec(memory_space=pltpu.VMEM)
    smem = pl.BlockSpec(memory_space=pltpu.SMEM)
    anywhere = pl.BlockSpec(memory_space=pl.ANY)

    def kernel(*refs):
        pair_kernel(second, late, sectors, refs)

    return pl.pallas_call(
        kernel,
        out_shape=[
            jax.ShapeDtypeStruct((count, *block), jnp.bfloat16),
            jax.ShapeDtypeStruct((count, *block), jnp.bfloat16),
            jax.ShapeDtypeStruct((1, double), jnp.float32),
            *(jax.ShapeDtypeStruct(shape, jnp.bfloat16) for shape in extra),
        ],
        in_specs=[smem] * 4 + [anywhere] * len(operands) + [vmem],
        out_specs=[anywhere, anywhere, vmem] + [anywhere] * len(extra),
        scratch_shapes=[
            pltpu.VMEM(left_shape, jnp.bfloat16),
            pltpu.VMEM(left_shape, jnp.bfloat16),
            pltpu.VMEM((count, *block), jnp.bfloat16),
            pltpu.VMEM((count, *coef_block), jnp.bfloat16),
            pltpu.VMEM((count, double, double), jnp.bfloat16),
            pltpu.VMEM((count, kept, double), jnp.float32),
            pltpu.VMEM((count, kept, kept), jnp.float32),
            pltpu.VMEM((count, kept, kept), jnp.float32),
            pltpu.VMEM((kept // LANES, PANEL * SUB, LANES), jnp.float32),
            pltpu.SemaphoreType.DMA((5,)),
            pltpu.SemaphoreType.DMA((4,)),
        ],
        compiler_params=pltpu.CompilerParams(vmem_limit_bytes=32 * 2**20),
        cost_estimate=pl.CostEstimate(
            flops=(count + 12) * 50 * kept * double * double,
            bytes_accessed=8 * count * kept * double * 2,
            transcendentals=0,
        ),
    )(sizes, partner_sizes, ranks, couplings, *operands, sketch_turned)


def place_kernel(last, half, scale_ref, refs):
    early = half // 2
    n = half - early
    if last:
        returned, _, out, buffer, in_semaphores, out_semaphores = refs
        parts = [(returned, half + early, n)]
        odd = [
            (returned.at[pl.ds(0, n), 0], out.at[0, pl.ds(early, n), 0]),
            (returned.at[pl.ds(0, n), 1], out.at[0, pl.ds(early - 1, n), 1]),
        ]
    else:
        keep_early, keep_late, returned, lower, out, buffer, in_semaphores, out_semaphores = refs
        parts = [(keep_early, 0, early), (keep_late, early, n), (returned, half, early)]
        odd = [
            (returned.at[pl.ds(0, early), 0], out.at[0, pl.ds(0, early), 0]),
            (keep_early.at[pl.ds(0, early), 0], out.at[0, pl.ds(half, early), 0]),
            (keep_early.at[pl.ds(0, early), 1], out.at[0, pl.ds(half - 1, early), 1]),
            (keep_late.at[pl.ds(0, n), 0], out.at[0, pl.ds(half + early, n), 0]),
            (keep_late.at[pl.ds(0, n), 1], out.at[0, pl.ds(half + early - 1, n), 1]),
            (lower, out.at[0, pl.ds(2 * half - 1, 1), 1]),
        ]
        if early > 1:
            odd.append((returned.at[pl.ds(1, early - 1), 1], out.at[0, pl.ds(0, early - 1), 1]))
    is_even = lax.rem(lax.axis_index("chain"), 2) == 0

    @pl.when(jnp.logical_not(is_even))
    def _():
        run_copies(odd, out_semaphores)

    @pl.when(is_even)
    def _():
        coming, going, filled = [], [], 0
        for index, (source, start, size) in enumerate(parts):
            room = buffer.at[pl.ds(filled, size)]
            coming.append(pltpu.make_async_copy(source, room, in_semaphores.at[index]))
            going.append(
                pltpu.make_async_copy(room, out.at[0, pl.ds(start, size)], out_semaphores.at[index])
            )
            filled += size
        for copy in coming:
            copy.start()
        filled = 0
        for index, (source, start, size) in enumerate(parts):
            coming[index].wait()

            @pl.loop(filled, filled + size)
            def _(sector):
                for s in range(2):
                    scaled = buffer[sector, s].astype(jnp.float32) * scale_ref[0]
                    buffer[sector, s] = scaled.astype(jnp.bfloat16)

            going[index].start()
            filled += size
        for copy in going:
            copy.wait()


def place(last, half, scale, operands, site):
    anywhere = pl.BlockSpec(memory_space=pl.ANY)
    early = half // 2
    rows = half - early if last else half + early

    def kernel(scale_ref, *refs):
        place_kernel(last, half, scale_ref, refs)

    return pl.pallas_call(
        kernel,
        out_shape=jax.ShapeDtypeStruct(site.shape, site.dtype),
        in_specs=[pl.BlockSpec(memory_space=pltpu.SMEM)] + [anywhere] * len(operands),
        out_specs=anywhere,
        scratch_shapes=[
            pltpu.VMEM((rows, *site.shape[2:]), site.dtype),
            pltpu.SemaphoreType.DMA((3,)),
            pltpu.SemaphoreType.DMA((7,)),
        ],
        input_output_aliases={2: 0} if last else {},
        compiler_params=pltpu.CompilerParams(vmem_limit_bytes=16 * 2**20),
        cost_estimate=pl.CostEstimate(
            flops=0, bytes_accessed=2 * rows * site.size // site.shape[1] * 2, transcendentals=0
        ),
    )(scale, *operands)


def move(value, target_of):
    sites, parts = lax.axis_size("chain"), lax.axis_size("block")
    pairs = []
    for site in range(sites):
        for part in range(parts):
            target = target_of(site, part)
            if target is not None and 0 <= target[1] < parts:
                pairs.append((site * parts + part, (target[0] % sites) * parts + target[1]))
    return lax.ppermute(value, ("chain", "block"), pairs)


def by_parity(even_target, odd_target):
    return lambda c, b: even_target(c, b) if c % 2 == 0 else odd_target(c, b)


def nowhere(c, b):
    return None


def joined(*parts):
    return jnp.concatenate(parts, axis=0)


def body(site_tensors, sketch, bond_sizes, kept_ranks, couplings):
    sectors = site_tensors.shape[1]
    half = sectors // 2
    early = half // 2
    width = site_tensors.shape[-1]
    kept = sketch.shape[1]
    parts = lax.axis_size("block")
    is_even = lax.axis_index("chain") % 2 == 0
    own = site_tensors[0]
    sketch_turned = jnp.transpose(sketch)

    def pick(even_value, odd_value):
        return jnp.where(is_even, even_value, odd_value)

    def update(second, late, *operands):
        return pair_update(
            second, late, bond_sizes, partner_sizes, kept_ranks, couplings, operands, sketch_turned
        )

    across = by_parity(lambda c, b: (c + 1, b), lambda c, b: (c - 1, b))
    got_early = move(pick(own[half - 1 : half + early], own[: early + 1]), across)
    partner_sizes = move(bond_sizes, across)
    edge = move(
        pick(own[-1:], own[:1]), by_parity(lambda c, b: (c, b + 1), lambda c, b: (c, b - 1))
    )
    corner = move(own[-1:, 1], by_parity(nowhere, lambda c, b: (c - 1, b + 1)))
    sent = pick(own[half + early :], own[early + 1 : half + 1])
    sent, got_early = lax.optimization_barrier((sent, got_early))
    got_late = move(sent, across)
    send_early, keep_early, norm_early, basis_first = update(
        False, False, site_tensors, got_early, got_early, edge, corner
    )

    along = by_parity(lambda c, b: (c + 2, b), lambda c, b: (c - 2, b))
    carried_early = move(send_early, along)
    basis_above = move(
        basis_first, by_parity(lambda c, b: (c - 1, b - 1), lambda c, b: (c - 1, b))
    )
    send_late, keep_late, norm_late, coef_last, send_next = update(
        False, True, site_tensors, got_early, got_late, edge, corner
    )
    norm_even = jnp.sum(norm_early) + jnp.sum(norm_late)
    carried_next = move(send_next, along)
    coef_below = move(
        coef_last, by_parity(lambda c, b: (c + 1, b), lambda c, b: (c + 1, b + 1))
    )
    send_late, carried_early, carried_next, coef_below = lax.optimization_barrier(
        (send_late, carried_early, carried_next, coef_below)
    )
    carried_late = move(send_late, along)

    back = by_parity(lambda c, b: (c - 1, b), lambda c, b: (c + 1, b))
    send_early, kept_early, norm_early, lower_first = update(
        True, False, keep_early, keep_late, carried_early, carried_next, carried_next, coef_below
    )
    returned_early = move(send_early, back)
    lower_above = move(lower_first, by_parity(lambda c, b: (c - 1, b - 1), nowhere))
    send_late, kept_late, norm_late = update(
        True, True, keep_early, keep_late, carried_early, carried_next, carried_late, basis_above
    )
    send_late, returned_early = lax.optimization_barrier((send_late, returned_early))
    returned_late = move(send_late, back)

    norm_odd = jnp.sum(norm_early) + jnp.sum(norm_late)
    norms = lax.psum(jnp.stack([norm_even, norm_odd]), "block")
    from_left = move(norms, by_parity(nowhere, lambda c, b: (c + 1, b)))
    from_second = move(norms[:1], by_parity(lambda c, b: (c + 2, b), nowhere))
    target = float(sectors * parts * kept * width)
    scale = jnp.sqrt(target / (from_left[0] + from_second[0]))
    scale = scale * jnp.sqrt(target / (scale * scale * (norms[1] + from_left[1])))
    scale = scale[None]

    site = place(
        False, half, scale, (kept_early, kept_late, returned_early, lower_above), site_tensors
    )
    return place(True, half, scale, (returned_late, site), site_tensors)


def solution(mesh):
    placed = (
        P("chain", "block", None, None, None),
        P(),
        P("chain", None, None),
        P("chain", None, None),
        P("chain", None, None),
    )
    return jax.shard_map(
        body,
        mesh=mesh,
        in_specs=placed,
        out_specs=P("chain", "block", None, None, None),
        check_vma=False,
    )
```

```python
import math

import jax
import jax.numpy as jnp
from jax import lax
from jax.experimental import pallas as pl
from jax.experimental.pallas import tpu as pltpu
from jax.sharding import PartitionSpec as P

tau_step = 0.5
SUB = 8
LANES = 128
PANEL = 32
PART = 8
UNROLL = 2
FIRST = (((0,), (0,)), ((), ()))
LAST = (((1,), (1,)), ((), ()))
PLAIN = (((1,), (0,)), ((), ()))


def gate_terms(hopping, ising_term, field_term):
    rotation = 0.5 * tau_step * hopping
    middle_scale = jnp.exp(0.25 * tau_step * ising_term)
    weight_empty = jnp.exp(-tau_step * (0.25 * ising_term - 0.5 * field_term))
    weight_full = jnp.exp(-tau_step * (0.25 * ising_term + 0.5 * field_term))
    grown, shrunk = jnp.exp(rotation), jnp.exp(-rotation)
    weight_stay = middle_scale * (0.5 * (grown + shrunk))
    weight_swap = -middle_scale * (0.5 * (grown - shrunk))
    return weight_empty, weight_stay, weight_swap, weight_full


def dot(left, right, dims):
    return lax.dot_general(left, right, dims, preferred_element_type=jnp.float32)


def spread(row, lane_index):
    return jnp.take_along_axis(row, lane_index, axis=1)


def refined_reciprocal(value):
    guess = pltpu.reciprocal(value, approx=True)
    return guess * (2.0 - value * guess)


def factor_panel(rows_ref, first, tile):
    lanes = rows_ref.shape[0] * LANES
    lane = lax.broadcasted_iota(jnp.int32, (SUB, lanes), 1)
    zero = jnp.zeros((SUB, LANES), jnp.int32)
    mine = slice(tile * LANES, (tile + 1) * LANES)
    stop = first + PANEL

    def load(index):
        at = slice(index * SUB, (index + 1) * SUB)
        return jnp.concatenate([rows_ref[half, at, :] for half in range(lanes // LANES)], axis=1)

    def wide(value):
        return jnp.concatenate([value] * (lanes // LANES), axis=1)

    def store(index, value):
        at = slice(index * SUB, (index + 1) * SUB)
        for half in range(lanes // LANES):
            rows_ref[half, at, :] = value[:, half * LANES : (half + 1) * LANES]

    for start in range(0, PANEL, PART):
        rows = [load(start + i) for i in range(PART)]
        base = first - tile * LANES + start
        entry = [
            [spread(rows[i][:, mine], base + j + zero) if j >= i else None for j in range(PART)]
            for i in range(PART)
        ]
        later = []
        for step in range(PART):
            k = first + start + step
            inverted = refined_reciprocal(entry[step][step])
            unit = jnp.where(lane == k, 1.0, rows[step])
            for other in range(step + 1, PART):
                ratio = entry[step][other] * inverted
                for column in range(other, PART):
                    entry[other][column] = entry[other][column] - ratio * entry[step][column]
                rows[other] = jnp.where(lane == k, 0.0, rows[other]) - wide(ratio) * unit
            done = jnp.where((lane > k) & (lane < stop), 0.0, unit)
            store(start + step, done * wide(lax.rsqrt(entry[step][step])))
            hidden = jnp.where((lane > k) & (lane < first + start + PART), 0.0, unit)
            later.append(hidden * wide(inverted))
        for i in range(start + PART, PANEL):
            hide = (lane >= first + start) & (lane < first + start + PART)
            row = jnp.where(hide, 0.0, load(i))
            for step in range(PART):
                row = row - wide(spread(rows[step][:, mine], first - tile * LANES + i + zero)) * later[step]
            store(i, row)


def in_parts(value):
    high = value.astype(jnp.bfloat16)
    rest = value - high.astype(jnp.float32)
    middle = rest.astype(jnp.bfloat16)
    return high, middle, (rest - middle.astype(jnp.float32)).astype(jnp.bfloat16)


def run_copies(plan, semaphores):
    copies = [
        pltpu.make_async_copy(source, place, semaphores.at[index])
        for index, (source, place) in enumerate(plan)
    ]
    for copy in copies:
        copy.start()
    for copy in copies:
        copy.wait()


def run_by_parity(even_plan, odd_plan, semaphores):
    is_even = lax.rem(lax.axis_index("chain"), 2) == 0

    @pl.when(is_even)
    def _():
        run_copies(even_plan, semaphores)

    @pl.when(jnp.logical_not(is_even))
    def _():
        run_copies(odd_plan, semaphores)


def chunk_sizes(half):
    early = max(half // 2, 1)
    return early, early - 1


def cut(line, first, count, place):
    plan = []
    for source, start, size in line:
        low, high = max(first, start), min(first + count, start + size)
        if low < high:
            plan.append((source(low - start, high - low), place(low - first, high - low)))
    return plan


def whole(ref):
    return lambda start, size: ref.at[pl.ds(start, size)]


def plane(ref, s):
    return lambda start, size: ref.at[pl.ds(start, size), s]


def first_plans(first_of, count, half, early, operands, left, right):
    own, got_early, got_late, edge, corner = operands
    own = own.at[0]
    late, sectors = half - early, 2 * half

    def plans(first, left_line, right_line, extra):
        zero_line = [(plane(ref, 0), start, size) for ref, start, size in right_line]
        one_line = [(plane(ref, 1), start, size) for ref, start, size in right_line]
        return [
            *cut([(whole(ref), start, size) for ref, start, size in left_line], first - 1, count + 1, whole(left)),
            *cut(zero_line, first, count + 1, plane(right, 0)),
            *cut(one_line + extra, first - 1, count + 1, plane(right, 1)),
        ]

    even = plans(
        first_of[0],
        [(edge, -1, 1), (own, 0, sectors)],
        [(got_early, 0, early + 1), (got_late, early + 1, late)],
        [(whole(corner), -1, 1)],
    )
    odd = plans(
        first_of[1],
        [(got_late, half - 1, late), (got_early, sectors - early - 1, early + 1)],
        [(own, 0, sectors), (edge, sectors, 1)],
        [],
    )
    return even, odd


def second_plans(first_of, count, half, early, operands, left, right):
    keep_early, keep_late, carried_early, carried_late, far, near = operands
    late, sectors = half - early, 2 * half

    def plans(first, left_line, right_line):
        return [
            *cut([(whole(ref), start, size) for ref, start, size in left_line], first - 1, count + 1, whole(left)),
            *cut([(whole(ref), start, size) for ref, start, size in right_line], first, count + 1, whole(right)),
        ]

    even = plans(
        first_of[0],
        [(far, -1, 1), (carried_early, 0, early), (carried_late, early, late)],
        [(keep_early, 0, early), (keep_late, early, late), (near, half, 1)],
    )
    odd = plans(
        first_of[1],
        [(near, half - 1, 1), (keep_late, half, late), (keep_early, sectors - early, early)],
        [(carried_late, half, late), (carried_early, sectors - early, early), (far, sectors, 1)],
    )
    return even, odd


def pair_kernel(second, late, sectors, refs):
    half = sectors // 2
    early, next_early = chunk_sizes(half)
    part = next_early if second else early
    first_of = (part, half) if late else (0, sectors - part)
    sizes, partner_sizes, ranks, couplings = refs[:4]
    operand_count = 6 if second else 5
    operands = refs[4 : 4 + operand_count]
    sketch_ref = refs[4 + operand_count]
    outputs = refs[5 + operand_count : -11]
    (
        left_ref,
        right_ref,
        basis_ref,
        coef_ref,
        two_ref,
        sample_ref,
        gram_ref,
        inverse_ref,
        rows_ref,
        in_semaphores,
        out_semaphores,
    ) = refs[-11:]
    send, keep, norm_ref, *extras = outputs
    count, kept, double = sample_ref.shape
    width = double // 2
    plans = second_plans if second else first_plans
    run_by_parity(*plans(first_of, count, half, early, operands, left_ref, right_ref), in_semaphores)

    parity = lax.rem(lax.axis_index("chain"), 2)
    is_even = parity == 0
    first = lax.axis_index("block") * sectors + jnp.where(is_even, *first_of)
    bond = parity if second else 1 - parity
    total = sizes.shape[2]

    def left_size(sector):
        at = jnp.clip(sector, 0, total - 1)
        return jnp.where(is_even, sizes[0, 0, at], partner_sizes[0, 0, at])

    def middle_size(sector):
        at = jnp.clip(sector, 0, total - 1)
        size = jnp.where(is_even, sizes[0, 1, at], sizes[0, 0, at])
        return jnp.where(sector < total, size, 0)

    def right_size(sector):
        at = jnp.clip(sector, 0, total - 1)
        size = jnp.where(is_even, partner_sizes[0, 1, at], sizes[0, 1, at])
        return jnp.where(sector < total, size, 0)

    row_index = lax.broadcasted_iota(jnp.int32, (kept, 1), 0)
    eye = (
        lax.broadcasted_iota(jnp.int32, (kept, kept), 0)
        == lax.broadcasted_iota(jnp.int32, (kept, kept), 1)
    )
    block_row = lax.broadcasted_iota(jnp.int32, (width, width), 0)
    block_column = lax.broadcasted_iota(jnp.int32, (width, width), 1)
    column = lax.broadcasted_iota(jnp.int32, (1, width), 1)

    def left(m, s, sector):
        if second:
            return left_ref[m, :, s * width : (s + 1) * width]
        inside = (column < middle_size(sector + s)).astype(jnp.float32).astype(jnp.bfloat16)
        return left_ref[m, s] * inside

    def right(m, s):
        if second:
            return right_ref[m, :, s * width : (s + 1) * width]
        return right_ref[m, s]

    def product(a, b):
        rounded = dot(a, b, LAST if second else PLAIN).astype(jnp.bfloat16)
        return rounded.astype(jnp.float32)

    def put(m, rows, columns, value, row_limit, column_limit):
        if not second:
            value = jnp.where(
                (block_row < row_limit) & (block_column < column_limit), value, 0.0
            )
        two_ref[m, rows, columns] = value.astype(jnp.bfloat16)

    w_empty, w_stay, w_swap, w_full = gate_terms(
        *(jnp.full((1, width), couplings[0, bond, term], jnp.float32) for term in range(3))
    )

    @pl.loop(0, count, unroll=min(UNROLL, count))
    def _(m):
        sector = first + m
        below_zero, below_one = left(m, 0, sector - 1), left(m, 1, sector - 1)
        here_zero, here_one = left(m + 1, 0, sector), left(m + 1, 1, sector)
        same_zero, same_one = right(m, 0), right(m, 1)
        next_zero, next_one = right(m + 1, 0), right(m + 1, 1)
        low, high = slice(0, width), slice(width, double)
        rows_low, rows_high = left_size(sector), left_size(sector - 1)
        columns_low, columns_high = right_size(sector), right_size(sector + 1)
        put(m, low, low, w_empty * product(here_zero, same_zero), rows_low, columns_low)
        put(
            m,
            low,
            high,
            w_stay * product(here_zero, next_one) + w_swap * product(here_one, next_zero),
            rows_low,
            columns_high,
        )
        put(
            m,
            high,
            low,
            w_swap * product(below_zero, same_one) + w_stay * product(below_one, same_zero),
            rows_high,
            columns_low,
        )
        put(m, high, high, w_full * product(below_one, next_one), rows_high, columns_high)
        sample = dot(sketch_ref[...], two_ref[m], LAST)
        keep_rows = row_index < ranks[0, bond, sector]
        sample = jnp.where(keep_rows, sample, 0.0)
        sample_ref[m] = sample
        high_part, middle_part, low_part = in_parts(sample)
        cross = dot(high_part, middle_part, LAST) + dot(high_part, low_part, LAST)
        gram = dot(high_part, high_part, LAST) + (
            dot(middle_part, middle_part, LAST) + (cross + jnp.transpose(cross))
        )
        gram_ref[m] = gram + jnp.where(eye & jnp.logical_not(keep_rows), 1.0, 0.0)

    lane = lax.broadcasted_iota(jnp.int32, (1, kept), 1)
    for tile in range(kept // LANES):
        @pl.loop(0, LANES // PANEL)
        def _(panel):
            first = pl.multiple_of(tile * LANES + panel * PANEL, PANEL)
            here = pl.ds(first, PANEL)
            stop = first + PANEL
            for m in range(count):
                for half in range(kept // LANES):
                    span = slice(half * LANES, (half + 1) * LANES)
                    rows_ref[half, pl.ds(m, PANEL, stride=SUB), :] = gram_ref[m, here, span]
            factor_panel(rows_ref, first, tile)
            for m in range(count):
                solved = jnp.concatenate(
                    [
                        rows_ref[half, pl.ds(m, PANEL, stride=SUB), :]
                        for half in range(kept // LANES)
                    ],
                    axis=1,
                )
                inverse_ref[m, here, :] = jnp.where(lane < stop, solved, 0.0)
                high, middle, low = in_parts(solved)
                one = jnp.concatenate([high, high, middle, middle, high, low], axis=0)
                two = jnp.concatenate([high, middle, high, middle, low, high], axis=0)
                change = dot(one, two, FIRST)
                kept_part = jnp.where((lane >= first) & (lane < stop), 0.0, gram_ref[m])
                gram_ref[m] = kept_part - change

    norm_ref[...] = jnp.zeros_like(norm_ref)

    @pl.loop(0, count, unroll=min(UNROLL, count))
    def _(m):
        inverse_high, inverse_middle, _ = in_parts(inverse_ref[m])
        sample_high, sample_middle, _ = in_parts(sample_ref[m])
        solved = dot(inverse_high, sample_high, PLAIN) + (
            dot(inverse_high, sample_middle, PLAIN) + dot(inverse_middle, sample_high, PLAIN)
        )
        solved = solved * math.sqrt(width)
        basis = solved.astype(jnp.bfloat16)
        if second:
            for s in range(2):
                turned = jnp.transpose(solved[:, s * width : (s + 1) * width])
                basis_ref[m, s] = turned.astype(jnp.bfloat16)
        else:
            basis_ref[m] = basis
        coef = dot(basis, two_ref[m], PLAIN)
        norm_ref[...] += jnp.sum(coef * coef, axis=0, keepdims=True)
        rounded = coef.astype(jnp.bfloat16)
        if second:
            for s in range(2):
                coef_ref[m, s] = rounded[:, s * width : (s + 1) * width]
        else:
            coef_ref[m] = rounded


    basis_first = basis_ref.at[pl.ds(0, 1)]
    coef_last = coef_ref.at[pl.ds(count - 1, 1)]
    if second:
        even, odd = [(basis_ref, send), (coef_ref, keep)], [(coef_ref, send), (basis_ref, keep)]
        if extras:
            even.append((basis_ref.at[pl.ds(0, 1), 1], extras[0]))
            odd.append((basis_ref.at[pl.ds(0, 1), 1], extras[0]))
    else:
        even, odd = [(coef_ref, send), (basis_ref, keep)], [(basis_ref, send), (coef_ref, keep)]
        even.append((coef_last if late else basis_first, extras[0]))
        odd.append((basis_first if late else coef_last, extras[0]))
    run_by_parity(even, odd, out_semaphores)


def pair_update(second, late, sizes, partner_sizes, ranks, couplings, operands, sketch_turned):
    kept, double = sketch_turned.shape
    width = double // 2
    sectors = sizes.shape[2] // lax.axis_size("block")
    half = sectors // 2
    early, next_early = chunk_sizes(half)
    part = next_early if second else early
    count = half - part if late else part
    block = (2, width, kept) if second else (kept, double)
    coef_block = (2, kept, width) if second else (kept, double)
    extra = [(1, kept, double)]
    if second:
        extra = [(1, width, kept)] if not late or next_early == 0 else []
    left_shape = (count + 1, kept, double) if second else (count + 1, 2, width, width)
    vmem = pl.BlockSpec(memory_space=pltpu.VMEM)
    smem = pl.BlockSpec(memory_space=pltpu.SMEM)
    anywhere = pl.BlockSpec(memory_space=pl.ANY)

    def kernel(*refs):
        pair_kernel(second, late, sectors, refs)

    return pl.pallas_call(
        kernel,
        out_shape=[
            jax.ShapeDtypeStruct((count, *block), jnp.bfloat16),
            jax.ShapeDtypeStruct((count, *block), jnp.bfloat16),
            jax.ShapeDtypeStruct((1, double), jnp.float32),
            *(jax.ShapeDtypeStruct(shape, jnp.bfloat16) for shape in extra),
        ],
        in_specs=[smem] * 4 + [anywhere] * len(operands) + [vmem],
        out_specs=[anywhere, anywhere, vmem] + [anywhere] * len(extra),
        scratch_shapes=[
            pltpu.VMEM(left_shape, jnp.bfloat16),
            pltpu.VMEM(left_shape, jnp.bfloat16),
            pltpu.VMEM((count, *block), jnp.bfloat16),
            pltpu.VMEM((count, *coef_block), jnp.bfloat16),
            pltpu.VMEM((count, double, double), jnp.bfloat16),
            pltpu.VMEM((count, kept, double), jnp.float32),
            pltpu.VMEM((count, kept, kept), jnp.float32),
            pltpu.VMEM((count, kept, kept), jnp.float32),
            pltpu.VMEM((kept // LANES, PANEL * SUB, LANES), jnp.float32),
            pltpu.SemaphoreType.DMA((8,)),
            pltpu.SemaphoreType.DMA((3,)),
        ],
        compiler_params=pltpu.CompilerParams(vmem_limit_bytes=32 * 2**20),
        cost_estimate=pl.CostEstimate(
            flops=(count + 12) * 50 * kept * double * double,
            bytes_accessed=8 * count * kept * double * 2,
            transcendentals=0,
        ),
    )(sizes, partner_sizes, ranks, couplings, *operands, sketch_turned)


def place_kernel(last, half, scale_ref, refs):
    _, early = chunk_sizes(half)
    late, sectors = half - early, 2 * half
    if last:
        returned_late, _, out, buffer, in_semaphores, out_semaphores = refs
        even_line = [(returned_late, half, late)]
        odd_line = [(returned_late, early, late)]
        lower_line = []
    else:
        if early:
            keep_late, lower, keep_early, returned_early = refs[:4]
            even_line = [(keep_early, 0, early), (keep_late, early, late), (returned_early, sectors - early, early)]
            odd_line = [(returned_early, 0, early), (keep_late, half, late), (keep_early, sectors - early, early)]
        else:
            keep_late, lower = refs[:2]
            even_line, odd_line = [(keep_late, 0, late)], [(keep_late, half, late)]
        lower_line = [(whole(lower), sectors, 1)]
        out, buffer, in_semaphores, out_semaphores = refs[-4:]
    target = out.at[0]
    zero_line = [(plane(ref, 0), start, size) for ref, start, size in odd_line]
    one_line = [(plane(ref, 1), start, size) for ref, start, size in odd_line]
    odd = cut(zero_line, 0, sectors, plane(target, 0))
    odd += cut(one_line + lower_line, 1, sectors, plane(target, 1))
    parts = even_line
    is_even = lax.rem(lax.axis_index("chain"), 2) == 0

    @pl.when(jnp.logical_not(is_even))
    def _():
        run_copies(odd, out_semaphores)

    @pl.when(is_even)
    def _():
        coming, going, filled = [], [], 0
        for index, (source, start, size) in enumerate(parts):
            room = buffer.at[pl.ds(filled, size)]
            coming.append(pltpu.make_async_copy(source, room, in_semaphores.at[index]))
            going.append(
                pltpu.make_async_copy(room, out.at[0, pl.ds(start, size)], out_semaphores.at[index])
            )
            filled += size
        for copy in coming:
            copy.start()
        filled = 0
        for index, (source, start, size) in enumerate(parts):
            coming[index].wait()

            @pl.loop(filled, filled + size)
            def _(sector):
                for s in range(2):
                    scaled = buffer[sector, s].astype(jnp.float32) * scale_ref[0]
                    buffer[sector, s] = scaled.astype(jnp.bfloat16)

            going[index].start()
            filled += size
        for copy in going:
            copy.wait()


def place(last, half, scale, operands, site):
    anywhere = pl.BlockSpec(memory_space=pl.ANY)
    _, early = chunk_sizes(half)
    rows = half - early if last else half + early

    def kernel(scale_ref, *refs):
        place_kernel(last, half, scale_ref, refs)

    return pl.pallas_call(
        kernel,
        out_shape=jax.ShapeDtypeStruct(site.shape, site.dtype),
        in_specs=[pl.BlockSpec(memory_space=pltpu.SMEM)] + [anywhere] * len(operands),
        out_specs=anywhere,
        scratch_shapes=[
            pltpu.VMEM((rows, *site.shape[2:]), site.dtype),
            pltpu.SemaphoreType.DMA((3,)),
            pltpu.SemaphoreType.DMA((7,)),
        ],
        input_output_aliases={2: 0} if last else {},
        compiler_params=pltpu.CompilerParams(vmem_limit_bytes=16 * 2**20),
        cost_estimate=pl.CostEstimate(
            flops=0, bytes_accessed=2 * rows * site.size // site.shape[1] * 2, transcendentals=0
        ),
    )(scale, *operands)


def move(value, target_of):
    sites, parts = lax.axis_size("chain"), lax.axis_size("block")
    pairs = []
    for site in range(sites):
        for part in range(parts):
            target = target_of(site, part)
            if target is not None and 0 <= target[1] < parts:
                pairs.append((site * parts + part, (target[0] % sites) * parts + target[1]))
    return lax.ppermute(value, ("chain", "block"), pairs)


def by_parity(even_target, odd_target):
    return lambda c, b: even_target(c, b) if c % 2 == 0 else odd_target(c, b)


def nowhere(c, b):
    return None


def joined(*parts):
    return jnp.concatenate(parts, axis=0)


def body(site_tensors, sketch, bond_sizes, kept_ranks, couplings):
    sectors = site_tensors.shape[1]
    half = sectors // 2
    early, next_early = chunk_sizes(half)
    width = site_tensors.shape[-1]
    kept = sketch.shape[1]
    parts = lax.axis_size("block")
    is_even = lax.axis_index("chain") % 2 == 0
    own = site_tensors[0]
    sketch_turned = jnp.transpose(sketch)

    def pick(even_value, odd_value):
        return jnp.where(is_even, even_value, odd_value)

    def update(second, late, *operands):
        return pair_update(
            second, late, bond_sizes, partner_sizes, kept_ranks, couplings, operands, sketch_turned
        )

    across = by_parity(lambda c, b: (c + 1, b), lambda c, b: (c - 1, b))
    got_early = move(pick(own[sectors - early - 1 :], own[: early + 1]), across)
    partner_sizes = move(bond_sizes, across)
    edge = move(
        pick(own[-1:], own[:1]), by_parity(lambda c, b: (c, b + 1), lambda c, b: (c, b - 1))
    )
    corner = move(own[-1:, 1], by_parity(nowhere, lambda c, b: (c - 1, b + 1)))
    sent = pick(own[half - 1 : sectors - early - 1], own[early + 1 : half + 1])
    sent, got_early = lax.optimization_barrier((sent, got_early))
    got_late = move(sent, across)
    send_early, keep_early, norm_early, halo_early = update(
        False, False, site_tensors, got_early, got_early, edge, corner
    )

    along = by_parity(lambda c, b: (c + 2, b), lambda c, b: (c - 2, b))
    far = move(
        halo_early, by_parity(lambda c, b: (c - 1, b - 1), lambda c, b: (c + 1, b + 1))
    )
    carried_early = move(send_early, along)
    send_late, keep_late, norm_late, halo_late = update(
        False, True, site_tensors, got_early, got_late, edge, corner
    )
    norm_even = jnp.sum(norm_early) + jnp.sum(norm_late)
    send_late, carried_early = lax.optimization_barrier((send_late, carried_early))
    near = move(halo_late, across)
    carried_late = move(send_late, along)

    back = by_parity(lambda c, b: (c - 1, b), lambda c, b: (c + 1, b))
    norm_odd = 0.0
    first_parts = ()
    if next_early:
        send_early, kept_early, norm_early, lower_first = update(
            True, False, keep_early, keep_early, carried_early, carried_early, far, far
        )
        norm_odd = jnp.sum(norm_early)
        send_early, carried_late = lax.optimization_barrier((send_early, carried_late))
        returned_early = move(send_early, back)
        first_parts = (kept_early, returned_early)
    send_late, kept_late, norm_late, *lower = update(
        True, True, keep_early, keep_late, carried_early, carried_late, far, near
    )
    if next_early == 0:
        lower_first = lower[0]
    lower_above = move(lower_first, by_parity(lambda c, b: (c - 1, b - 1), nowhere))
    if next_early:
        send_late, returned_early = lax.optimization_barrier((send_late, returned_early))
        first_parts = (kept_early, returned_early)
    returned_late = move(send_late, back)

    norm_odd = norm_odd + jnp.sum(norm_late)
    norms = lax.psum(jnp.stack([norm_even, norm_odd]), "block")
    from_left = move(norms, by_parity(nowhere, lambda c, b: (c + 1, b)))
    from_second = move(norms[:1], by_parity(lambda c, b: (c + 2, b), nowhere))
    target = float(sectors * parts * kept * width)
    scale = jnp.sqrt(target / (from_left[0] + from_second[0]))
    scale = scale * jnp.sqrt(target / (scale * scale * (norms[1] + from_left[1])))
    scale = scale[None]

    site = place(False, half, scale, (kept_late, lower_above, *first_parts), site_tensors)
    return place(True, half, scale, (returned_late, site), site_tensors)


def solution(mesh):
    placed = (
        P("chain", "block", None, None, None),
        P(),
        P("chain", None, None),
        P("chain", None, None),
        P("chain", None, None),
    )
    return jax.shard_map(
        body,
        mesh=mesh,
        in_specs=placed,
        out_specs=P("chain", "block", None, None, None),
        check_vma=False,
    )
```

```python
import math

import jax
import jax.numpy as jnp
from jax import lax
from jax.experimental import pallas as pl
from jax.experimental.pallas import tpu as pltpu
from jax.sharding import PartitionSpec as P

tau_step = 0.5
SUB = 8
LANES = 128
PANEL = 32
PART = 8
UNROLL = 2
FIRST = (((0,), (0,)), ((), ()))
LAST = (((1,), (1,)), ((), ()))
PLAIN = (((1,), (0,)), ((), ()))


def gate_terms(hopping, ising_term, field_term):
    rotation = 0.5 * tau_step * hopping
    middle_scale = jnp.exp(0.25 * tau_step * ising_term)
    weight_empty = jnp.exp(-tau_step * (0.25 * ising_term - 0.5 * field_term))
    weight_full = jnp.exp(-tau_step * (0.25 * ising_term + 0.5 * field_term))
    grown, shrunk = jnp.exp(rotation), jnp.exp(-rotation)
    weight_stay = middle_scale * (0.5 * (grown + shrunk))
    weight_swap = -middle_scale * (0.5 * (grown - shrunk))
    return weight_empty, weight_stay, weight_swap, weight_full


def dot(left, right, dims):
    return lax.dot_general(left, right, dims, preferred_element_type=jnp.float32)


def spread(row, lane_index):
    return jnp.take_along_axis(row, lane_index, axis=1)


def refined_reciprocal(value):
    guess = pltpu.reciprocal(value, approx=True)
    return guess * (2.0 - value * guess)


def factor_panel(rows_ref, first, tile):
    lanes = rows_ref.shape[0] * LANES
    lane = lax.broadcasted_iota(jnp.int32, (SUB, lanes), 1)
    zero = jnp.zeros((SUB, LANES), jnp.int32)
    mine = slice(tile * LANES, (tile + 1) * LANES)
    stop = first + PANEL

    def load(index):
        at = slice(index * SUB, (index + 1) * SUB)
        return jnp.concatenate([rows_ref[half, at, :] for half in range(lanes // LANES)], axis=1)

    def wide(value):
        return jnp.concatenate([value] * (lanes // LANES), axis=1)

    def store(index, value):
        at = slice(index * SUB, (index + 1) * SUB)
        for half in range(lanes // LANES):
            rows_ref[half, at, :] = value[:, half * LANES : (half + 1) * LANES]

    for start in range(0, PANEL, PART):
        rows = [load(start + i) for i in range(PART)]
        base = first - tile * LANES + start
        entry = [
            [spread(rows[i][:, mine], base + j + zero) if j >= i else None for j in range(PART)]
            for i in range(PART)
        ]
        later = []
        for step in range(PART):
            k = first + start + step
            inverted = refined_reciprocal(entry[step][step])
            unit = jnp.where(lane == k, 1.0, rows[step])
            for other in range(step + 1, PART):
                ratio = entry[step][other] * inverted
                for column in range(other, PART):
                    entry[other][column] = entry[other][column] - ratio * entry[step][column]
                rows[other] = jnp.where(lane == k, 0.0, rows[other]) - wide(ratio) * unit
            done = jnp.where((lane > k) & (lane < stop), 0.0, unit)
            store(start + step, done * wide(lax.rsqrt(entry[step][step])))
            hidden = jnp.where((lane > k) & (lane < first + start + PART), 0.0, unit)
            later.append(hidden * wide(inverted))
        for i in range(start + PART, PANEL):
            hide = (lane >= first + start) & (lane < first + start + PART)
            row = jnp.where(hide, 0.0, load(i))
            for step in range(PART):
                row = row - wide(spread(rows[step][:, mine], first - tile * LANES + i + zero)) * later[step]
            store(i, row)


def in_parts(value):
    high = value.astype(jnp.bfloat16)
    rest = value - high.astype(jnp.float32)
    middle = rest.astype(jnp.bfloat16)
    return high, middle, (rest - middle.astype(jnp.float32)).astype(jnp.bfloat16)


def run_copies(plan, semaphores):
    copies = [
        pltpu.make_async_copy(source, place, semaphores.at[index])
        for index, (source, place) in enumerate(plan)
    ]
    for copy in copies:
        copy.start()
    for copy in copies:
        copy.wait()


def run_by_parity(even_plan, odd_plan, semaphores):
    is_even = lax.rem(lax.axis_index("chain"), 2) == 0

    @pl.when(is_even)
    def _():
        run_copies(even_plan, semaphores)

    @pl.when(jnp.logical_not(is_even))
    def _():
        run_copies(odd_plan, semaphores)


def chunk_sizes(half):
    early = max(half // 2, 1)
    return early, early - 1


def cut(line, first, count, place):
    plan = []
    for source, start, size in line:
        low, high = max(first, start), min(first + count, start + size)
        if low < high:
            plan.append((source(low - start, high - low), place(low - first, high - low)))
    return plan


def whole(ref):
    return lambda start, size: ref.at[pl.ds(start, size)]


def plane(ref, s):
    return lambda start, size: ref.at[pl.ds(start, size), s]


def first_plans(first_of, count, half, early, operands, left, right):
    own, got_early, got_late, edge, corner = operands
    own = own.at[0]
    late, sectors = half - early, 2 * half

    def plans(first, left_line, right_line, extra):
        zero_line = [(plane(ref, 0), start, size) for ref, start, size in right_line]
        one_line = [(plane(ref, 1), start, size) for ref, start, size in right_line]
        return [
            *cut([(whole(ref), start, size) for ref, start, size in left_line], first - 1, count + 1, whole(left)),
            *cut(zero_line, first, count + 1, plane(right, 0)),
            *cut(one_line + extra, first - 1, count + 1, plane(right, 1)),
        ]

    even = plans(
        first_of[0],
        [(edge, -1, 1), (own, 0, sectors)],
        [(got_early, 0, early + 1), (got_late, early + 1, late)],
        [(whole(corner), -1, 1)],
    )
    odd = plans(
        first_of[1],
        [(got_late, half - 1, late), (got_early, sectors - early - 1, early + 1)],
        [(own, 0, sectors), (edge, sectors, 1)],
        [],
    )
    return even, odd


def second_plans(first_of, count, half, early, operands, left, right):
    keep_early, keep_late, carried_early, carried_late, far, near = operands
    late, sectors = half - early, 2 * half

    def plans(first, left_line, right_line):
        return [
            *cut([(whole(ref), start, size) for ref, start, size in left_line], first - 1, count + 1, whole(left)),
            *cut([(whole(ref), start, size) for ref, start, size in right_line], first, count + 1, whole(right)),
        ]

    even = plans(
        first_of[0],
        [(far, -1, 1), (carried_early, 0, early), (carried_late, early, late)],
        [(keep_early, 0, early), (keep_late, early, late), (near, half, 1)],
    )
    odd = plans(
        first_of[1],
        [(near, half - 1, 1), (keep_late, half, late), (keep_early, sectors - early, early)],
        [(carried_late, half, late), (carried_early, sectors - early, early), (far, sectors, 1)],
    )
    return even, odd


def pair_kernel(second, late, sectors, refs):
    half = sectors // 2
    early, next_early = chunk_sizes(half)
    part = next_early if second else early
    first_of = (part, half) if late else (0, sectors - part)
    sizes, partner_sizes, ranks, couplings = refs[:4]
    operand_count = 6 if second else 5
    operands = refs[4 : 4 + operand_count]
    sketch_ref = refs[4 + operand_count]
    outputs = refs[5 + operand_count : -9]
    (
        left_ref,
        right_ref,
        two_ref,
        sample_ref,
        gram_ref,
        inverse_ref,
        rows_ref,
        square_ref,
        in_semaphores,
    ) = refs[-9:]
    send, keep, norm_ref, *extras = outputs
    count, kept, double = sample_ref.shape
    width = double // 2
    plans = second_plans if second else first_plans
    run_by_parity(*plans(first_of, count, half, early, operands, left_ref, right_ref), in_semaphores)

    parity = lax.rem(lax.axis_index("chain"), 2)
    is_even = parity == 0
    first = lax.axis_index("block") * sectors + jnp.where(is_even, *first_of)
    bond = parity if second else 1 - parity
    total = sizes.shape[2]

    def left_size(sector):
        at = jnp.clip(sector, 0, total - 1)
        return jnp.where(is_even, sizes[0, 0, at], partner_sizes[0, 0, at])

    def middle_size(sector):
        at = jnp.clip(sector, 0, total - 1)
        size = jnp.where(is_even, sizes[0, 1, at], sizes[0, 0, at])
        return jnp.where(sector < total, size, 0)

    def right_size(sector):
        at = jnp.clip(sector, 0, total - 1)
        size = jnp.where(is_even, partner_sizes[0, 1, at], sizes[0, 1, at])
        return jnp.where(sector < total, size, 0)

    row_index = lax.broadcasted_iota(jnp.int32, (kept, 1), 0)
    eye = (
        lax.broadcasted_iota(jnp.int32, (kept, kept), 0)
        == lax.broadcasted_iota(jnp.int32, (kept, kept), 1)
    )
    block_row = lax.broadcasted_iota(jnp.int32, (width, width), 0)
    block_column = lax.broadcasted_iota(jnp.int32, (width, width), 1)
    column = lax.broadcasted_iota(jnp.int32, (1, width), 1)

    def left(m, s, sector):
        if second:
            return left_ref[m, :, s * width : (s + 1) * width]
        inside = (column < middle_size(sector + s)).astype(jnp.float32).astype(jnp.bfloat16)
        return left_ref[m, s] * inside

    def right(m, s):
        if second:
            return right_ref[m, :, s * width : (s + 1) * width]
        return right_ref[m, s]

    def product(a, b):
        rounded = dot(a, b, LAST if second else PLAIN).astype(jnp.bfloat16)
        return rounded.astype(jnp.float32)

    def put(m, rows, columns, value, row_limit, column_limit):
        if not second:
            value = jnp.where(
                (block_row < row_limit) & (block_column < column_limit), value, 0.0
            )
        two_ref[m, rows, columns] = value.astype(jnp.bfloat16)

    w_empty, w_stay, w_swap, w_full = gate_terms(
        *(jnp.full((1, width), couplings[0, bond, term], jnp.float32) for term in range(3))
    )

    @pl.loop(0, count, unroll=min(UNROLL, count))
    def _(m):
        sector = first + m
        below_zero, below_one = left(m, 0, sector - 1), left(m, 1, sector - 1)
        here_zero, here_one = left(m + 1, 0, sector), left(m + 1, 1, sector)
        same_zero, same_one = right(m, 0), right(m, 1)
        next_zero, next_one = right(m + 1, 0), right(m + 1, 1)
        low, high = slice(0, width), slice(width, double)
        rows_low, rows_high = left_size(sector), left_size(sector - 1)
        columns_low, columns_high = right_size(sector), right_size(sector + 1)
        put(m, low, low, w_empty * product(here_zero, same_zero), rows_low, columns_low)
        put(
            m,
            low,
            high,
            w_stay * product(here_zero, next_one) + w_swap * product(here_one, next_zero),
            rows_low,
            columns_high,
        )
        put(
            m,
            high,
            low,
            w_swap * product(below_zero, same_one) + w_stay * product(below_one, same_zero),
            rows_high,
            columns_low,
        )
        put(m, high, high, w_full * product(below_one, next_one), rows_high, columns_high)
        sample = dot(sketch_ref[...], two_ref[m], LAST)
        keep_rows = row_index < ranks[0, bond, sector]
        sample = jnp.where(keep_rows, sample, 0.0)
        sample_ref[m] = sample
        high_part, middle_part, low_part = in_parts(sample)
        cross = dot(high_part, middle_part, LAST) + dot(high_part, low_part, LAST)
        gram = dot(high_part, high_part, LAST) + (
            dot(middle_part, middle_part, LAST) + (cross + jnp.transpose(cross))
        )
        gram_ref[m] = gram + jnp.where(eye & jnp.logical_not(keep_rows), 1.0, 0.0)

    lane = lax.broadcasted_iota(jnp.int32, (1, kept), 1)
    for tile in range(kept // LANES):
        below = slice(tile * LANES, kept)

        @pl.loop(0, LANES // PANEL)
        def _(panel):
            first = pl.multiple_of(tile * LANES + panel * PANEL, PANEL)
            here = pl.ds(first, PANEL)
            stop = first + PANEL
            for m in range(count):
                for half in range(kept // LANES):
                    span = slice(half * LANES, (half + 1) * LANES)
                    rows_ref[half, pl.ds(m, PANEL, stride=SUB), :] = gram_ref[m, here, span]
            factor_panel(rows_ref, first, tile)
            for m in range(count):
                solved = jnp.concatenate(
                    [
                        rows_ref[half, pl.ds(m, PANEL, stride=SUB), :]
                        for half in range(kept // LANES)
                    ],
                    axis=1,
                )
                inverse_ref[m, here, :] = jnp.where(lane < stop, solved, 0.0)
                high, middle, low = in_parts(solved)
                one = jnp.concatenate([high, high, middle, middle, high, low], axis=0)[:, below]
                two = jnp.concatenate([high, middle, high, middle, low, high], axis=0)
                change = dot(one, two, FIRST)
                kept_part = jnp.where((lane >= first) & (lane < stop), 0.0, gram_ref[m, below, :])
                gram_ref[m, below, :] = kept_part - change

    square_ref[...] = jnp.zeros_like(square_ref)

    @pl.loop(0, count, unroll=min(UNROLL, count))
    def _(m):
        inverse_high, inverse_middle, _ = in_parts(inverse_ref[m])
        sample_high, sample_middle, _ = in_parts(sample_ref[m])
        solved = dot(inverse_high, sample_high, PLAIN) + (
            dot(inverse_high, sample_middle, PLAIN) + dot(inverse_middle, sample_high, PLAIN)
        )
        solved = solved * math.sqrt(width)
        basis = solved.astype(jnp.bfloat16)
        coef = dot(basis, two_ref[m], PLAIN)
        square_ref[...] += jnp.sum(coef * coef, axis=0, keepdims=True)
        if second:
            for s in range(2):
                span = slice(s * width, (s + 1) * width)
                turned = jnp.transpose(solved[:, span])
                send[m, s] = jnp.where(is_even, turned, coef[:, span]).astype(jnp.bfloat16)
                keep[m, s] = jnp.where(is_even, coef[:, span], turned).astype(jnp.bfloat16)
        else:
            send[m] = jnp.where(is_even, coef, solved).astype(jnp.bfloat16)
            keep[m] = jnp.where(is_even, solved, coef).astype(jnp.bfloat16)

    norm_ref[0] = jnp.sum(square_ref[...])
    if second:
        if extras:
            extras[0][0] = send[0, 1]
    else:
        at = jnp.where(is_even, count - 1, 0) if late else jnp.where(is_even, 0, count - 1)
        extras[0][0] = send[at] if late else keep[at]


def pair_update(second, late, sizes, partner_sizes, ranks, couplings, operands, sketch_turned):
    kept, double = sketch_turned.shape
    width = double // 2
    sectors = sizes.shape[2] // lax.axis_size("block")
    half = sectors // 2
    early, next_early = chunk_sizes(half)
    part = next_early if second else early
    count = half - part if late else part
    block = (2, width, kept) if second else (kept, double)
    extra = [(1, kept, double)]
    if second:
        extra = [(1, width, kept)] if not late or next_early == 0 else []
    left_shape = (count + 1, kept, double) if second else (count + 1, 2, width, width)
    vmem = pl.BlockSpec(memory_space=pltpu.VMEM)
    smem = pl.BlockSpec(memory_space=pltpu.SMEM)
    anywhere = pl.BlockSpec(memory_space=pl.ANY)

    def kernel(*refs):
        pair_kernel(second, late, sectors, refs)

    return pl.pallas_call(
        kernel,
        out_shape=[
            jax.ShapeDtypeStruct((count, *block), jnp.bfloat16),
            jax.ShapeDtypeStruct((count, *block), jnp.bfloat16),
            jax.ShapeDtypeStruct((1,), jnp.float32),
            *(jax.ShapeDtypeStruct(shape, jnp.bfloat16) for shape in extra),
        ],
        in_specs=[smem] * 4 + [anywhere] * len(operands) + [vmem],
        out_specs=[vmem, vmem, smem] + [vmem] * len(extra),
        scratch_shapes=[
            pltpu.VMEM(left_shape, jnp.bfloat16),
            pltpu.VMEM(left_shape, jnp.bfloat16),
            pltpu.VMEM((count, double, double), jnp.bfloat16),
            pltpu.VMEM((count, kept, double), jnp.float32),
            pltpu.VMEM((count, kept, kept), jnp.float32),
            pltpu.VMEM((count, kept, kept), jnp.float32),
            pltpu.VMEM((kept // LANES, PANEL * SUB, LANES), jnp.float32),
            pltpu.VMEM((1, double), jnp.float32),
            pltpu.SemaphoreType.DMA((8,)),
        ],
        compiler_params=pltpu.CompilerParams(vmem_limit_bytes=32 * 2**20),
        cost_estimate=pl.CostEstimate(
            flops=(count + 12) * 50 * kept * double * double,
            bytes_accessed=8 * count * kept * double * 2,
            transcendentals=0,
        ),
    )(sizes, partner_sizes, ranks, couplings, *operands, sketch_turned)


def place_kernel(last, half, target, norm_refs, refs):
    _, early = chunk_sizes(half)
    late, sectors = half - early, 2 * half
    if last:
        returned_late, _, out, buffer, in_semaphores, out_semaphores = refs
        even_line = [(returned_late, half, late)]
        odd_line = [(returned_late, early, late)]
        lower_line = []
    else:
        if early:
            keep_late, lower, keep_early, returned_early = refs[:4]
            even_line = [(keep_early, 0, early), (keep_late, early, late), (returned_early, sectors - early, early)]
            odd_line = [(returned_early, 0, early), (keep_late, half, late), (keep_early, sectors - early, early)]
        else:
            keep_late, lower = refs[:2]
            even_line, odd_line = [(keep_late, 0, late)], [(keep_late, half, late)]
        lower_line = [(whole(lower), sectors, 1)]
        out, buffer, in_semaphores, out_semaphores = refs[-4:]
    site = out.at[0]
    zero_line = [(plane(ref, 0), start, size) for ref, start, size in odd_line]
    one_line = [(plane(ref, 1), start, size) for ref, start, size in odd_line]
    odd = cut(zero_line, 0, sectors, plane(site, 0))
    odd += cut(one_line + lower_line, 1, sectors, plane(site, 1))
    parts = even_line
    is_even = lax.rem(lax.axis_index("chain"), 2) == 0

    @pl.when(jnp.logical_not(is_even))
    def _():
        run_copies(odd, out_semaphores)

    @pl.when(is_even)
    def _():
        norms, from_left, from_second = norm_refs
        rows = (1, buffer.shape[-1])
        norm_even = jnp.full(rows, from_left[0] + from_second[0], jnp.float32)
        norm_odd = jnp.full(rows, norms[1] + from_left[1], jnp.float32)
        scale_even = jnp.sqrt(target / norm_even)
        scale = scale_even * jnp.sqrt(target / (scale_even * scale_even * norm_odd))
        coming, going, filled = [], [], 0
        for index, (source, start, size) in enumerate(parts):
            room = buffer.at[pl.ds(filled, size)]
            coming.append(pltpu.make_async_copy(source, room, in_semaphores.at[index]))
            going.append(
                pltpu.make_async_copy(room, out.at[0, pl.ds(start, size)], out_semaphores.at[index])
            )
            filled += size
        for copy in coming:
            copy.start()
        filled = 0
        for index, (source, start, size) in enumerate(parts):
            coming[index].wait()

            @pl.loop(filled, filled + size)
            def _(sector):
                for s in range(2):
                    scaled = buffer[sector, s].astype(jnp.float32) * scale
                    buffer[sector, s] = scaled.astype(jnp.bfloat16)

            going[index].start()
            filled += size
        for copy in going:
            copy.wait()


def place(last, half, target, norms, operands, site):
    anywhere = pl.BlockSpec(memory_space=pl.ANY)
    _, early = chunk_sizes(half)
    rows = half - early if last else half + early

    def kernel(*refs):
        place_kernel(last, half, target, refs[:3], refs[3:])

    return pl.pallas_call(
        kernel,
        out_shape=jax.ShapeDtypeStruct(site.shape, site.dtype),
        in_specs=[pl.BlockSpec(memory_space=pltpu.SMEM)] * 3 + [anywhere] * len(operands),
        out_specs=anywhere,
        scratch_shapes=[
            pltpu.VMEM((rows, *site.shape[2:]), site.dtype),
            pltpu.SemaphoreType.DMA((3,)),
            pltpu.SemaphoreType.DMA((7,)),
        ],
        input_output_aliases={4: 0} if last else {},
        compiler_params=pltpu.CompilerParams(vmem_limit_bytes=16 * 2**20),
        cost_estimate=pl.CostEstimate(
            flops=0, bytes_accessed=2 * rows * site.size // site.shape[1] * 2, transcendentals=0
        ),
    )(*norms, *operands)


def move(value, target_of):
    sites, parts = lax.axis_size("chain"), lax.axis_size("block")
    pairs = []
    for site in range(sites):
        for part in range(parts):
            target = target_of(site, part)
            if target is not None and 0 <= target[1] < parts:
                pairs.append((site * parts + part, (target[0] % sites) * parts + target[1]))
    return lax.ppermute(value, ("chain", "block"), pairs)


def by_parity(even_target, odd_target):
    return lambda c, b: even_target(c, b) if c % 2 == 0 else odd_target(c, b)


def nowhere(c, b):
    return None


def joined(*parts):
    return jnp.concatenate(parts, axis=0)


def body(site_tensors, sketch, bond_sizes, kept_ranks, couplings):
    sectors = site_tensors.shape[1]
    half = sectors // 2
    early, next_early = chunk_sizes(half)
    width = site_tensors.shape[-1]
    kept = sketch.shape[1]
    parts = lax.axis_size("block")
    is_even = lax.axis_index("chain") % 2 == 0
    own = site_tensors[0]
    sketch_turned = jnp.transpose(sketch)

    def pick(even_value, odd_value):
        return jnp.where(is_even, even_value, odd_value)

    def update(second, late, *operands):
        return pair_update(
            second, late, bond_sizes, partner_sizes, kept_ranks, couplings, operands, sketch_turned
        )

    across = by_parity(lambda c, b: (c + 1, b), lambda c, b: (c - 1, b))
    got_early = move(pick(own[sectors - early - 1 :], own[: early + 1]), across)
    partner_sizes = move(bond_sizes, across)
    edge = move(
        pick(own[-1:], own[:1]), by_parity(lambda c, b: (c, b + 1), lambda c, b: (c, b - 1))
    )
    corner = move(own[-1:, 1], by_parity(nowhere, lambda c, b: (c - 1, b + 1)))
    sent = pick(own[half - 1 : sectors - early - 1], own[early + 1 : half + 1])
    sent, got_early = lax.optimization_barrier((sent, got_early))
    got_late = move(sent, across)
    send_early, keep_early, norm_early, halo_early = update(
        False, False, site_tensors, got_early, got_early, edge, corner
    )

    along = by_parity(lambda c, b: (c + 2, b), lambda c, b: (c - 2, b))
    far = move(
        halo_early, by_parity(lambda c, b: (c - 1, b - 1), lambda c, b: (c + 1, b + 1))
    )
    carried_early = move(send_early, along)
    send_late, keep_late, norm_late, halo_late = update(
        False, True, site_tensors, got_early, got_late, edge, corner
    )
    norm_even = norm_early + norm_late
    send_late, halo_late, carried_early = lax.optimization_barrier(
        (send_late, halo_late, carried_early)
    )
    carried_late = move(send_late, along)
    near = move(halo_late, across)

    back = by_parity(lambda c, b: (c - 1, b), lambda c, b: (c + 1, b))
    norm_odd = 0.0
    first_parts = ()
    if next_early:
        send_early, kept_early, norm_early, lower_first = update(
            True, False, keep_early, keep_early, carried_early, carried_early, far, far
        )
        norm_odd = norm_early
        send_early, carried_late = lax.optimization_barrier((send_early, carried_late))
        returned_early = move(send_early, back)
        first_parts = (kept_early, returned_early)
    send_late, kept_late, norm_late, *lower = update(
        True, True, keep_early, keep_late, carried_early, carried_late, far, near
    )
    if next_early == 0:
        lower_first = lower[0]
    lower_above = move(lower_first, by_parity(lambda c, b: (c - 1, b - 1), nowhere))
    if next_early:
        send_late, returned_early = lax.optimization_barrier((send_late, returned_early))
        first_parts = (kept_early, returned_early)
    returned_late = move(send_late, back)

    norms = lax.psum(joined(norm_even, norm_odd + norm_late), "block")
    from_left = move(norms, by_parity(nowhere, lambda c, b: (c + 1, b)))
    from_second = move(norms, by_parity(lambda c, b: (c + 2, b), nowhere))
    target = float(sectors * parts * kept * width)
    norms = (norms, from_left, from_second)

    site = place(False, half, target, norms, (kept_late, lower_above, *first_parts), site_tensors)
    return place(True, half, target, norms, (returned_late, site), site_tensors)


def solution(mesh):
    placed = (
        P("chain", "block", None, None, None),
        P(),
        P("chain", None, None),
        P("chain", None, None),
        P("chain", None, None),
    )
    return jax.shard_map(
        body,
        mesh=mesh,
        in_specs=placed,
        out_specs=P("chain", "block", None, None, None),
        check_vma=False,
    )
```

```python
import math

import jax
import jax.numpy as jnp
from jax import lax
from jax.experimental import pallas as pl
from jax.experimental.pallas import tpu as pltpu
from jax.sharding import PartitionSpec as P

tau_step = 0.5
SUB = 8
LANES = 128
PANEL = 32
PART = 8
UNROLL = 2
FIRST = (((0,), (0,)), ((), ()))
LAST = (((1,), (1,)), ((), ()))
PLAIN = (((1,), (0,)), ((), ()))


def gate_terms(hopping, ising_term, field_term):
    rotation = 0.5 * tau_step * hopping
    middle_scale = jnp.exp(0.25 * tau_step * ising_term)
    weight_empty = jnp.exp(-tau_step * (0.25 * ising_term - 0.5 * field_term))
    weight_full = jnp.exp(-tau_step * (0.25 * ising_term + 0.5 * field_term))
    grown, shrunk = jnp.exp(rotation), jnp.exp(-rotation)
    weight_stay = middle_scale * (0.5 * (grown + shrunk))
    weight_swap = -middle_scale * (0.5 * (grown - shrunk))
    return weight_empty, weight_stay, weight_swap, weight_full


def dot(left, right, dims):
    return lax.dot_general(left, right, dims, preferred_element_type=jnp.float32)


def spread(row, lane_index):
    return jnp.take_along_axis(row, lane_index, axis=1)


def refined_reciprocal(value):
    guess = pltpu.reciprocal(value, approx=True)
    return guess * (2.0 - value * guess)


def factor_panel(rows_ref, first, tile):
    lanes = rows_ref.shape[0] * LANES
    lane = lax.broadcasted_iota(jnp.int32, (SUB, lanes), 1)
    zero = jnp.zeros((SUB, LANES), jnp.int32)
    mine = slice(tile * LANES, (tile + 1) * LANES)
    stop = first + PANEL

    def load(index):
        at = slice(index * SUB, (index + 1) * SUB)
        return jnp.concatenate([rows_ref[half, at, :] for half in range(lanes // LANES)], axis=1)

    def wide(value):
        return jnp.concatenate([value] * (lanes // LANES), axis=1)

    def store(index, value):
        at = slice(index * SUB, (index + 1) * SUB)
        for half in range(lanes // LANES):
            rows_ref[half, at, :] = value[:, half * LANES : (half + 1) * LANES]

    for start in range(0, PANEL, PART):
        rows = [load(start + i) for i in range(PART)]
        base = first - tile * LANES + start
        entry = [
            [spread(rows[i][:, mine], base + j + zero) if j >= i else None for j in range(PART)]
            for i in range(PART)
        ]
        later = []
        for step in range(PART):
            k = first + start + step
            inverted = refined_reciprocal(entry[step][step])
            unit = jnp.where(lane == k, 1.0, rows[step])
            for other in range(step + 1, PART):
                ratio = entry[step][other] * inverted
                for column in range(other, PART):
                    entry[other][column] = entry[other][column] - ratio * entry[step][column]
                rows[other] = jnp.where(lane == k, 0.0, rows[other]) - wide(ratio) * unit
            done = jnp.where((lane > k) & (lane < stop), 0.0, unit)
            store(start + step, done * wide(lax.rsqrt(entry[step][step])))
            hidden = jnp.where((lane > k) & (lane < first + start + PART), 0.0, unit)
            later.append(hidden * wide(inverted))
        for i in range(start + PART, PANEL):
            hide = (lane >= first + start) & (lane < first + start + PART)
            row = jnp.where(hide, 0.0, load(i))
            for step in range(PART):
                row = row - wide(spread(rows[step][:, mine], first - tile * LANES + i + zero)) * later[step]
            store(i, row)


def in_parts(value):
    high = value.astype(jnp.bfloat16)
    rest = value - high.astype(jnp.float32)
    middle = rest.astype(jnp.bfloat16)
    return high, middle, (rest - middle.astype(jnp.float32)).astype(jnp.bfloat16)


def run_copies(plan, semaphores):
    copies = [
        pltpu.make_async_copy(source, place, semaphores.at[index])
        for index, (source, place) in enumerate(plan)
    ]
    for copy in copies:
        copy.start()
    for copy in copies:
        copy.wait()


def run_by_parity(even_plan, odd_plan, semaphores):
    is_even = lax.rem(lax.axis_index("chain"), 2) == 0

    @pl.when(is_even)
    def _():
        run_copies(even_plan, semaphores)

    @pl.when(jnp.logical_not(is_even))
    def _():
        run_copies(odd_plan, semaphores)


def chunk_sizes(half):
    early = max(half // 2, 1)
    return early, early - 1


def cut(line, first, count, place):
    plan = []
    for source, start, size in line:
        low, high = max(first, start), min(first + count, start + size)
        if low < high:
            plan.append((source(low - start, high - low), place(low - first, high - low)))
    return plan


def whole(ref):
    return lambda start, size: ref.at[pl.ds(start, size)]


def plane(ref, s):
    return lambda start, size: ref.at[pl.ds(start, size), s]


def first_plans(first_of, count, half, early, operands, left, right):
    own, got_early, got_late, edge, corner = operands
    own = own.at[0]
    late, sectors = half - early, 2 * half

    def plans(first, left_line, right_line, extra):
        zero_line = [(plane(ref, 0), start, size) for ref, start, size in right_line]
        one_line = [(plane(ref, 1), start, size) for ref, start, size in right_line]
        return [
            *cut([(whole(ref), start, size) for ref, start, size in left_line], first - 1, count + 1, whole(left)),
            *cut(zero_line, first, count + 1, plane(right, 0)),
            *cut(one_line + extra, first - 1, count + 1, plane(right, 1)),
        ]

    even = plans(
        first_of[0],
        [(edge, -1, 1), (own, 0, sectors)],
        [(got_early, 0, early + 1), (got_late, early + 1, late)],
        [(whole(corner), -1, 1)],
    )
    odd = plans(
        first_of[1],
        [(got_late, half - 1, late), (got_early, sectors - early - 1, early + 1)],
        [(own, 0, sectors), (edge, sectors, 1)],
        [],
    )
    return even, odd


def second_plans(first_of, count, half, early, operands, left, right):
    keep_early, keep_late, carried_early, carried_late, far, near = operands
    late, sectors = half - early, 2 * half

    def plans(first, left_line, right_line):
        return [
            *cut([(whole(ref), start, size) for ref, start, size in left_line], first - 1, count + 1, whole(left)),
            *cut([(whole(ref), start, size) for ref, start, size in right_line], first, count + 1, whole(right)),
        ]

    even = plans(
        first_of[0],
        [(far, -1, 1), (carried_early, 0, early), (carried_late, early, late)],
        [(keep_early, 0, early), (keep_late, early, late), (near, half, 1)],
    )
    odd = plans(
        first_of[1],
        [(near, half - 1, 1), (keep_late, half, late), (keep_early, sectors - early, early)],
        [(carried_late, half, late), (carried_early, sectors - early, early), (far, sectors, 1)],
    )
    return even, odd


def pair_kernel(second, late, sectors, refs):
    half = sectors // 2
    early, next_early = chunk_sizes(half)
    part = next_early if second else early
    first_of = (part, half) if late else (0, sectors - part)
    sizes, partner_sizes, ranks, couplings = refs[:4]
    operand_count = 6 if second else 5
    operands = refs[4 : 4 + operand_count]
    sketch_ref = refs[4 + operand_count]
    outputs = refs[5 + operand_count : -9]
    (
        left_ref,
        right_ref,
        two_ref,
        sample_ref,
        gram_ref,
        inverse_ref,
        rows_ref,
        square_ref,
        in_semaphores,
    ) = refs[-9:]
    if second and late:
        send, send_last, keep, norm_ref, *extras = outputs
    else:
        send, keep, norm_ref, *extras = outputs
    count, kept, double = sample_ref.shape
    width = double // 2
    plans = second_plans if second else first_plans
    run_by_parity(*plans(first_of, count, half, early, operands, left_ref, right_ref), in_semaphores)

    parity = lax.rem(lax.axis_index("chain"), 2)
    is_even = parity == 0
    first = lax.axis_index("block") * sectors + jnp.where(is_even, *first_of)
    bond = parity if second else 1 - parity
    total = sizes.shape[2]

    def left_size(sector):
        at = jnp.clip(sector, 0, total - 1)
        return jnp.where(is_even, sizes[0, 0, at], partner_sizes[0, 0, at])

    def middle_size(sector):
        at = jnp.clip(sector, 0, total - 1)
        size = jnp.where(is_even, sizes[0, 1, at], sizes[0, 0, at])
        return jnp.where(sector < total, size, 0)

    def right_size(sector):
        at = jnp.clip(sector, 0, total - 1)
        size = jnp.where(is_even, partner_sizes[0, 1, at], sizes[0, 1, at])
        return jnp.where(sector < total, size, 0)

    row_index = lax.broadcasted_iota(jnp.int32, (kept, 1), 0)
    eye = (
        lax.broadcasted_iota(jnp.int32, (kept, kept), 0)
        == lax.broadcasted_iota(jnp.int32, (kept, kept), 1)
    )
    block_row = lax.broadcasted_iota(jnp.int32, (width, width), 0)
    block_column = lax.broadcasted_iota(jnp.int32, (width, width), 1)
    column = lax.broadcasted_iota(jnp.int32, (1, width), 1)

    def left(m, s, sector):
        if second:
            return left_ref[m, :, s * width : (s + 1) * width]
        inside = (column < middle_size(sector + s)).astype(jnp.float32).astype(jnp.bfloat16)
        return left_ref[m, s] * inside

    def right(m, s):
        if second:
            return right_ref[m, :, s * width : (s + 1) * width]
        return right_ref[m, s]

    def product(a, b):
        rounded = dot(a, b, LAST if second else PLAIN).astype(jnp.bfloat16)
        return rounded.astype(jnp.float32)

    def put(m, rows, columns, value, row_limit, column_limit):
        if not second:
            value = jnp.where(
                (block_row < row_limit) & (block_column < column_limit), value, 0.0
            )
        two_ref[m, rows, columns] = value.astype(jnp.bfloat16)

    w_empty, w_stay, w_swap, w_full = gate_terms(
        *(jnp.full((1, width), couplings[0, bond, term], jnp.float32) for term in range(3))
    )

    @pl.loop(0, count, unroll=min(UNROLL, count))
    def _(m):
        sector = first + m
        below_zero, below_one = left(m, 0, sector - 1), left(m, 1, sector - 1)
        here_zero, here_one = left(m + 1, 0, sector), left(m + 1, 1, sector)
        same_zero, same_one = right(m, 0), right(m, 1)
        next_zero, next_one = right(m + 1, 0), right(m + 1, 1)
        low, high = slice(0, width), slice(width, double)
        rows_low, rows_high = left_size(sector), left_size(sector - 1)
        columns_low, columns_high = right_size(sector), right_size(sector + 1)
        put(m, low, low, w_empty * product(here_zero, same_zero), rows_low, columns_low)
        put(
            m,
            low,
            high,
            w_stay * product(here_zero, next_one) + w_swap * product(here_one, next_zero),
            rows_low,
            columns_high,
        )
        put(
            m,
            high,
            low,
            w_swap * product(below_zero, same_one) + w_stay * product(below_one, same_zero),
            rows_high,
            columns_low,
        )
        put(m, high, high, w_full * product(below_one, next_one), rows_high, columns_high)
        sample = dot(sketch_ref[...], two_ref[m], LAST)
        keep_rows = row_index < ranks[0, bond, sector]
        sample = jnp.where(keep_rows, sample, 0.0)
        sample_ref[m] = sample
        high_part, middle_part, low_part = in_parts(sample)
        cross = dot(high_part, middle_part, LAST) + dot(high_part, low_part, LAST)
        gram = dot(high_part, high_part, LAST) + (
            dot(middle_part, middle_part, LAST) + (cross + jnp.transpose(cross))
        )
        gram_ref[m] = gram + jnp.where(eye & jnp.logical_not(keep_rows), 1.0, 0.0)

    lane = lax.broadcasted_iota(jnp.int32, (1, kept), 1)
    for tile in range(kept // LANES):
        below = slice(tile * LANES, kept)

        @pl.loop(0, LANES // PANEL)
        def _(panel):
            first = pl.multiple_of(tile * LANES + panel * PANEL, PANEL)
            here = pl.ds(first, PANEL)
            stop = first + PANEL
            for m in range(count):
                for half in range(kept // LANES):
                    span = slice(half * LANES, (half + 1) * LANES)
                    rows_ref[half, pl.ds(m, PANEL, stride=SUB), :] = gram_ref[m, here, span]
            factor_panel(rows_ref, first, tile)
            for m in range(count):
                solved = jnp.concatenate(
                    [
                        rows_ref[half, pl.ds(m, PANEL, stride=SUB), :]
                        for half in range(kept // LANES)
                    ],
                    axis=1,
                )
                inverse_ref[m, here, :] = jnp.where(lane < stop, solved, 0.0)
                high, middle, low = in_parts(solved)
                one = jnp.concatenate([high, high, middle, middle, high, low], axis=0)[:, below]
                two = jnp.concatenate([high, middle, high, middle, low, high], axis=0)
                change = dot(one, two, FIRST)
                kept_part = jnp.where((lane >= first) & (lane < stop), 0.0, gram_ref[m, below, :])
                gram_ref[m, below, :] = kept_part - change

    square_ref[...] = jnp.zeros_like(square_ref)

    def finish(m, send, place):
        inverse_high, inverse_middle, _ = in_parts(inverse_ref[m])
        sample_high, sample_middle, _ = in_parts(sample_ref[m])
        solved = dot(inverse_high, sample_high, PLAIN) + (
            dot(inverse_high, sample_middle, PLAIN) + dot(inverse_middle, sample_high, PLAIN)
        )
        solved = solved * math.sqrt(width)
        basis = solved.astype(jnp.bfloat16)
        coef = dot(basis, two_ref[m], PLAIN)
        square_ref[...] += jnp.sum(coef * coef, axis=0, keepdims=True)
        if second:
            for s in range(2):
                span = slice(s * width, (s + 1) * width)
                turned = jnp.transpose(solved[:, span])
                send[place, s] = jnp.where(is_even, turned, coef[:, span]).astype(jnp.bfloat16)
                keep[m, s] = jnp.where(is_even, coef[:, span], turned).astype(jnp.bfloat16)
        else:
            send[place] = jnp.where(is_even, coef, solved).astype(jnp.bfloat16)
            keep[m] = jnp.where(is_even, solved, coef).astype(jnp.bfloat16)

    pieces = [(0, send.shape[0], send)]
    if second and late:
        pieces.append((send.shape[0], send_last.shape[0], send_last))
    for start, size, piece in pieces:

        @pl.loop(0, size, unroll=min(UNROLL, size))
        def _(index, start=start, piece=piece):
            finish(start + index, piece, index)

    norm_ref[0] = jnp.sum(square_ref[...])
    if second:
        if extras:
            extras[0][0] = send[0, 1]
    else:
        at = jnp.where(is_even, count - 1, 0) if late else jnp.where(is_even, 0, count - 1)
        extras[0][0] = send[at] if late else keep[at]


def pair_update(second, late, sizes, partner_sizes, ranks, couplings, operands, sketch_turned):
    kept, double = sketch_turned.shape
    width = double // 2
    sectors = sizes.shape[2] // lax.axis_size("block")
    half = sectors // 2
    early, next_early = chunk_sizes(half)
    part = next_early if second else early
    count = half - part if late else part
    block = (2, width, kept) if second else (kept, double)
    extra = [(1, kept, double)]
    if second:
        extra = [(1, width, kept)] if not late or next_early == 0 else []
    pieces = [count]
    if second and late:
        pieces = [count - count // 2, count // 2]
    left_shape = (count + 1, kept, double) if second else (count + 1, 2, width, width)
    vmem = pl.BlockSpec(memory_space=pltpu.VMEM)
    smem = pl.BlockSpec(memory_space=pltpu.SMEM)
    anywhere = pl.BlockSpec(memory_space=pl.ANY)

    def kernel(*refs):
        pair_kernel(second, late, sectors, refs)

    return pl.pallas_call(
        kernel,
        out_shape=[
            *(jax.ShapeDtypeStruct((size, *block), jnp.bfloat16) for size in pieces),
            jax.ShapeDtypeStruct((count, *block), jnp.bfloat16),
            jax.ShapeDtypeStruct((1,), jnp.float32),
            *(jax.ShapeDtypeStruct(shape, jnp.bfloat16) for shape in extra),
        ],
        in_specs=[smem] * 4 + [anywhere] * len(operands) + [vmem],
        out_specs=[vmem] * len(pieces) + [vmem, smem] + [vmem] * len(extra),
        scratch_shapes=[
            pltpu.VMEM(left_shape, jnp.bfloat16),
            pltpu.VMEM(left_shape, jnp.bfloat16),
            pltpu.VMEM((count, double, double), jnp.bfloat16),
            pltpu.VMEM((count, kept, double), jnp.float32),
            pltpu.VMEM((count, kept, kept), jnp.float32),
            pltpu.VMEM((count, kept, kept), jnp.float32),
            pltpu.VMEM((kept // LANES, PANEL * SUB, LANES), jnp.float32),
            pltpu.VMEM((1, double), jnp.float32),
            pltpu.SemaphoreType.DMA((8,)),
        ],
        compiler_params=pltpu.CompilerParams(vmem_limit_bytes=32 * 2**20),
        cost_estimate=pl.CostEstimate(
            flops=(count + 12) * 50 * kept * double * double,
            bytes_accessed=8 * count * kept * double * 2,
            transcendentals=0,
        ),
    )(sizes, partner_sizes, ranks, couplings, *operands, sketch_turned)


def place_kernel(last, half, target, norm_refs, refs):
    _, early = chunk_sizes(half)
    late, sectors = half - early, 2 * half
    final = late // 2
    main = late - final
    if last:
        returned_last, _, out, buffer, in_semaphores, out_semaphores = refs
        even_line = [(returned_last, half + main, final)]
        odd_line = [(returned_last, early + main, final)]
        lower_line = []
    else:
        keep_late, returned_late, lower = refs[:3]
        even_line = [(keep_late, early, late), (returned_late, half, main)]
        odd_line = [(returned_late, early, main), (keep_late, half, late)]
        if early:
            keep_early, returned_early = refs[3:5]
            even_line += [(keep_early, 0, early), (returned_early, sectors - early, early)]
            odd_line += [(returned_early, 0, early), (keep_early, sectors - early, early)]
        lower_line = [(whole(lower), sectors, 1)]
        out, buffer, in_semaphores, out_semaphores = refs[-4:]
    site = out.at[0]
    zero_line = [(plane(ref, 0), start, size) for ref, start, size in odd_line]
    one_line = [(plane(ref, 1), start, size) for ref, start, size in odd_line]
    odd = cut(zero_line, 0, sectors, plane(site, 0))
    odd += cut(one_line + lower_line, 1, sectors, plane(site, 1))
    parts = even_line
    is_even = lax.rem(lax.axis_index("chain"), 2) == 0

    @pl.when(jnp.logical_not(is_even))
    def _():
        run_copies(odd, out_semaphores)

    @pl.when(is_even)
    def _():
        norms, from_left, from_second = norm_refs
        rows = (1, buffer.shape[-1])
        norm_even = jnp.full(rows, from_left[0] + from_second[0], jnp.float32)
        norm_odd = jnp.full(rows, norms[1] + from_left[1], jnp.float32)
        scale_even = jnp.sqrt(target / norm_even)
        scale = scale_even * jnp.sqrt(target / (scale_even * scale_even * norm_odd))
        coming, going, filled = [], [], 0
        for index, (source, start, size) in enumerate(parts):
            room = buffer.at[pl.ds(filled, size)]
            coming.append(pltpu.make_async_copy(source, room, in_semaphores.at[index]))
            going.append(
                pltpu.make_async_copy(room, out.at[0, pl.ds(start, size)], out_semaphores.at[index])
            )
            filled += size
        for copy in coming:
            copy.start()
        filled = 0
        for index, (source, start, size) in enumerate(parts):
            coming[index].wait()

            @pl.loop(filled, filled + size)
            def _(sector):
                for s in range(2):
                    scaled = buffer[sector, s].astype(jnp.float32) * scale
                    buffer[sector, s] = scaled.astype(jnp.bfloat16)

            going[index].start()
            filled += size
        for copy in going:
            copy.wait()


def place(last, half, target, norms, operands, site):
    anywhere = pl.BlockSpec(memory_space=pl.ANY)
    _, early = chunk_sizes(half)
    final = (half - early) // 2
    rows = final if last else 2 * half - final

    def kernel(*refs):
        place_kernel(last, half, target, refs[:3], refs[3:])

    return pl.pallas_call(
        kernel,
        out_shape=jax.ShapeDtypeStruct(site.shape, site.dtype),
        in_specs=[pl.BlockSpec(memory_space=pltpu.SMEM)] * 3 + [anywhere] * len(operands),
        out_specs=anywhere,
        scratch_shapes=[
            pltpu.VMEM((rows, *site.shape[2:]), site.dtype),
            pltpu.SemaphoreType.DMA((4,)),
            pltpu.SemaphoreType.DMA((9,)),
        ],
        input_output_aliases={4: 0} if last else {},
        compiler_params=pltpu.CompilerParams(vmem_limit_bytes=16 * 2**20),
        cost_estimate=pl.CostEstimate(
            flops=0, bytes_accessed=2 * rows * site.size // site.shape[1] * 2, transcendentals=0
        ),
    )(*norms, *operands)


def move(value, target_of):
    sites, parts = lax.axis_size("chain"), lax.axis_size("block")
    pairs = []
    for site in range(sites):
        for part in range(parts):
            target = target_of(site, part)
            if target is not None and 0 <= target[1] < parts:
                pairs.append((site * parts + part, (target[0] % sites) * parts + target[1]))
    return lax.ppermute(value, ("chain", "block"), pairs)


def by_parity(even_target, odd_target):
    return lambda c, b: even_target(c, b) if c % 2 == 0 else odd_target(c, b)


def nowhere(c, b):
    return None


def joined(*parts):
    return jnp.concatenate(parts, axis=0)


def body(site_tensors, sketch, bond_sizes, kept_ranks, couplings):
    sectors = site_tensors.shape[1]
    half = sectors // 2
    early, next_early = chunk_sizes(half)
    width = site_tensors.shape[-1]
    kept = sketch.shape[1]
    parts = lax.axis_size("block")
    is_even = lax.axis_index("chain") % 2 == 0
    own = site_tensors[0]
    sketch_turned = jnp.transpose(sketch)

    def pick(even_value, odd_value):
        return jnp.where(is_even, even_value, odd_value)

    def update(second, late, *operands):
        return pair_update(
            second, late, bond_sizes, partner_sizes, kept_ranks, couplings, operands, sketch_turned
        )

    across = by_parity(lambda c, b: (c + 1, b), lambda c, b: (c - 1, b))
    got_early = move(pick(own[sectors - early - 1 :], own[: early + 1]), across)
    partner_sizes = move(bond_sizes, across)
    edge = move(
        pick(own[-1:], own[:1]), by_parity(lambda c, b: (c, b + 1), lambda c, b: (c, b - 1))
    )
    corner = move(own[-1:, 1], by_parity(nowhere, lambda c, b: (c - 1, b + 1)))
    sent = pick(own[half - 1 : sectors - early - 1], own[early + 1 : half + 1])
    sent, got_early = lax.optimization_barrier((sent, got_early))
    got_late = move(sent, across)
    send_early, keep_early, norm_early, halo_early = update(
        False, False, site_tensors, got_early, got_early, edge, corner
    )

    along = by_parity(lambda c, b: (c + 2, b), lambda c, b: (c - 2, b))
    far = move(
        halo_early, by_parity(lambda c, b: (c - 1, b - 1), lambda c, b: (c + 1, b + 1))
    )
    carried_early = move(send_early, along)
    send_late, keep_late, norm_late, halo_late = update(
        False, True, site_tensors, got_early, got_late, edge, corner
    )
    norm_even = norm_early + norm_late
    carried_late = move(send_late, along)
    near = move(halo_late, across)

    back = by_parity(lambda c, b: (c - 1, b), lambda c, b: (c + 1, b))
    norm_odd = 0.0
    first_parts = ()
    if next_early:
        send_early, kept_early, norm_early, lower_first = update(
            True, False, keep_early, keep_early, carried_early, carried_early, far, far
        )
        norm_odd = norm_early
        send_early, carried_late = lax.optimization_barrier((send_early, carried_late))
        returned_early = move(send_early, back)
        first_parts = (kept_early, returned_early)
    send_late, send_last, kept_late, norm_late, *lower = update(
        True, True, keep_early, keep_late, carried_early, carried_late, far, near
    )
    if next_early == 0:
        lower_first = lower[0]
    lower_above = move(lower_first, by_parity(lambda c, b: (c - 1, b - 1), nowhere))
    if next_early:
        send_late, returned_early, lower_above = lax.optimization_barrier(
            (send_late, returned_early, lower_above)
        )
        first_parts = (kept_early, returned_early)
    returned_late = move(send_late, back)

    norms = lax.psum(joined(norm_even, norm_odd + norm_late), "block")
    from_left = move(norms, by_parity(nowhere, lambda c, b: (c + 1, b)))
    from_second = move(norms, by_parity(lambda c, b: (c + 2, b), nowhere))
    send_last, from_left, from_second = lax.optimization_barrier(
        (send_last, from_left, from_second)
    )
    returned_last = move(send_last, back)
    target = float(sectors * parts * kept * width)
    norms = (norms, from_left, from_second)
    ready = (kept_late, returned_late, lower_above, *first_parts)
    site = place(False, half, target, norms, ready, site_tensors)
    return place(True, half, target, norms, (returned_last, site), site_tensors)


def solution(mesh):
    placed = (
        P("chain", "block", None, None, None),
        P(),
        P("chain", None, None),
        P("chain", None, None),
        P("chain", None, None),
    )
    return jax.shard_map(
        body,
        mesh=mesh,
        in_specs=placed,
        out_specs=P("chain", "block", None, None, None),
        check_vma=False,
    )
```

```python
import math

import jax
import jax.numpy as jnp
from jax import lax
from jax.experimental import pallas as pl
from jax.experimental.pallas import tpu as pltpu
from jax.sharding import PartitionSpec as P

tau_step = 0.5
SUB = 8
LANES = 128
PANEL = 32
PART = 8
UNROLL = 2
FIRST = (((0,), (0,)), ((), ()))
LAST = (((1,), (1,)), ((), ()))
PLAIN = (((1,), (0,)), ((), ()))


def gate_terms(hopping, ising_term, field_term):
    rotation = 0.5 * tau_step * hopping
    middle_scale = jnp.exp(0.25 * tau_step * ising_term)
    weight_empty = jnp.exp(-tau_step * (0.25 * ising_term - 0.5 * field_term))
    weight_full = jnp.exp(-tau_step * (0.25 * ising_term + 0.5 * field_term))
    grown, shrunk = jnp.exp(rotation), jnp.exp(-rotation)
    weight_stay = middle_scale * (0.5 * (grown + shrunk))
    weight_swap = -middle_scale * (0.5 * (grown - shrunk))
    return weight_empty, weight_stay, weight_swap, weight_full


def dot(left, right, dims):
    return lax.dot_general(left, right, dims, preferred_element_type=jnp.float32)


def spread(row, lane_index):
    return jnp.take_along_axis(row, lane_index, axis=1)


def refined_reciprocal(value):
    guess = pltpu.reciprocal(value, approx=True)
    return guess * (2.0 - value * guess)


def factor_panel(rows_ref, first, tile):
    lanes = rows_ref.shape[0] * LANES
    lane = lax.broadcasted_iota(jnp.int32, (SUB, lanes), 1)
    zero = jnp.zeros((SUB, LANES), jnp.int32)
    mine = slice(tile * LANES, (tile + 1) * LANES)
    stop = first + PANEL

    def load(index):
        at = slice(index * SUB, (index + 1) * SUB)
        return jnp.concatenate([rows_ref[half, at, :] for half in range(lanes // LANES)], axis=1)

    def wide(value):
        return jnp.concatenate([value] * (lanes // LANES), axis=1)

    def store(index, value):
        at = slice(index * SUB, (index + 1) * SUB)
        for half in range(lanes // LANES):
            rows_ref[half, at, :] = value[:, half * LANES : (half + 1) * LANES]

    for start in range(0, PANEL, PART):
        rows = [load(start + i) for i in range(PART)]
        base = first - tile * LANES + start
        entry = [
            [spread(rows[i][:, mine], base + j + zero) if j >= i else None for j in range(PART)]
            for i in range(PART)
        ]
        later = []
        for step in range(PART):
            k = first + start + step
            inverted = refined_reciprocal(entry[step][step])
            unit = jnp.where(lane == k, 1.0, rows[step])
            for other in range(step + 1, PART):
                ratio = entry[step][other] * inverted
                for column in range(other, PART):
                    entry[other][column] = entry[other][column] - ratio * entry[step][column]
                rows[other] = jnp.where(lane == k, 0.0, rows[other]) - wide(ratio) * unit
            done = jnp.where((lane > k) & (lane < stop), 0.0, unit)
            store(start + step, done * wide(lax.rsqrt(entry[step][step])))
            hidden = jnp.where((lane > k) & (lane < first + start + PART), 0.0, unit)
            later.append(hidden * wide(inverted))
        for i in range(start + PART, PANEL):
            hide = (lane >= first + start) & (lane < first + start + PART)
            row = jnp.where(hide, 0.0, load(i))
            for step in range(PART):
                row = row - wide(spread(rows[step][:, mine], first - tile * LANES + i + zero)) * later[step]
            store(i, row)


def in_parts(value):
    high = value.astype(jnp.bfloat16)
    rest = value - high.astype(jnp.float32)
    middle = rest.astype(jnp.bfloat16)
    return high, middle, (rest - middle.astype(jnp.float32)).astype(jnp.bfloat16)


def run_copies(plan, semaphores):
    copies = [
        pltpu.make_async_copy(source, place, semaphores.at[index])
        for index, (source, place) in enumerate(plan)
    ]
    for copy in copies:
        copy.start()
    for copy in copies:
        copy.wait()


def run_by_parity(even_plan, odd_plan, semaphores):
    is_even = lax.rem(lax.axis_index("chain"), 2) == 0

    @pl.when(is_even)
    def _():
        run_copies(even_plan, semaphores)

    @pl.when(jnp.logical_not(is_even))
    def _():
        run_copies(odd_plan, semaphores)


def chunk_sizes(half):
    early = max(half // 2, 1)
    return early, early - 1


def cut(line, first, count, place):
    plan = []
    for source, start, size in line:
        low, high = max(first, start), min(first + count, start + size)
        if low < high:
            plan.append((source(low - start, high - low), place(low - first, high - low)))
    return plan


def whole(ref):
    return lambda start, size: ref.at[pl.ds(start, size)]


def plane(ref, s):
    return lambda start, size: ref.at[pl.ds(start, size), s]


def first_plans(first_of, count, half, early, operands, left, right):
    own, got_early, got_late, edge, corner = operands
    own = own.at[0]
    late, sectors = half - early, 2 * half

    def plans(first, left_line, right_line, extra):
        zero_line = [(plane(ref, 0), start, size) for ref, start, size in right_line]
        one_line = [(plane(ref, 1), start, size) for ref, start, size in right_line]
        return [
            *cut([(whole(ref), start, size) for ref, start, size in left_line], first - 1, count + 1, whole(left)),
            *cut(zero_line, first, count + 1, plane(right, 0)),
            *cut(one_line + extra, first - 1, count + 1, plane(right, 1)),
        ]

    even = plans(
        first_of[0],
        [(edge, -1, 1), (own, 0, sectors)],
        [(got_early, 0, early + 1), (got_late, early + 1, late)],
        [(whole(corner), -1, 1)],
    )
    odd = plans(
        first_of[1],
        [(got_late, half - 1, late), (got_early, sectors - early - 1, early + 1)],
        [(own, 0, sectors), (edge, sectors, 1)],
        [],
    )
    return even, odd


def second_plans(first_of, count, half, early, operands, left, right):
    keep_early, keep_late, carried_early, carried_late, far, near = operands
    late, sectors = half - early, 2 * half

    def plans(first, left_line, right_line):
        return [
            *cut([(whole(ref), start, size) for ref, start, size in left_line], first - 1, count + 1, whole(left)),
            *cut([(whole(ref), start, size) for ref, start, size in right_line], first, count + 1, whole(right)),
        ]

    even = plans(
        first_of[0],
        [(far, -1, 1), (carried_early, 0, early), (carried_late, early, late)],
        [(keep_early, 0, early), (keep_late, early, late), (near, half, 1)],
    )
    odd = plans(
        first_of[1],
        [(near, half - 1, 1), (keep_late, half, late), (keep_early, sectors - early, early)],
        [(carried_late, half, late), (carried_early, sectors - early, early), (far, sectors, 1)],
    )
    return even, odd


def pair_kernel(second, late, sectors, refs):
    half = sectors // 2
    early, next_early = chunk_sizes(half)
    part = next_early if second else early
    first_of = (part, half) if late else (0, sectors - part)
    table, partner_sizes = refs[:2]
    operand_count = 6 if second else 5
    operands = refs[2 : 2 + operand_count]
    sketch_ref = refs[2 + operand_count]
    outputs = refs[3 + operand_count : -9]
    (
        left_ref,
        right_ref,
        two_ref,
        sample_ref,
        gram_ref,
        inverse_ref,
        rows_ref,
        square_ref,
        in_semaphores,
    ) = refs[-9:]
    send, keep, norm_ref, *extras = outputs
    count, kept, double = sample_ref.shape
    width = double // 2
    plans = second_plans if second else first_plans
    run_by_parity(*plans(first_of, count, half, early, operands, left_ref, right_ref), in_semaphores)

    parity = lax.rem(lax.axis_index("chain"), 2)
    is_even = parity == 0
    first = lax.axis_index("block") * sectors + jnp.where(is_even, *first_of)
    bond = parity if second else 1 - parity
    total = table.shape[1]

    def size_of(row, sector):
        return table[row, sector].astype(jnp.int32)


    def left_size(sector):
        at = jnp.clip(sector, 0, total - 1)
        return jnp.where(is_even, size_of(0, at), partner_sizes[0, 0, at])

    def middle_size(sector):
        at = jnp.clip(sector, 0, total - 1)
        size = size_of(jnp.where(is_even, 1, 0), at)
        return jnp.where(sector < total, size, 0)

    def right_size(sector):
        at = jnp.clip(sector, 0, total - 1)
        size = jnp.where(is_even, partner_sizes[0, 1, at], size_of(1, at))
        return jnp.where(sector < total, size, 0)

    row_index = lax.broadcasted_iota(jnp.int32, (kept, 1), 0)
    eye = (
        lax.broadcasted_iota(jnp.int32, (kept, kept), 0)
        == lax.broadcasted_iota(jnp.int32, (kept, kept), 1)
    )
    block_row = lax.broadcasted_iota(jnp.int32, (width, width), 0)
    block_column = lax.broadcasted_iota(jnp.int32, (width, width), 1)
    column = lax.broadcasted_iota(jnp.int32, (1, width), 1)

    def left(m, s, sector):
        if second:
            return left_ref[m, :, s * width : (s + 1) * width]
        inside = (column < middle_size(sector + s)).astype(jnp.float32).astype(jnp.bfloat16)
        return left_ref[m, s] * inside

    def right(m, s):
        if second:
            return right_ref[m, :, s * width : (s + 1) * width]
        return right_ref[m, s]

    def product(a, b):
        rounded = dot(a, b, LAST if second else PLAIN).astype(jnp.bfloat16)
        return rounded.astype(jnp.float32)

    def put(m, rows, columns, value, row_limit, column_limit):
        if not second:
            value = jnp.where(
                (block_row < row_limit) & (block_column < column_limit), value, 0.0
            )
        two_ref[m, rows, columns] = value.astype(jnp.bfloat16)

    w_empty, w_stay, w_swap, w_full = gate_terms(
        *(jnp.full((1, width), table[4 + bond, term], jnp.float32) for term in range(3))
    )

    @pl.loop(0, count, unroll=min(UNROLL, count))
    def _(m):
        sector = first + m
        below_zero, below_one = left(m, 0, sector - 1), left(m, 1, sector - 1)
        here_zero, here_one = left(m + 1, 0, sector), left(m + 1, 1, sector)
        same_zero, same_one = right(m, 0), right(m, 1)
        next_zero, next_one = right(m + 1, 0), right(m + 1, 1)
        low, high = slice(0, width), slice(width, double)
        rows_low, rows_high = left_size(sector), left_size(sector - 1)
        columns_low, columns_high = right_size(sector), right_size(sector + 1)
        put(m, low, low, w_empty * product(here_zero, same_zero), rows_low, columns_low)
        put(
            m,
            low,
            high,
            w_stay * product(here_zero, next_one) + w_swap * product(here_one, next_zero),
            rows_low,
            columns_high,
        )
        put(
            m,
            high,
            low,
            w_swap * product(below_zero, same_one) + w_stay * product(below_one, same_zero),
            rows_high,
            columns_low,
        )
        put(m, high, high, w_full * product(below_one, next_one), rows_high, columns_high)
        sample = dot(sketch_ref[...], two_ref[m], LAST)
        keep_rows = row_index < size_of(2 + bond, sector)
        sample = jnp.where(keep_rows, sample, 0.0)
        sample_ref[m] = sample
        high_part, middle_part, low_part = in_parts(sample)
        cross = dot(high_part, middle_part, LAST) + dot(high_part, low_part, LAST)
        gram = dot(high_part, high_part, LAST) + (
            dot(middle_part, middle_part, LAST) + (cross + jnp.transpose(cross))
        )
        gram_ref[m] = gram + jnp.where(eye & jnp.logical_not(keep_rows), 1.0, 0.0)

    lane = lax.broadcasted_iota(jnp.int32, (1, kept), 1)
    for tile in range(kept // LANES):
        below = slice(tile * LANES, kept)

        @pl.loop(0, LANES // PANEL)
        def _(panel):
            first = pl.multiple_of(tile * LANES + panel * PANEL, PANEL)
            here = pl.ds(first, PANEL)
            stop = first + PANEL
            for m in range(count):
                for half in range(kept // LANES):
                    span = slice(half * LANES, (half + 1) * LANES)
                    rows_ref[half, pl.ds(m, PANEL, stride=SUB), :] = gram_ref[m, here, span]
            factor_panel(rows_ref, first, tile)
            for m in range(count):
                solved = jnp.concatenate(
                    [
                        rows_ref[half, pl.ds(m, PANEL, stride=SUB), :]
                        for half in range(kept // LANES)
                    ],
                    axis=1,
                )
                inverse_ref[m, here, :] = jnp.where(lane < stop, solved, 0.0)
                high, middle, low = in_parts(solved)
                one = jnp.concatenate([high, high, middle, middle, high, low], axis=0)[:, below]
                two = jnp.concatenate([high, middle, high, middle, low, high], axis=0)
                change = dot(one, two, FIRST)
                kept_part = jnp.where((lane >= first) & (lane < stop), 0.0, gram_ref[m, below, :])
                gram_ref[m, below, :] = kept_part - change

    square_ref[...] = jnp.zeros_like(square_ref)

    @pl.loop(0, count, unroll=min(UNROLL, count))
    def _(m):
        inverse_high, inverse_middle, _ = in_parts(inverse_ref[m])
        sample_high, sample_middle, _ = in_parts(sample_ref[m])
        solved = dot(inverse_high, sample_high, PLAIN) + (
            dot(inverse_high, sample_middle, PLAIN) + dot(inverse_middle, sample_high, PLAIN)
        )
        solved = solved * math.sqrt(width)
        basis = solved.astype(jnp.bfloat16)
        coef = dot(basis, two_ref[m], PLAIN)
        square_ref[...] += jnp.sum(coef * coef, axis=0, keepdims=True)
        if second:
            for s in range(2):
                span = slice(s * width, (s + 1) * width)
                turned = jnp.transpose(solved[:, span])
                send[m, s] = jnp.where(is_even, turned, coef[:, span]).astype(jnp.bfloat16)
                keep[m, s] = jnp.where(is_even, coef[:, span], turned).astype(jnp.bfloat16)
        else:
            send[m] = jnp.where(is_even, coef, solved).astype(jnp.bfloat16)
            keep[m] = jnp.where(is_even, solved, coef).astype(jnp.bfloat16)

    norm_ref[0] = jnp.sum(square_ref[...])
    if second:
        if extras:
            extras[0][0] = send[0, 1]
    else:
        at = jnp.where(is_even, count - 1, 0) if late else jnp.where(is_even, 0, count - 1)
        extras[0][0] = send[at] if late else keep[at]


def pair_update(second, late, table, partner_sizes, operands, sketch_turned):
    kept, double = sketch_turned.shape
    width = double // 2
    sectors = table.shape[1] // lax.axis_size("block")
    half = sectors // 2
    early, next_early = chunk_sizes(half)
    part = next_early if second else early
    count = half - part if late else part
    block = (2, width, kept) if second else (kept, double)
    extra = [(1, kept, double)]
    if second:
        extra = [(1, width, kept)] if not late or next_early == 0 else []
    left_shape = (count + 1, kept, double) if second else (count + 1, 2, width, width)
    vmem = pl.BlockSpec(memory_space=pltpu.VMEM)
    smem = pl.BlockSpec(memory_space=pltpu.SMEM)
    anywhere = pl.BlockSpec(memory_space=pl.ANY)

    def kernel(*refs):
        pair_kernel(second, late, sectors, refs)

    return pl.pallas_call(
        kernel,
        out_shape=[
            jax.ShapeDtypeStruct((count, *block), jnp.bfloat16),
            jax.ShapeDtypeStruct((count, *block), jnp.bfloat16),
            jax.ShapeDtypeStruct((1,), jnp.float32),
            *(jax.ShapeDtypeStruct(shape, jnp.bfloat16) for shape in extra),
        ],
        in_specs=[smem] * 2 + [anywhere] * len(operands) + [vmem],
        out_specs=[vmem, vmem, smem] + [vmem] * len(extra),
        scratch_shapes=[
            pltpu.VMEM(left_shape, jnp.bfloat16),
            pltpu.VMEM(left_shape, jnp.bfloat16),
            pltpu.VMEM((count, double, double), jnp.bfloat16),
            pltpu.VMEM((count, kept, double), jnp.float32),
            pltpu.VMEM((count, kept, kept), jnp.float32),
            pltpu.VMEM((count, kept, kept), jnp.float32),
            pltpu.VMEM((kept // LANES, PANEL * SUB, LANES), jnp.float32),
            pltpu.VMEM((1, double), jnp.float32),
            pltpu.SemaphoreType.DMA((8,)),
        ],
        compiler_params=pltpu.CompilerParams(vmem_limit_bytes=32 * 2**20),
        cost_estimate=pl.CostEstimate(
            flops=(count + 12) * 50 * kept * double * double,
            bytes_accessed=8 * count * kept * double * 2,
            transcendentals=0,
        ),
    )(table, partner_sizes, *operands, sketch_turned)


def place_kernel(last, half, target, norm_refs, refs):
    _, early = chunk_sizes(half)
    late, sectors = half - early, 2 * half
    if last:
        returned_late, _, out, buffer, in_semaphores, out_semaphores = refs
        even_line = [(returned_late, half, late)]
        odd_line = [(returned_late, early, late)]
        lower_line = []
    else:
        if early:
            keep_late, lower, keep_early, returned_early = refs[:4]
            even_line = [(keep_early, 0, early), (keep_late, early, late), (returned_early, sectors - early, early)]
            odd_line = [(returned_early, 0, early), (keep_late, half, late), (keep_early, sectors - early, early)]
        else:
            keep_late, lower = refs[:2]
            even_line, odd_line = [(keep_late, 0, late)], [(keep_late, half, late)]
        lower_line = [(whole(lower), sectors, 1)]
        out, buffer, in_semaphores, out_semaphores = refs[-4:]
    site = out.at[0]
    zero_line = [(plane(ref, 0), start, size) for ref, start, size in odd_line]
    one_line = [(plane(ref, 1), start, size) for ref, start, size in odd_line]
    odd = cut(zero_line, 0, sectors, plane(site, 0))
    odd += cut(one_line + lower_line, 1, sectors, plane(site, 1))
    parts = even_line
    is_even = lax.rem(lax.axis_index("chain"), 2) == 0

    @pl.when(jnp.logical_not(is_even))
    def _():
        run_copies(odd, out_semaphores)

    @pl.when(is_even)
    def _():
        norms, from_second = norm_refs
        rows = (1, buffer.shape[-1])
        norm_even = jnp.full(rows, from_second[0], jnp.float32)
        norm_odd = jnp.full(rows, norms[1] + from_second[1], jnp.float32)
        scale_even = jnp.sqrt(target / norm_even)
        scale = scale_even * jnp.sqrt(target / (scale_even * scale_even * norm_odd))
        coming, going, filled = [], [], 0
        for index, (source, start, size) in enumerate(parts):
            room = buffer.at[pl.ds(filled, size)]
            coming.append(pltpu.make_async_copy(source, room, in_semaphores.at[index]))
            going.append(
                pltpu.make_async_copy(room, out.at[0, pl.ds(start, size)], out_semaphores.at[index])
            )
            filled += size
        for copy in coming:
            copy.start()
        filled = 0
        for index, (source, start, size) in enumerate(parts):
            coming[index].wait()

            @pl.loop(filled, filled + size)
            def _(sector):
                for s in range(2):
                    scaled = buffer[sector, s].astype(jnp.float32) * scale
                    buffer[sector, s] = scaled.astype(jnp.bfloat16)

            going[index].start()
            filled += size
        for copy in going:
            copy.wait()


def place(last, half, target, norms, operands, site):
    anywhere = pl.BlockSpec(memory_space=pl.ANY)
    _, early = chunk_sizes(half)
    rows = half - early if last else half + early

    def kernel(*refs):
        place_kernel(last, half, target, refs[:2], refs[2:])

    return pl.pallas_call(
        kernel,
        out_shape=jax.ShapeDtypeStruct(site.shape, site.dtype),
        in_specs=[pl.BlockSpec(memory_space=pltpu.SMEM)] * 2 + [anywhere] * len(operands),
        out_specs=anywhere,
        scratch_shapes=[
            pltpu.VMEM((rows, *site.shape[2:]), site.dtype),
            pltpu.SemaphoreType.DMA((3,)),
            pltpu.SemaphoreType.DMA((7,)),
        ],
        input_output_aliases={3: 0} if last else {},
        compiler_params=pltpu.CompilerParams(vmem_limit_bytes=16 * 2**20),
        cost_estimate=pl.CostEstimate(
            flops=0, bytes_accessed=2 * rows * site.size // site.shape[1] * 2, transcendentals=0
        ),
    )(*norms, *operands)


def move(value, target_of):
    sites, parts = lax.axis_size("chain"), lax.axis_size("block")
    pairs = []
    for site in range(sites):
        for part in range(parts):
            target = target_of(site, part)
            if target is not None and 0 <= target[1] < parts:
                pairs.append((site * parts + part, (target[0] % sites) * parts + target[1]))
    return lax.ppermute(value, ("chain", "block"), pairs)


def by_parity(even_target, odd_target):
    return lambda c, b: even_target(c, b) if c % 2 == 0 else odd_target(c, b)


def nowhere(c, b):
    return None


def joined(*parts):
    return jnp.concatenate(parts, axis=0)


def body(site_tensors, sketch, bond_sizes, kept_ranks, couplings):
    sectors = site_tensors.shape[1]
    half = sectors // 2
    early, next_early = chunk_sizes(half)
    width = site_tensors.shape[-1]
    kept = sketch.shape[1]
    parts = lax.axis_size("block")
    is_even = lax.axis_index("chain") % 2 == 0
    own = site_tensors[0]
    sketch_turned = jnp.transpose(sketch)

    terms = jnp.pad(couplings[0], ((0, 0), (0, bond_sizes.shape[2] - couplings.shape[2])))
    table = joined(
        bond_sizes[0].astype(jnp.float32), kept_ranks[0].astype(jnp.float32), terms
    )

    def pick(even_value, odd_value):
        return jnp.where(is_even, even_value, odd_value)

    def update(second, late, *operands):
        return pair_update(
            second, late, table, partner_sizes, operands, sketch_turned
        )

    across = by_parity(lambda c, b: (c + 1, b), lambda c, b: (c - 1, b))
    got_early = move(pick(own[sectors - early - 1 :], own[: early + 1]), across)
    partner_sizes = move(bond_sizes, across)
    edge = move(
        pick(own[-1:], own[:1]), by_parity(lambda c, b: (c, b + 1), lambda c, b: (c, b - 1))
    )
    corner = move(own[-1:, 1], by_parity(nowhere, lambda c, b: (c - 1, b + 1)))
    sent = pick(own[half - 1 : sectors - early - 1], own[early + 1 : half + 1])
    sent, got_early = lax.optimization_barrier((sent, got_early))
    got_late = move(sent, across)
    send_early, keep_early, norm_early, halo_early = update(
        False, False, site_tensors, got_early, got_early, edge, corner
    )

    along = by_parity(lambda c, b: (c + 2, b), lambda c, b: (c - 2, b))
    far = move(
        halo_early, by_parity(lambda c, b: (c - 1, b - 1), lambda c, b: (c + 1, b + 1))
    )
    carried_early = move(send_early, along)
    send_late, keep_late, norm_late, halo_late = update(
        False, True, site_tensors, got_early, got_late, edge, corner
    )
    norm_even = norm_early + norm_late
    carried_late = move(send_late, along)
    near = move(halo_late, across)

    back = by_parity(lambda c, b: (c - 1, b), lambda c, b: (c + 1, b))
    norm_odd = 0.0
    first_parts = ()
    if next_early:
        send_early, kept_early, norm_early, lower_first = update(
            True, False, keep_early, keep_early, carried_early, carried_early, far, far
        )
        norm_odd = norm_early
        send_early, carried_late = lax.optimization_barrier((send_early, carried_late))
        returned_early = move(send_early, back)
        first_parts = (kept_early, returned_early)
    send_late, kept_late, norm_late, *lower = update(
        True, True, keep_early, keep_late, carried_early, carried_late, far, near
    )
    if next_early == 0:
        lower_first = lower[0]
    lower_above = move(lower_first, by_parity(lambda c, b: (c - 1, b - 1), nowhere))
    if next_early:
        send_late, returned_early, lower_above = lax.optimization_barrier(
            (send_late, returned_early, lower_above)
        )
        first_parts = (kept_early, returned_early)
    returned_late = move(send_late, back)

    norms = lax.psum(joined(norm_even, norm_odd + norm_late), "block")
    from_right = move(norms, by_parity(nowhere, lambda c, b: (c - 1, b)))
    from_second = move(
        from_right + jnp.where(jnp.arange(2) == 0, norms, 0.0),
        by_parity(lambda c, b: (c + 2, b), nowhere),
    )
    target = float(sectors * parts * kept * width)
    norms = (norms, from_second)

    site = place(False, half, target, norms, (kept_late, lower_above, *first_parts), site_tensors)
    return place(True, half, target, norms, (returned_late, site), site_tensors)


def solution(mesh):
    placed = (
        P("chain", "block", None, None, None),
        P(),
        P("chain", None, None),
        P("chain", None, None),
        P("chain", None, None),
    )
    return jax.shard_map(
        body,
        mesh=mesh,
        in_specs=placed,
        out_specs=P("chain", "block", None, None, None),
        check_vma=False,
    )
```

```python
import math

import jax
import jax.numpy as jnp
from jax import lax
from jax.experimental import pallas as pl
from jax.experimental.pallas import tpu as pltpu
from jax.sharding import PartitionSpec as P

tau_step = 0.5
SUB = 8
LANES = 128
PANEL = 32
PART = 8
UNROLL = 2
FIRST = (((0,), (0,)), ((), ()))
LAST = (((1,), (1,)), ((), ()))
PLAIN = (((1,), (0,)), ((), ()))


def gate_terms(hopping, ising_term, field_term):
    rotation = 0.5 * tau_step * hopping
    middle_scale = jnp.exp(0.25 * tau_step * ising_term)
    weight_empty = jnp.exp(-tau_step * (0.25 * ising_term - 0.5 * field_term))
    weight_full = jnp.exp(-tau_step * (0.25 * ising_term + 0.5 * field_term))
    grown, shrunk = jnp.exp(rotation), jnp.exp(-rotation)
    weight_stay = middle_scale * (0.5 * (grown + shrunk))
    weight_swap = -middle_scale * (0.5 * (grown - shrunk))
    return weight_empty, weight_stay, weight_swap, weight_full


def dot(left, right, dims):
    return lax.dot_general(left, right, dims, preferred_element_type=jnp.float32)


def spread(row, lane_index):
    return jnp.take_along_axis(row, lane_index, axis=1)


def refined_reciprocal(value):
    guess = pltpu.reciprocal(value, approx=True)
    return guess * (2.0 - value * guess)


def factor_panel(rows_ref, first, tile):
    lanes = rows_ref.shape[0] * LANES
    lane = lax.broadcasted_iota(jnp.int32, (SUB, lanes), 1)
    zero = jnp.zeros((SUB, LANES), jnp.int32)
    mine = slice(tile * LANES, (tile + 1) * LANES)
    stop = first + PANEL

    def load(index):
        at = slice(index * SUB, (index + 1) * SUB)
        return jnp.concatenate([rows_ref[half, at, :] for half in range(lanes // LANES)], axis=1)

    def wide(value):
        return jnp.concatenate([value] * (lanes // LANES), axis=1)

    def store(index, value):
        at = slice(index * SUB, (index + 1) * SUB)
        for half in range(lanes // LANES):
            rows_ref[half, at, :] = value[:, half * LANES : (half + 1) * LANES]

    for start in range(0, PANEL, PART):
        rows = [load(start + i) for i in range(PART)]
        base = first - tile * LANES + start
        entry = [
            [spread(rows[i][:, mine], base + j + zero) if j >= i else None for j in range(PART)]
            for i in range(PART)
        ]
        later = []
        for step in range(PART):
            k = first + start + step
            inverted = refined_reciprocal(entry[step][step])
            unit = jnp.where(lane == k, 1.0, rows[step])
            for other in range(step + 1, PART):
                ratio = entry[step][other] * inverted
                for column in range(other, PART):
                    entry[other][column] = entry[other][column] - ratio * entry[step][column]
                rows[other] = jnp.where(lane == k, 0.0, rows[other]) - wide(ratio) * unit
            done = jnp.where((lane > k) & (lane < stop), 0.0, unit)
            store(start + step, done * wide(lax.rsqrt(entry[step][step])))
            hidden = jnp.where((lane > k) & (lane < first + start + PART), 0.0, unit)
            later.append(hidden * wide(inverted))
        for i in range(start + PART, PANEL):
            hide = (lane >= first + start) & (lane < first + start + PART)
            row = jnp.where(hide, 0.0, load(i))
            for step in range(PART):
                row = row - wide(spread(rows[step][:, mine], first - tile * LANES + i + zero)) * later[step]
            store(i, row)


def in_parts(value):
    high = value.astype(jnp.bfloat16)
    rest = value - high.astype(jnp.float32)
    middle = rest.astype(jnp.bfloat16)
    return high, middle, (rest - middle.astype(jnp.float32)).astype(jnp.bfloat16)


def run_copies(plan, semaphores):
    copies = [
        pltpu.make_async_copy(source, place, semaphores.at[index])
        for index, (source, place) in enumerate(plan)
    ]
    for copy in copies:
        copy.start()
    for copy in copies:
        copy.wait()


def run_by_parity(even_plan, odd_plan, semaphores):
    is_even = lax.rem(lax.axis_index("chain"), 2) == 0

    @pl.when(is_even)
    def _():
        run_copies(even_plan, semaphores)

    @pl.when(jnp.logical_not(is_even))
    def _():
        run_copies(odd_plan, semaphores)


def chunk_sizes(half):
    early = max(half // 2, 1)
    return early, early - 1


def cut(line, first, count, place):
    plan = []
    for source, start, size in line:
        low, high = max(first, start), min(first + count, start + size)
        if low < high:
            plan.append((source(low - start, high - low), place(low - first, high - low)))
    return plan


def whole(ref):
    return lambda start, size: ref.at[pl.ds(start, size)]


def plane(ref, s):
    return lambda start, size: ref.at[pl.ds(start, size), s]


def first_plans(first_of, count, half, early, operands, left, right):
    own, got_early, got_late, edge, corner = operands
    own = own.at[0]
    late, sectors = half - early, 2 * half

    def plans(first, left_line, right_line, extra):
        zero_line = [(plane(ref, 0), start, size) for ref, start, size in right_line]
        one_line = [(plane(ref, 1), start, size) for ref, start, size in right_line]
        return [
            *cut([(whole(ref), start, size) for ref, start, size in left_line], first - 1, count + 1, whole(left)),
            *cut(zero_line, first, count + 1, plane(right, 0)),
            *cut(one_line + extra, first - 1, count + 1, plane(right, 1)),
        ]

    even = plans(
        first_of[0],
        [(edge, -1, 1), (own, 0, sectors)],
        [(got_early, 0, early + 1), (got_late, early + 1, late)],
        [(whole(corner), -1, 1)],
    )
    odd = plans(
        first_of[1],
        [(got_late, half - 1, late), (got_early, sectors - early - 1, early + 1)],
        [(own, 0, sectors), (edge, sectors, 1)],
        [],
    )
    return even, odd


def second_plans(first_of, count, half, early, operands, left, right):
    keep_early, keep_late, carried_early, carried_late, far, near = operands
    late, sectors = half - early, 2 * half

    def plans(first, left_line, right_line):
        return [
            *cut([(whole(ref), start, size) for ref, start, size in left_line], first - 1, count + 1, whole(left)),
            *cut([(whole(ref), start, size) for ref, start, size in right_line], first, count + 1, whole(right)),
        ]

    even = plans(
        first_of[0],
        [(far, -1, 1), (carried_early, 0, early), (carried_late, early, late)],
        [(keep_early, 0, early), (keep_late, early, late), (near, half, 1)],
    )
    odd = plans(
        first_of[1],
        [(near, half - 1, 1), (keep_late, half, late), (keep_early, sectors - early, early)],
        [(carried_late, half, late), (carried_early, sectors - early, early), (far, sectors, 1)],
    )
    return even, odd


def pair_kernel(second, late, sectors, refs):
    half = sectors // 2
    early, next_early = chunk_sizes(half)
    part = next_early if second else early
    first_of = (part, half) if late else (0, sectors - part)
    table, partner_sizes = refs[:2]
    operand_count = 6 if second else 5
    operands = refs[2 : 2 + operand_count]
    sketch_ref = refs[2 + operand_count]
    outputs = refs[3 + operand_count : -9]
    (
        left_ref,
        right_ref,
        two_ref,
        sample_ref,
        gram_ref,
        inverse_ref,
        rows_ref,
        square_ref,
        in_semaphores,
    ) = refs[-9:]
    send, keep, norm_ref, *extras = outputs
    count, kept, double = sample_ref.shape
    width = double // 2
    plans = second_plans if second else first_plans
    run_by_parity(*plans(first_of, count, half, early, operands, left_ref, right_ref), in_semaphores)

    parity = lax.rem(lax.axis_index("chain"), 2)
    is_even = parity == 0
    first = lax.axis_index("block") * sectors + jnp.where(is_even, *first_of)
    bond = parity if second else 1 - parity
    total = table.shape[1]

    def size_of(row, sector):
        return table[row, sector].astype(jnp.int32)


    def left_size(sector):
        at = jnp.clip(sector, 0, total - 1)
        return jnp.where(is_even, size_of(0, at), partner_sizes[0, 0, at])

    def middle_size(sector):
        at = jnp.clip(sector, 0, total - 1)
        size = size_of(jnp.where(is_even, 1, 0), at)
        return jnp.where(sector < total, size, 0)

    def right_size(sector):
        at = jnp.clip(sector, 0, total - 1)
        size = jnp.where(is_even, partner_sizes[0, 1, at], size_of(1, at))
        return jnp.where(sector < total, size, 0)

    row_index = lax.broadcasted_iota(jnp.int32, (kept, 1), 0)
    eye = (
        lax.broadcasted_iota(jnp.int32, (kept, kept), 0)
        == lax.broadcasted_iota(jnp.int32, (kept, kept), 1)
    )
    block_row = lax.broadcasted_iota(jnp.int32, (width, width), 0)
    block_column = lax.broadcasted_iota(jnp.int32, (width, width), 1)
    column = lax.broadcasted_iota(jnp.int32, (1, width), 1)

    def left(m, s, sector):
        if second:
            return left_ref[m, :, s * width : (s + 1) * width]
        inside = (column < middle_size(sector + s)).astype(jnp.float32).astype(jnp.bfloat16)
        return left_ref[m, s] * inside

    def right(m, s):
        if second:
            return right_ref[m, :, s * width : (s + 1) * width]
        return right_ref[m, s]

    def product(a, b):
        rounded = dot(a, b, LAST if second else PLAIN).astype(jnp.bfloat16)
        return rounded.astype(jnp.float32)

    def put(m, rows, columns, value, row_limit, column_limit):
        if not second:
            value = jnp.where(
                (block_row < row_limit) & (block_column < column_limit), value, 0.0
            )
        two_ref[m, rows, columns] = value.astype(jnp.bfloat16)

    w_empty, w_stay, w_swap, w_full = gate_terms(
        *(jnp.full((1, width), table[4 + bond, term], jnp.float32) for term in range(3))
    )

    @pl.loop(0, count, unroll=min(UNROLL, count))
    def _(m):
        sector = first + m
        below_zero, below_one = left(m, 0, sector - 1), left(m, 1, sector - 1)
        here_zero, here_one = left(m + 1, 0, sector), left(m + 1, 1, sector)
        same_zero, same_one = right(m, 0), right(m, 1)
        next_zero, next_one = right(m + 1, 0), right(m + 1, 1)
        low, high = slice(0, width), slice(width, double)
        rows_low, rows_high = left_size(sector), left_size(sector - 1)
        columns_low, columns_high = right_size(sector), right_size(sector + 1)
        put(m, low, low, w_empty * product(here_zero, same_zero), rows_low, columns_low)
        put(
            m,
            low,
            high,
            w_stay * product(here_zero, next_one) + w_swap * product(here_one, next_zero),
            rows_low,
            columns_high,
        )
        put(
            m,
            high,
            low,
            w_swap * product(below_zero, same_one) + w_stay * product(below_one, same_zero),
            rows_high,
            columns_low,
        )
        put(m, high, high, w_full * product(below_one, next_one), rows_high, columns_high)
        sample = dot(sketch_ref[...], two_ref[m], LAST)
        keep_rows = row_index < size_of(2 + bond, sector)
        sample = jnp.where(keep_rows, sample, 0.0)
        sample_ref[m] = sample
        high_part, middle_part, low_part = in_parts(sample)
        cross = dot(high_part, middle_part, LAST) + dot(high_part, low_part, LAST)
        gram = dot(high_part, high_part, LAST) + (
            dot(middle_part, middle_part, LAST) + (cross + jnp.transpose(cross))
        )
        gram_ref[m] = gram + jnp.where(eye & jnp.logical_not(keep_rows), 1.0, 0.0)

    lane = lax.broadcasted_iota(jnp.int32, (1, kept), 1)
    for tile in range(kept // LANES):
        below = slice(tile * LANES, kept)

        @pl.loop(0, LANES // PANEL)
        def _(panel):
            first = pl.multiple_of(tile * LANES + panel * PANEL, PANEL)
            here = pl.ds(first, PANEL)
            stop = first + PANEL
            for m in range(count):
                for half in range(kept // LANES):
                    span = slice(half * LANES, (half + 1) * LANES)
                    rows_ref[half, pl.ds(m, PANEL, stride=SUB), :] = gram_ref[m, here, span]
            factor_panel(rows_ref, first, tile)
            for m in range(count):
                solved = jnp.concatenate(
                    [
                        rows_ref[half, pl.ds(m, PANEL, stride=SUB), :]
                        for half in range(kept // LANES)
                    ],
                    axis=1,
                )
                inverse_ref[m, here, :] = jnp.where(lane < stop, solved, 0.0)
                high, middle, low = in_parts(solved)
                one = jnp.concatenate([high, high, middle, middle, high, low], axis=0)[:, below]
                two = jnp.concatenate([high, middle, high, middle, low, high], axis=0)
                change = dot(one, two, FIRST)
                kept_part = jnp.where((lane >= first) & (lane < stop), 0.0, gram_ref[m, below, :])
                gram_ref[m, below, :] = kept_part - change

    square_ref[...] = jnp.zeros_like(square_ref)

    @pl.loop(0, count, unroll=min(UNROLL, count))
    def _(m):
        inverse_high, inverse_middle, _ = in_parts(inverse_ref[m])
        sample_high, sample_middle, _ = in_parts(sample_ref[m])
        solved = dot(inverse_high, sample_high, PLAIN) + (
            dot(inverse_high, sample_middle, PLAIN) + dot(inverse_middle, sample_high, PLAIN)
        )
        solved = solved * math.sqrt(width)
        basis = solved.astype(jnp.bfloat16)
        coef = dot(basis, two_ref[m], PLAIN)
        square_ref[...] += jnp.sum(coef * coef, axis=0, keepdims=True)
        if second:
            for s in range(2):
                span = slice(s * width, (s + 1) * width)
                turned = jnp.transpose(solved[:, span])
                send[m, s] = jnp.where(is_even, turned, coef[:, span]).astype(jnp.bfloat16)
                keep[m, s] = jnp.where(is_even, coef[:, span], turned).astype(jnp.bfloat16)
        else:
            send[m] = jnp.where(is_even, coef, solved).astype(jnp.bfloat16)
            keep[m] = jnp.where(is_even, solved, coef).astype(jnp.bfloat16)

    norm_ref[0] = jnp.sum(square_ref[...])
    if second:
        if extras:
            extras[0][0] = send[0, 1]
    else:
        at = jnp.where(is_even, count - 1, 0) if late else jnp.where(is_even, 0, count - 1)
        extras[0][0] = send[at] if late else keep[at]


def pair_update(second, late, table, partner_sizes, operands, sketch_turned):
    kept, double = sketch_turned.shape
    width = double // 2
    sectors = table.shape[1] // lax.axis_size("block")
    half = sectors // 2
    early, next_early = chunk_sizes(half)
    part = next_early if second else early
    count = half - part if late else part
    block = (2, width, kept) if second else (kept, double)
    extra = [(1, kept, double)]
    if second:
        extra = [(1, width, kept)] if not late or next_early == 0 else []
    left_shape = (count + 1, kept, double) if second else (count + 1, 2, width, width)
    vmem = pl.BlockSpec(memory_space=pltpu.VMEM)
    smem = pl.BlockSpec(memory_space=pltpu.SMEM)
    anywhere = pl.BlockSpec(memory_space=pl.ANY)
    places = [anywhere] * len(operands)
    if not second:
        places[0] = pl.BlockSpec(memory_space=pltpu.HBM)

    def kernel(*refs):
        pair_kernel(second, late, sectors, refs)

    return pl.pallas_call(
        kernel,
        out_shape=[
            jax.ShapeDtypeStruct((count, *block), jnp.bfloat16),
            jax.ShapeDtypeStruct((count, *block), jnp.bfloat16),
            jax.ShapeDtypeStruct((1,), jnp.float32),
            *(jax.ShapeDtypeStruct(shape, jnp.bfloat16) for shape in extra),
        ],
        in_specs=[smem] * 2 + places + [vmem],
        out_specs=[vmem, vmem, smem] + [vmem] * len(extra),
        scratch_shapes=[
            pltpu.VMEM(left_shape, jnp.bfloat16),
            pltpu.VMEM(left_shape, jnp.bfloat16),
            pltpu.VMEM((count, double, double), jnp.bfloat16),
            pltpu.VMEM((count, kept, double), jnp.float32),
            pltpu.VMEM((count, kept, kept), jnp.float32),
            pltpu.VMEM((count, kept, kept), jnp.float32),
            pltpu.VMEM((kept // LANES, PANEL * SUB, LANES), jnp.float32),
            pltpu.VMEM((1, double), jnp.float32),
            pltpu.SemaphoreType.DMA((8,)),
        ],
        compiler_params=pltpu.CompilerParams(vmem_limit_bytes=32 * 2**20),
        cost_estimate=pl.CostEstimate(
            flops=(count + 12) * 50 * kept * double * double,
            bytes_accessed=8 * count * kept * double * 2,
            transcendentals=0,
        ),
    )(table, partner_sizes, *operands, sketch_turned)


def place_kernel(last, half, target, norm_refs, refs):
    _, early = chunk_sizes(half)
    late, sectors = half - early, 2 * half
    if last:
        returned_late, _, out, buffer, in_semaphores, out_semaphores = refs
        even_line = [(returned_late, half, late)]
        odd_line = [(returned_late, early, late)]
        lower_line = []
    else:
        if early:
            keep_late, lower, keep_early, returned_early = refs[:4]
            even_line = [(keep_early, 0, early), (keep_late, early, late), (returned_early, sectors - early, early)]
            odd_line = [(returned_early, 0, early), (keep_late, half, late), (keep_early, sectors - early, early)]
        else:
            keep_late, lower = refs[:2]
            even_line, odd_line = [(keep_late, 0, late)], [(keep_late, half, late)]
        lower_line = [(whole(lower), sectors, 1)]
        out, buffer, in_semaphores, out_semaphores = refs[-4:]
    site = out.at[0]
    zero_line = [(plane(ref, 0), start, size) for ref, start, size in odd_line]
    one_line = [(plane(ref, 1), start, size) for ref, start, size in odd_line]
    odd = cut(zero_line, 0, sectors, plane(site, 0))
    odd += cut(one_line + lower_line, 1, sectors, plane(site, 1))
    parts = even_line
    is_even = lax.rem(lax.axis_index("chain"), 2) == 0

    @pl.when(jnp.logical_not(is_even))
    def _():
        run_copies(odd, out_semaphores)

    @pl.when(is_even)
    def _():
        norms, from_second = norm_refs
        rows = (1, buffer.shape[-1])
        norm_even = jnp.full(rows, from_second[0], jnp.float32)
        norm_odd = jnp.full(rows, norms[1] + from_second[1], jnp.float32)
        scale_even = jnp.sqrt(target / norm_even)
        scale = scale_even * jnp.sqrt(target / (scale_even * scale_even * norm_odd))
        coming, going, filled = [], [], 0
        for index, (source, start, size) in enumerate(parts):
            room = buffer.at[pl.ds(filled, size)]
            coming.append(pltpu.make_async_copy(source, room, in_semaphores.at[index]))
            going.append(
                pltpu.make_async_copy(room, out.at[0, pl.ds(start, size)], out_semaphores.at[index])
            )
            filled += size
        for copy in coming:
            copy.start()
        filled = 0
        for index, (source, start, size) in enumerate(parts):
            coming[index].wait()

            @pl.loop(filled, filled + size)
            def _(sector):
                for s in range(2):
                    scaled = buffer[sector, s].astype(jnp.float32) * scale
                    buffer[sector, s] = scaled.astype(jnp.bfloat16)

            going[index].start()
            filled += size
        for copy in going:
            copy.wait()


def place(last, half, target, norms, operands, site):
    anywhere = pl.BlockSpec(memory_space=pl.ANY)
    _, early = chunk_sizes(half)
    places = [anywhere] * len(operands)
    if not last and early:
        places[-1] = pl.BlockSpec(memory_space=pltpu.HBM)
    rows = half - early if last else half + early

    def kernel(*refs):
        place_kernel(last, half, target, refs[:2], refs[2:])

    return pl.pallas_call(
        kernel,
        out_shape=jax.ShapeDtypeStruct(site.shape, site.dtype),
        in_specs=[pl.BlockSpec(memory_space=pltpu.SMEM)] * 2 + places,
        out_specs=anywhere,
        scratch_shapes=[
            pltpu.VMEM((rows, *site.shape[2:]), site.dtype),
            pltpu.SemaphoreType.DMA((3,)),
            pltpu.SemaphoreType.DMA((7,)),
        ],
        input_output_aliases={3: 0} if last else {},
        compiler_params=pltpu.CompilerParams(vmem_limit_bytes=16 * 2**20),
        cost_estimate=pl.CostEstimate(
            flops=0, bytes_accessed=2 * rows * site.size // site.shape[1] * 2, transcendentals=0
        ),
    )(*norms, *operands)


def move(value, target_of):
    sites, parts = lax.axis_size("chain"), lax.axis_size("block")
    pairs = []
    for site in range(sites):
        for part in range(parts):
            target = target_of(site, part)
            if target is not None and 0 <= target[1] < parts:
                pairs.append((site * parts + part, (target[0] % sites) * parts + target[1]))
    return lax.ppermute(value, ("chain", "block"), pairs)


def by_parity(even_target, odd_target):
    return lambda c, b: even_target(c, b) if c % 2 == 0 else odd_target(c, b)


def nowhere(c, b):
    return None


def joined(*parts):
    return jnp.concatenate(parts, axis=0)


def body(site_tensors, sketch, bond_sizes, kept_ranks, couplings):
    sectors = site_tensors.shape[1]
    half = sectors // 2
    early, next_early = chunk_sizes(half)
    width = site_tensors.shape[-1]
    kept = sketch.shape[1]
    parts = lax.axis_size("block")
    is_even = lax.axis_index("chain") % 2 == 0
    own = site_tensors[0]
    sketch_turned = jnp.transpose(sketch)

    terms = jnp.pad(couplings[0], ((0, 0), (0, bond_sizes.shape[2] - couplings.shape[2])))
    table = joined(
        bond_sizes[0].astype(jnp.float32), kept_ranks[0].astype(jnp.float32), terms
    )

    def pick(even_value, odd_value):
        return jnp.where(is_even, even_value, odd_value)

    def update(second, late, *operands):
        return pair_update(
            second, late, table, partner_sizes, operands, sketch_turned
        )

    across = by_parity(lambda c, b: (c + 1, b), lambda c, b: (c - 1, b))
    got_early = move(pick(own[sectors - early - 1 :], own[: early + 1]), across)
    partner_sizes = move(bond_sizes, across)
    edge = move(
        pick(own[-1:], own[:1]), by_parity(lambda c, b: (c, b + 1), lambda c, b: (c, b - 1))
    )
    corner = move(own[-1:, 1], by_parity(nowhere, lambda c, b: (c - 1, b + 1)))
    sent = pick(own[half - 1 : sectors - early - 1], own[early + 1 : half + 1])
    sent, got_early = lax.optimization_barrier((sent, got_early))
    got_late = move(sent, across)
    send_early, keep_early, norm_early, halo_early = update(
        False, False, site_tensors, got_early, got_early, edge, corner
    )

    along = by_parity(lambda c, b: (c + 2, b), lambda c, b: (c - 2, b))
    far = move(
        halo_early, by_parity(lambda c, b: (c - 1, b - 1), lambda c, b: (c + 1, b + 1))
    )
    carried_early = move(send_early, along)
    send_late, keep_late, norm_late, halo_late = update(
        False, True, site_tensors, got_early, got_late, edge, corner
    )
    norm_even = norm_early + norm_late
    carried_late = move(send_late, along)
    near = move(halo_late, across)

    back = by_parity(lambda c, b: (c - 1, b), lambda c, b: (c + 1, b))
    norm_odd = 0.0
    first_parts = ()
    if next_early:
        send_early, kept_early, norm_early, lower_first = update(
            True, False, keep_early, keep_early, carried_early, carried_early, far, far
        )
        norm_odd = norm_early
        send_early, carried_late = lax.optimization_barrier((send_early, carried_late))
        returned_early = move(send_early, back)
        first_parts = (kept_early, returned_early)
    send_late, kept_late, norm_late, *lower = update(
        True, True, keep_early, keep_late, carried_early, carried_late, far, near
    )
    if next_early == 0:
        lower_first = lower[0]
    lower_above = move(lower_first, by_parity(lambda c, b: (c - 1, b - 1), nowhere))
    if next_early:
        send_late, returned_early, lower_above = lax.optimization_barrier(
            (send_late, returned_early, lower_above)
        )
        first_parts = (kept_early, returned_early)
    norms = lax.psum(joined(norm_even, norm_odd + norm_late), "block")
    from_right = move(norms, by_parity(nowhere, lambda c, b: (c - 1, b)))
    send_late, from_right = lax.optimization_barrier((send_late, from_right))
    returned_late = move(send_late, back)
    from_second = move(
        from_right + jnp.where(jnp.arange(2) == 0, norms, 0.0),
        by_parity(lambda c, b: (c + 2, b), nowhere),
    )
    target = float(sectors * parts * kept * width)
    norms = (norms, from_second)

    site = place(False, half, target, norms, (kept_late, lower_above, *first_parts), site_tensors)
    return place(True, half, target, norms, (returned_late, site), site_tensors)


def solution(mesh):
    placed = (
        P("chain", "block", None, None, None),
        P(),
        P("chain", None, None),
        P("chain", None, None),
        P("chain", None, None),
    )
    return jax.shard_map(
        body,
        mesh=mesh,
        in_specs=placed,
        out_specs=P("chain", "block", None, None, None),
        check_vma=False,
    )
```

```python
import math

import jax
import jax.numpy as jnp
from jax import lax
from jax.experimental import pallas as pl
from jax.experimental.pallas import tpu as pltpu
from jax.sharding import PartitionSpec as P

tau_step = 0.5
SUB = 8
LANES = 128
PANEL = 32
PART = 8
UNROLL = 2
FIRST = (((0,), (0,)), ((), ()))
LAST = (((1,), (1,)), ((), ()))
PLAIN = (((1,), (0,)), ((), ()))


def gate_terms(hopping, ising_term, field_term):
    rotation = 0.5 * tau_step * hopping
    middle_scale = jnp.exp(0.25 * tau_step * ising_term)
    weight_empty = jnp.exp(-tau_step * (0.25 * ising_term - 0.5 * field_term))
    weight_full = jnp.exp(-tau_step * (0.25 * ising_term + 0.5 * field_term))
    grown, shrunk = jnp.exp(rotation), jnp.exp(-rotation)
    weight_stay = middle_scale * (0.5 * (grown + shrunk))
    weight_swap = -middle_scale * (0.5 * (grown - shrunk))
    return weight_empty, weight_stay, weight_swap, weight_full


def dot(left, right, dims):
    return lax.dot_general(left, right, dims, preferred_element_type=jnp.float32)


def spread(row, lane_index):
    return jnp.take_along_axis(row, lane_index, axis=1)


def refined_reciprocal(value):
    guess = pltpu.reciprocal(value, approx=True)
    return guess * (2.0 - value * guess)


def factor_panel(rows_ref, first, tile):
    lanes = rows_ref.shape[0] * LANES
    lane = lax.broadcasted_iota(jnp.int32, (SUB, lanes), 1)
    zero = jnp.zeros((SUB, LANES), jnp.int32)
    mine = slice(tile * LANES, (tile + 1) * LANES)
    stop = first + PANEL

    def load(index):
        at = slice(index * SUB, (index + 1) * SUB)
        return jnp.concatenate([rows_ref[half, at, :] for half in range(lanes // LANES)], axis=1)

    def wide(value):
        return jnp.concatenate([value] * (lanes // LANES), axis=1)

    def store(index, value):
        at = slice(index * SUB, (index + 1) * SUB)
        for half in range(lanes // LANES):
            rows_ref[half, at, :] = value[:, half * LANES : (half + 1) * LANES]

    for start in range(0, PANEL, PART):
        rows = [load(start + i) for i in range(PART)]
        base = first - tile * LANES + start
        entry = [
            [spread(rows[i][:, mine], base + j + zero) if j >= i else None for j in range(PART)]
            for i in range(PART)
        ]
        later = []
        for step in range(PART):
            k = first + start + step
            inverted = refined_reciprocal(entry[step][step])
            unit = jnp.where(lane == k, 1.0, rows[step])
            for other in range(step + 1, PART):
                ratio = entry[step][other] * inverted
                for column in range(other, PART):
                    entry[other][column] = entry[other][column] - ratio * entry[step][column]
                rows[other] = jnp.where(lane == k, 0.0, rows[other]) - wide(ratio) * unit
            done = jnp.where((lane > k) & (lane < stop), 0.0, unit)
            store(start + step, done * wide(lax.rsqrt(entry[step][step])))
            hidden = jnp.where((lane > k) & (lane < first + start + PART), 0.0, unit)
            later.append(hidden * wide(inverted))
        for i in range(start + PART, PANEL):
            hide = (lane >= first + start) & (lane < first + start + PART)
            row = jnp.where(hide, 0.0, load(i))
            for step in range(PART):
                row = row - wide(spread(rows[step][:, mine], first - tile * LANES + i + zero)) * later[step]
            store(i, row)


def in_parts(value):
    high = value.astype(jnp.bfloat16)
    rest = value - high.astype(jnp.float32)
    middle = rest.astype(jnp.bfloat16)
    return high, middle, (rest - middle.astype(jnp.float32)).astype(jnp.bfloat16)


def run_copies(plan, semaphores):
    copies = [
        pltpu.make_async_copy(source, place, semaphores.at[index])
        for index, (source, place) in enumerate(plan)
    ]
    for copy in copies:
        copy.start()
    for copy in copies:
        copy.wait()


def run_by_parity(even_plan, odd_plan, semaphores):
    is_even = lax.rem(lax.axis_index("chain"), 2) == 0

    @pl.when(is_even)
    def _():
        run_copies(even_plan, semaphores)

    @pl.when(jnp.logical_not(is_even))
    def _():
        run_copies(odd_plan, semaphores)


def chunk_sizes(half):
    early = max(half // 2, 1)
    return early, early - 1


def cut(line, first, count, place):
    plan = []
    for source, start, size in line:
        low, high = max(first, start), min(first + count, start + size)
        if low < high:
            plan.append((source(low - start, high - low), place(low - first, high - low)))
    return plan


def whole(ref):
    return lambda start, size: ref.at[pl.ds(start, size)]


def plane(ref, s):
    return lambda start, size: ref.at[pl.ds(start, size), s]


def first_plans(first_of, count, half, early, operands, left, right):
    own, got_early, got_late, edge, corner = operands
    late, sectors = half - early, 2 * half
    if first_of[0] == 0:
        even_own, odd_own = (own, 0, early + 1), (own, sectors - early - 1, early + 1)
    else:
        even_own, odd_own = (own, early - 1, late + 2), (own, half - 1, late + 2)

    def plans(first, left_line, right_line, extra):
        zero_line = [(plane(ref, 0), start, size) for ref, start, size in right_line]
        one_line = [(plane(ref, 1), start, size) for ref, start, size in right_line]
        return [
            *cut([(whole(ref), start, size) for ref, start, size in left_line], first - 1, count + 1, whole(left)),
            *cut(zero_line, first, count + 1, plane(right, 0)),
            *cut(one_line + extra, first - 1, count + 1, plane(right, 1)),
        ]

    even = plans(
        first_of[0],
        [(edge, -1, 1), even_own],
        [(got_early, 0, early + 1), (got_late, early + 1, late)],
        [(whole(corner), -1, 1)],
    )
    odd = plans(
        first_of[1],
        [(got_late, half - 1, late), (got_early, sectors - early - 1, early + 1)],
        [odd_own, (edge, sectors, 1)],
        [],
    )
    return even, odd


def second_plans(first_of, count, half, early, operands, left, right):
    keep_early, keep_late, carried_early, carried_late, far, near = operands
    late, sectors = half - early, 2 * half

    def plans(first, left_line, right_line):
        return [
            *cut([(whole(ref), start, size) for ref, start, size in left_line], first - 1, count + 1, whole(left)),
            *cut([(whole(ref), start, size) for ref, start, size in right_line], first, count + 1, whole(right)),
        ]

    even = plans(
        first_of[0],
        [(far, -1, 1), (carried_early, 0, early), (carried_late, early, late)],
        [(keep_early, 0, early), (keep_late, early, late), (near, half, 1)],
    )
    odd = plans(
        first_of[1],
        [(near, half - 1, 1), (keep_late, half, late), (keep_early, sectors - early, early)],
        [(carried_late, half, late), (carried_early, sectors - early, early), (far, sectors, 1)],
    )
    return even, odd


def pair_kernel(second, late, sectors, refs):
    half = sectors // 2
    early, next_early = chunk_sizes(half)
    part = next_early if second else early
    first_of = (part, half) if late else (0, sectors - part)
    table, partner_sizes = refs[:2]
    operand_count = 6 if second else 5
    operands = refs[2 : 2 + operand_count]
    sketch_ref = refs[2 + operand_count]
    outputs = refs[3 + operand_count : -9]
    (
        left_ref,
        right_ref,
        two_ref,
        sample_ref,
        gram_ref,
        inverse_ref,
        rows_ref,
        square_ref,
        in_semaphores,
    ) = refs[-9:]
    send, keep, norm_ref, *extras = outputs
    count, kept, double = sample_ref.shape
    width = double // 2
    plans = second_plans if second else first_plans
    run_by_parity(*plans(first_of, count, half, early, operands, left_ref, right_ref), in_semaphores)

    parity = lax.rem(lax.axis_index("chain"), 2)
    is_even = parity == 0
    first = lax.axis_index("block") * sectors + jnp.where(is_even, *first_of)
    bond = parity if second else 1 - parity
    total = table.shape[1]

    def size_of(row, sector):
        return table[row, sector].astype(jnp.int32)


    def left_size(sector):
        at = jnp.clip(sector, 0, total - 1)
        return jnp.where(is_even, size_of(0, at), partner_sizes[0, 0, at])

    def middle_size(sector):
        at = jnp.clip(sector, 0, total - 1)
        size = size_of(jnp.where(is_even, 1, 0), at)
        return jnp.where(sector < total, size, 0)

    def right_size(sector):
        at = jnp.clip(sector, 0, total - 1)
        size = jnp.where(is_even, partner_sizes[0, 1, at], size_of(1, at))
        return jnp.where(sector < total, size, 0)

    row_index = lax.broadcasted_iota(jnp.int32, (kept, 1), 0)
    eye = (
        lax.broadcasted_iota(jnp.int32, (kept, kept), 0)
        == lax.broadcasted_iota(jnp.int32, (kept, kept), 1)
    )
    block_row = lax.broadcasted_iota(jnp.int32, (width, width), 0)
    block_column = lax.broadcasted_iota(jnp.int32, (width, width), 1)
    column = lax.broadcasted_iota(jnp.int32, (1, width), 1)

    def left(m, s, sector):
        if second:
            return left_ref[m, :, s * width : (s + 1) * width]
        inside = (column < middle_size(sector + s)).astype(jnp.float32).astype(jnp.bfloat16)
        return left_ref[m, s] * inside

    def right(m, s):
        if second:
            return right_ref[m, :, s * width : (s + 1) * width]
        return right_ref[m, s]

    def product(a, b):
        rounded = dot(a, b, LAST if second else PLAIN).astype(jnp.bfloat16)
        return rounded.astype(jnp.float32)

    def put(m, rows, columns, value, row_limit, column_limit):
        if not second:
            value = jnp.where(
                (block_row < row_limit) & (block_column < column_limit), value, 0.0
            )
        two_ref[m, rows, columns] = value.astype(jnp.bfloat16)

    w_empty, w_stay, w_swap, w_full = gate_terms(
        *(jnp.full((1, width), table[4 + bond, term], jnp.float32) for term in range(3))
    )

    @pl.loop(0, count, unroll=min(UNROLL, count))
    def _(m):
        sector = first + m
        below_zero, below_one = left(m, 0, sector - 1), left(m, 1, sector - 1)
        here_zero, here_one = left(m + 1, 0, sector), left(m + 1, 1, sector)
        same_zero, same_one = right(m, 0), right(m, 1)
        next_zero, next_one = right(m + 1, 0), right(m + 1, 1)
        low, high = slice(0, width), slice(width, double)
        rows_low, rows_high = left_size(sector), left_size(sector - 1)
        columns_low, columns_high = right_size(sector), right_size(sector + 1)
        put(m, low, low, w_empty * product(here_zero, same_zero), rows_low, columns_low)
        put(
            m,
            low,
            high,
            w_stay * product(here_zero, next_one) + w_swap * product(here_one, next_zero),
            rows_low,
            columns_high,
        )
        put(
            m,
            high,
            low,
            w_swap * product(below_zero, same_one) + w_stay * product(below_one, same_zero),
            rows_high,
            columns_low,
        )
        put(m, high, high, w_full * product(below_one, next_one), rows_high, columns_high)
        sample = dot(sketch_ref[...], two_ref[m], LAST)
        keep_rows = row_index < size_of(2 + bond, sector)
        sample = jnp.where(keep_rows, sample, 0.0)
        sample_ref[m] = sample
        high_part, middle_part, low_part = in_parts(sample)
        cross = dot(high_part, middle_part, LAST) + dot(high_part, low_part, LAST)
        gram = dot(high_part, high_part, LAST) + (
            dot(middle_part, middle_part, LAST) + (cross + jnp.transpose(cross))
        )
        gram_ref[m] = gram + jnp.where(eye & jnp.logical_not(keep_rows), 1.0, 0.0)

    lane = lax.broadcasted_iota(jnp.int32, (1, kept), 1)
    def eliminate(tile, first, below):
        here = pl.ds(first, PANEL)
        stop = first + PANEL
        for m in range(count):
            for half in range(kept // LANES):
                span = slice(half * LANES, (half + 1) * LANES)
                rows_ref[half, pl.ds(m, PANEL, stride=SUB), :] = gram_ref[m, here, span]
        factor_panel(rows_ref, first, tile)
        for m in range(count):
            solved = jnp.concatenate(
                [
                    rows_ref[half, pl.ds(m, PANEL, stride=SUB), :]
                    for half in range(kept // LANES)
                ],
                axis=1,
            )
            inverse_ref[m, here, :] = jnp.where(lane < stop, solved, 0.0)
            if below.start == kept:
                continue
            high, middle, low = in_parts(solved)
            one = jnp.concatenate([high, high, middle, middle, high, low], axis=0)[:, below]
            two = jnp.concatenate([high, middle, high, middle, low, high], axis=0)
            change = dot(one, two, FIRST)
            kept_part = jnp.where((lane >= first) & (lane < stop), 0.0, gram_ref[m, below, :])
            gram_ref[m, below, :] = kept_part - change

    for tile in range(kept // LANES):
        if second == late:
            for first in range(tile * LANES, (tile + 1) * LANES, PANEL):
                stop = first + PANEL
                eliminate(tile, first, slice(stop - stop % LANES, kept))
        else:

            @pl.loop(0, LANES // PANEL)
            def _(panel, tile=tile):
                first = pl.multiple_of(tile * LANES + panel * PANEL, PANEL)
                eliminate(tile, first, slice(tile * LANES, kept))

    square_ref[...] = jnp.zeros_like(square_ref)

    @pl.loop(0, count, unroll=min(UNROLL, count))
    def _(m):
        inverse_high, inverse_middle, _ = in_parts(inverse_ref[m])
        sample_high, sample_middle, _ = in_parts(sample_ref[m])
        solved = dot(inverse_high, sample_high, PLAIN) + (
            dot(inverse_high, sample_middle, PLAIN) + dot(inverse_middle, sample_high, PLAIN)
        )
        solved = solved * math.sqrt(width)
        basis = solved.astype(jnp.bfloat16)
        coef = dot(basis, two_ref[m], PLAIN)
        square_ref[...] += jnp.sum(coef * coef, axis=0, keepdims=True)
        if second:
            for s in range(2):
                span = slice(s * width, (s + 1) * width)
                turned = jnp.transpose(solved[:, span])
                send[m, s] = jnp.where(is_even, turned, coef[:, span]).astype(jnp.bfloat16)
                keep[m, s] = jnp.where(is_even, coef[:, span], turned).astype(jnp.bfloat16)
        else:
            send[m] = jnp.where(is_even, coef, solved).astype(jnp.bfloat16)
            keep[m] = jnp.where(is_even, solved, coef).astype(jnp.bfloat16)

    norm_ref[0] = jnp.sum(square_ref[...])
    if second:
        if extras:
            extras[0][0] = send[0, 1]
    else:
        at = jnp.where(is_even, count - 1, 0) if late else jnp.where(is_even, 0, count - 1)
        extras[0][0] = send[at] if late else keep[at]


def pair_update(second, late, table, partner_sizes, operands, sketch_turned):
    kept, double = sketch_turned.shape
    width = double // 2
    sectors = table.shape[1] // lax.axis_size("block")
    half = sectors // 2
    early, next_early = chunk_sizes(half)
    part = next_early if second else early
    count = half - part if late else part
    block = (2, width, kept) if second else (kept, double)
    extra = [(1, kept, double)]
    if second:
        extra = [(1, width, kept)] if not late or next_early == 0 else []
    left_shape = (count + 1, kept, double) if second else (count + 1, 2, width, width)
    vmem = pl.BlockSpec(memory_space=pltpu.VMEM)
    smem = pl.BlockSpec(memory_space=pltpu.SMEM)
    anywhere = pl.BlockSpec(memory_space=pl.ANY)

    def kernel(*refs):
        pair_kernel(second, late, sectors, refs)

    return pl.pallas_call(
        kernel,
        out_shape=[
            jax.ShapeDtypeStruct((count, *block), jnp.bfloat16),
            jax.ShapeDtypeStruct((count, *block), jnp.bfloat16),
            jax.ShapeDtypeStruct((1,), jnp.float32),
            *(jax.ShapeDtypeStruct(shape, jnp.bfloat16) for shape in extra),
        ],
        in_specs=[smem] * 2 + [anywhere] * len(operands) + [vmem],
        out_specs=[vmem, vmem, smem] + [vmem] * len(extra),
        scratch_shapes=[
            pltpu.VMEM(left_shape, jnp.bfloat16),
            pltpu.VMEM(left_shape, jnp.bfloat16),
            pltpu.VMEM((count, double, double), jnp.bfloat16),
            pltpu.VMEM((count, kept, double), jnp.float32),
            pltpu.VMEM((count, kept, kept), jnp.float32),
            pltpu.VMEM((count, kept, kept), jnp.float32),
            pltpu.VMEM((kept // LANES, PANEL * SUB, LANES), jnp.float32),
            pltpu.VMEM((1, double), jnp.float32),
            pltpu.SemaphoreType.DMA((8,)),
        ],
        compiler_params=pltpu.CompilerParams(vmem_limit_bytes=32 * 2**20),
        cost_estimate=pl.CostEstimate(
            flops=(count + 12) * 50 * kept * double * double,
            bytes_accessed=8 * count * kept * double * 2,
            transcendentals=0,
        ),
    )(table, partner_sizes, *operands, sketch_turned)


def place_kernel(half, target, norm_refs, refs):
    _, early = chunk_sizes(half)
    late, sectors = half - early, 2 * half
    keep_late, returned_late, lower = refs[:3]
    even_line = [(keep_late, early, late), (returned_late, half, late)]
    odd_line = [(returned_late, early, late), (keep_late, half, late)]
    if early:
        keep_early, returned_early = refs[3:5]
        even_line += [(keep_early, 0, early), (returned_early, sectors - early, early)]
        odd_line += [(returned_early, 0, early), (keep_early, sectors - early, early)]
    lower_line = [(whole(lower), sectors, 1)]
    out, buffer, in_semaphores, out_semaphores = refs[-4:]
    site = out.at[0]
    zero_line = [(plane(ref, 0), start, size) for ref, start, size in odd_line]
    one_line = [(plane(ref, 1), start, size) for ref, start, size in odd_line]
    odd = cut(zero_line, 0, sectors, plane(site, 0))
    odd += cut(one_line + lower_line, 1, sectors, plane(site, 1))
    parts = even_line
    is_even = lax.rem(lax.axis_index("chain"), 2) == 0

    @pl.when(jnp.logical_not(is_even))
    def _():
        run_copies(odd, out_semaphores)

    @pl.when(is_even)
    def _():
        norms, from_second = norm_refs
        rows = (1, buffer.shape[-1])
        norm_even = jnp.full(rows, from_second[0], jnp.float32)
        norm_odd = jnp.full(rows, norms[1] + from_second[1], jnp.float32)
        scale_even = jnp.sqrt(target / norm_even)
        scale = scale_even * jnp.sqrt(target / (scale_even * scale_even * norm_odd))
        coming, going, filled = [], [], 0
        for index, (source, start, size) in enumerate(parts):
            room = buffer.at[pl.ds(filled, size)]
            coming.append(pltpu.make_async_copy(source, room, in_semaphores.at[index]))
            going.append(
                pltpu.make_async_copy(room, out.at[0, pl.ds(start, size)], out_semaphores.at[index])
            )
            filled += size
        for copy in coming:
            copy.start()
        filled = 0
        for index, (source, start, size) in enumerate(parts):
            coming[index].wait()

            @pl.loop(filled, filled + size)
            def _(sector):
                for s in range(2):
                    scaled = buffer[sector, s].astype(jnp.float32) * scale
                    buffer[sector, s] = scaled.astype(jnp.bfloat16)

            going[index].start()
            filled += size
        for copy in going:
            copy.wait()


def place(half, target, norms, operands, site):
    anywhere = pl.BlockSpec(memory_space=pl.ANY)
    rows = 2 * half

    def kernel(*refs):
        place_kernel(half, target, refs[:2], refs[2:])

    return pl.pallas_call(
        kernel,
        out_shape=jax.ShapeDtypeStruct(site.shape, site.dtype),
        in_specs=[pl.BlockSpec(memory_space=pltpu.SMEM)] * 2 + [anywhere] * len(operands),
        out_specs=anywhere,
        scratch_shapes=[
            pltpu.VMEM((rows, *site.shape[2:]), site.dtype),
            pltpu.SemaphoreType.DMA((4,)),
            pltpu.SemaphoreType.DMA((9,)),
        ],
        compiler_params=pltpu.CompilerParams(vmem_limit_bytes=16 * 2**20),
        cost_estimate=pl.CostEstimate(
            flops=0, bytes_accessed=2 * rows * site.size // site.shape[1] * 2, transcendentals=0
        ),
    )(*norms, *operands)


def move(value, target_of):
    sites, parts = lax.axis_size("chain"), lax.axis_size("block")
    pairs = []
    for site in range(sites):
        for part in range(parts):
            target = target_of(site, part)
            if target is not None and 0 <= target[1] < parts:
                pairs.append((site * parts + part, (target[0] % sites) * parts + target[1]))
    return lax.ppermute(value, ("chain", "block"), pairs)


def by_parity(even_target, odd_target):
    return lambda c, b: even_target(c, b) if c % 2 == 0 else odd_target(c, b)


def nowhere(c, b):
    return None


def joined(*parts):
    return jnp.concatenate(parts, axis=0)


def body(site_tensors, sketch, bond_sizes, kept_ranks, couplings):
    sectors = site_tensors.shape[1]
    half = sectors // 2
    early, next_early = chunk_sizes(half)
    width = site_tensors.shape[-1]
    kept = sketch.shape[1]
    parts = lax.axis_size("block")
    is_even = lax.axis_index("chain") % 2 == 0
    own = site_tensors[0]
    sketch_turned = jnp.transpose(sketch)

    terms = jnp.pad(couplings[0], ((0, 0), (0, bond_sizes.shape[2] - couplings.shape[2])))
    table = joined(
        bond_sizes[0].astype(jnp.float32), kept_ranks[0].astype(jnp.float32), terms
    )

    def pick(even_value, odd_value):
        return jnp.where(is_even, even_value, odd_value)

    def update(second, late, *operands):
        return pair_update(
            second, late, table, partner_sizes, operands, sketch_turned
        )

    across = by_parity(lambda c, b: (c + 1, b), lambda c, b: (c - 1, b))
    got_early = move(pick(own[sectors - early - 1 :], own[: early + 1]), across)
    partner_sizes = move(bond_sizes, across)
    edge = move(
        pick(own[-1:], own[:1]), by_parity(lambda c, b: (c, b + 1), lambda c, b: (c, b - 1))
    )
    corner = move(own[-1:, 1], by_parity(nowhere, lambda c, b: (c - 1, b + 1)))
    sent = pick(own[half - 1 : sectors - early - 1], own[early + 1 : half + 1])
    own_early = pick(own[: early + 1], own[sectors - early - 1 :])
    own_late = pick(own[early - 1 : half + 1], own[half - 1 : sectors - early + 1])
    sent, got_early = lax.optimization_barrier((sent, got_early))
    got_late = move(sent, across)
    send_early, keep_early, norm_early, halo_early = update(
        False, False, own_early, got_early, got_early, edge, corner
    )

    along = by_parity(lambda c, b: (c + 2, b), lambda c, b: (c - 2, b))
    far = move(
        halo_early, by_parity(lambda c, b: (c - 1, b - 1), lambda c, b: (c + 1, b + 1))
    )
    carried_early = move(send_early, along)
    send_late, keep_late, norm_late, halo_late = update(
        False, True, own_late, got_early, got_late, edge, corner
    )
    norm_even = norm_early + norm_late
    carried_late = move(send_late, along)
    near = move(halo_late, across)

    back = by_parity(lambda c, b: (c - 1, b), lambda c, b: (c + 1, b))
    norm_odd = 0.0
    first_parts = ()
    if next_early:
        send_early, kept_early, norm_early, lower_first = update(
            True, False, keep_early, keep_early, carried_early, carried_early, far, far
        )
        norm_odd = norm_early
        send_early, carried_late = lax.optimization_barrier((send_early, carried_late))
        returned_early = move(send_early, back)
        first_parts = (kept_early, returned_early)
    send_late, kept_late, norm_late, *lower = update(
        True, True, keep_early, keep_late, carried_early, carried_late, far, near
    )
    if next_early == 0:
        lower_first = lower[0]
    lower_above = move(lower_first, by_parity(lambda c, b: (c - 1, b - 1), nowhere))
    if next_early:
        send_late, returned_early, lower_above = lax.optimization_barrier(
            (send_late, returned_early, lower_above)
        )
        first_parts = (kept_early, returned_early)
    returned_late = move(send_late, back)

    norms = lax.psum(joined(norm_even, norm_odd + norm_late), "block")
    from_right = move(norms, by_parity(nowhere, lambda c, b: (c - 1, b)))
    from_second = move(
        from_right + jnp.where(jnp.arange(2) == 0, norms, 0.0),
        by_parity(lambda c, b: (c + 2, b), nowhere),
    )
    target = float(sectors * parts * kept * width)
    norms = (norms, from_second)

    ready = (kept_late, returned_late, lower_above, *first_parts)
    return place(half, target, norms, ready, site_tensors)


def solution(mesh):
    placed = (
        P("chain", "block", None, None, None),
        P(),
        P("chain", None, None),
        P("chain", None, None),
        P("chain", None, None),
    )
    return jax.shard_map(
        body,
        mesh=mesh,
        in_specs=placed,
        out_specs=P("chain", "block", None, None, None),
        check_vma=False,
    )
```

```python
import math

import jax
import jax.numpy as jnp
from jax import lax
from jax.experimental import pallas as pl
from jax.experimental.pallas import tpu as pltpu
from jax.sharding import PartitionSpec as P

tau_step = 0.5
SUB = 8
LANES = 128
PANEL = 32
PART = 8
UNROLL = 2
FIRST = (((0,), (0,)), ((), ()))
LAST = (((1,), (1,)), ((), ()))
PLAIN = (((1,), (0,)), ((), ()))


def gate_terms(hopping, ising_term, field_term):
    rotation = 0.5 * tau_step * hopping
    middle_scale = jnp.exp(0.25 * tau_step * ising_term)
    weight_empty = jnp.exp(-tau_step * (0.25 * ising_term - 0.5 * field_term))
    weight_full = jnp.exp(-tau_step * (0.25 * ising_term + 0.5 * field_term))
    grown, shrunk = jnp.exp(rotation), jnp.exp(-rotation)
    weight_stay = middle_scale * (0.5 * (grown + shrunk))
    weight_swap = -middle_scale * (0.5 * (grown - shrunk))
    return weight_empty, weight_stay, weight_swap, weight_full


def dot(left, right, dims):
    return lax.dot_general(left, right, dims, preferred_element_type=jnp.float32)


def spread(row, lane_index):
    return jnp.take_along_axis(row, lane_index, axis=1)


def refined_reciprocal(value):
    guess = pltpu.reciprocal(value, approx=True)
    return guess * (2.0 - value * guess)


def factor_panel(rows_ref, first, tile):
    lanes = rows_ref.shape[0] * LANES
    lane = lax.broadcasted_iota(jnp.int32, (SUB, lanes), 1)
    zero = jnp.zeros((SUB, LANES), jnp.int32)
    mine = slice(tile * LANES, (tile + 1) * LANES)
    stop = first + PANEL

    def load(index):
        at = slice(index * SUB, (index + 1) * SUB)
        return jnp.concatenate([rows_ref[half, at, :] for half in range(lanes // LANES)], axis=1)

    def wide(value):
        return jnp.concatenate([value] * (lanes // LANES), axis=1)

    def store(index, value):
        at = slice(index * SUB, (index + 1) * SUB)
        for half in range(lanes // LANES):
            rows_ref[half, at, :] = value[:, half * LANES : (half + 1) * LANES]

    for start in range(0, PANEL, PART):
        rows = [load(start + i) for i in range(PART)]
        base = first - tile * LANES + start
        entry = [
            [spread(rows[i][:, mine], base + j + zero) if j >= i else None for j in range(PART)]
            for i in range(PART)
        ]
        later = []
        for step in range(PART):
            k = first + start + step
            inverted = refined_reciprocal(entry[step][step])
            unit = jnp.where(lane == k, 1.0, rows[step])
            for other in range(step + 1, PART):
                ratio = entry[step][other] * inverted
                for column in range(other, PART):
                    entry[other][column] = entry[other][column] - ratio * entry[step][column]
                rows[other] = jnp.where(lane == k, 0.0, rows[other]) - wide(ratio) * unit
            done = jnp.where((lane > k) & (lane < stop), 0.0, unit)
            store(start + step, done * wide(lax.rsqrt(entry[step][step])))
            hidden = jnp.where((lane > k) & (lane < first + start + PART), 0.0, unit)
            later.append(hidden * wide(inverted))
        for i in range(start + PART, PANEL):
            hide = (lane >= first + start) & (lane < first + start + PART)
            row = jnp.where(hide, 0.0, load(i))
            for step in range(PART):
                row = row - wide(spread(rows[step][:, mine], first - tile * LANES + i + zero)) * later[step]
            store(i, row)


def in_parts(value):
    high = value.astype(jnp.bfloat16)
    rest = value - high.astype(jnp.float32)
    middle = rest.astype(jnp.bfloat16)
    return high, middle, (rest - middle.astype(jnp.float32)).astype(jnp.bfloat16)


def run_copies(plan, semaphores):
    copies = [
        pltpu.make_async_copy(source, place, semaphores.at[index])
        for index, (source, place) in enumerate(plan)
    ]
    for copy in copies:
        copy.start()
    for copy in copies:
        copy.wait()


def run_by_parity(even_plan, odd_plan, semaphores):
    is_even = lax.rem(lax.axis_index("chain"), 2) == 0

    @pl.when(is_even)
    def _():
        run_copies(even_plan, semaphores)

    @pl.when(jnp.logical_not(is_even))
    def _():
        run_copies(odd_plan, semaphores)


def chunk_sizes(half):
    early = max(half // 2, 1)
    return early, early - 1


def cut(line, first, count, place):
    plan = []
    for source, start, size in line:
        low, high = max(first, start), min(first + count, start + size)
        if low < high:
            plan.append((source(low - start, high - low), place(low - first, high - low)))
    return plan


def whole(ref):
    return lambda start, size: ref.at[pl.ds(start, size)]


def plane(ref, s):
    return lambda start, size: ref.at[pl.ds(start, size), s]


def first_plans(first_of, count, half, early, operands, left, right):
    own, got_early, got_late, edge, corner = operands
    late, sectors = half - early, 2 * half
    if first_of[0] == 0:
        even_own, odd_own = (own, 0, early + 1), (own, sectors - early - 1, early + 1)
    else:
        even_own, odd_own = (own, early - 1, late + 2), (own, half - 1, late + 2)

    def plans(first, left_line, right_line, extra):
        zero_line = [(plane(ref, 0), start, size) for ref, start, size in right_line]
        one_line = [(plane(ref, 1), start, size) for ref, start, size in right_line]
        return [
            *cut([(whole(ref), start, size) for ref, start, size in left_line], first - 1, count + 1, whole(left)),
            *cut(zero_line, first, count + 1, plane(right, 0)),
            *cut(one_line + extra, first - 1, count + 1, plane(right, 1)),
        ]

    even = plans(
        first_of[0],
        [(edge, -1, 1), even_own],
        [(got_early, 0, early + 1), (got_late, early + 1, late)],
        [(whole(corner), -1, 1)],
    )
    odd = plans(
        first_of[1],
        [(got_late, half - 1, late), (got_early, sectors - early - 1, early + 1)],
        [odd_own, (edge, sectors, 1)],
        [],
    )
    return even, odd


def second_plans(first_of, count, half, early, operands, left, right):
    keep_early, keep_late, carried_early, carried_late, far, near = operands
    late, sectors = half - early, 2 * half

    def plans(first, left_line, right_line):
        return [
            *cut([(whole(ref), start, size) for ref, start, size in left_line], first - 1, count + 1, whole(left)),
            *cut([(whole(ref), start, size) for ref, start, size in right_line], first, count + 1, whole(right)),
        ]

    even = plans(
        first_of[0],
        [(far, -1, 1), (carried_early, 0, early), (carried_late, early, late)],
        [(keep_early, 0, early), (keep_late, early, late), (near, half, 1)],
    )
    odd = plans(
        first_of[1],
        [(near, half - 1, 1), (keep_late, half, late), (keep_early, sectors - early, early)],
        [(carried_late, half, late), (carried_early, sectors - early, early), (far, sectors, 1)],
    )
    return even, odd


def pair_kernel(second, late, sectors, refs):
    half = sectors // 2
    early, next_early = chunk_sizes(half)
    part = next_early if second else early
    first_of = (part, half) if late else (0, sectors - part)
    table, partner_sizes = refs[:2]
    operand_count = 6 if second else 5
    operands = refs[2 : 2 + operand_count]
    sketch_ref = refs[2 + operand_count]
    outputs = refs[3 + operand_count : -9]
    (
        left_ref,
        right_ref,
        two_ref,
        sample_ref,
        gram_ref,
        inverse_ref,
        rows_ref,
        square_ref,
        in_semaphores,
    ) = refs[-9:]
    send, keep, norm_ref, *extras = outputs
    count, kept, double = sample_ref.shape
    width = double // 2
    plans = second_plans if second else first_plans
    run_by_parity(*plans(first_of, count, half, early, operands, left_ref, right_ref), in_semaphores)

    parity = lax.rem(lax.axis_index("chain"), 2)
    is_even = parity == 0
    first = lax.axis_index("block") * sectors + jnp.where(is_even, *first_of)
    bond = parity if second else 1 - parity
    total = table.shape[1]

    def size_of(row, sector):
        return table[row, sector].astype(jnp.int32)


    def left_size(sector):
        at = jnp.clip(sector, 0, total - 1)
        return jnp.where(is_even, size_of(0, at), partner_sizes[0, 0, at])

    def middle_size(sector):
        at = jnp.clip(sector, 0, total - 1)
        size = size_of(jnp.where(is_even, 1, 0), at)
        return jnp.where(sector < total, size, 0)

    def right_size(sector):
        at = jnp.clip(sector, 0, total - 1)
        size = jnp.where(is_even, partner_sizes[0, 1, at], size_of(1, at))
        return jnp.where(sector < total, size, 0)

    row_index = lax.broadcasted_iota(jnp.int32, (kept, 1), 0)
    eye = (
        lax.broadcasted_iota(jnp.int32, (kept, kept), 0)
        == lax.broadcasted_iota(jnp.int32, (kept, kept), 1)
    )
    block_row = lax.broadcasted_iota(jnp.int32, (width, width), 0)
    block_column = lax.broadcasted_iota(jnp.int32, (width, width), 1)
    column = lax.broadcasted_iota(jnp.int32, (1, width), 1)

    def left(m, s, sector):
        if second:
            return left_ref[m, :, s * width : (s + 1) * width]
        inside = (column < middle_size(sector + s)).astype(jnp.float32).astype(jnp.bfloat16)
        return left_ref[m, s] * inside

    def right(m, s):
        if second:
            return right_ref[m, :, s * width : (s + 1) * width]
        return right_ref[m, s]

    def product(a, b):
        rounded = dot(a, b, LAST if second else PLAIN).astype(jnp.bfloat16)
        return rounded.astype(jnp.float32)

    def put(m, rows, columns, value, row_limit, column_limit):
        if not second:
            value = jnp.where(
                (block_row < row_limit) & (block_column < column_limit), value, 0.0
            )
        two_ref[m, rows, columns] = value.astype(jnp.bfloat16)

    w_empty, w_stay, w_swap, w_full = gate_terms(
        *(jnp.full((1, width), table[4 + bond, term], jnp.float32) for term in range(3))
    )

    @pl.loop(0, count, unroll=min(UNROLL, count))
    def _(m):
        sector = first + m
        below_zero, below_one = left(m, 0, sector - 1), left(m, 1, sector - 1)
        here_zero, here_one = left(m + 1, 0, sector), left(m + 1, 1, sector)
        same_zero, same_one = right(m, 0), right(m, 1)
        next_zero, next_one = right(m + 1, 0), right(m + 1, 1)
        low, high = slice(0, width), slice(width, double)
        rows_low, rows_high = left_size(sector), left_size(sector - 1)
        columns_low, columns_high = right_size(sector), right_size(sector + 1)
        put(m, low, low, w_empty * product(here_zero, same_zero), rows_low, columns_low)
        put(
            m,
            low,
            high,
            w_stay * product(here_zero, next_one) + w_swap * product(here_one, next_zero),
            rows_low,
            columns_high,
        )
        put(
            m,
            high,
            low,
            w_swap * product(below_zero, same_one) + w_stay * product(below_one, same_zero),
            rows_high,
            columns_low,
        )
        put(m, high, high, w_full * product(below_one, next_one), rows_high, columns_high)
        sample = dot(sketch_ref[...], two_ref[m], LAST)
        keep_rows = row_index < size_of(2 + bond, sector)
        sample = jnp.where(keep_rows, sample, 0.0)
        sample_ref[m] = sample
        high_part, middle_part, low_part = in_parts(sample)
        cross = dot(high_part, middle_part, LAST) + dot(high_part, low_part, LAST)
        gram = dot(high_part, high_part, LAST) + (
            dot(middle_part, middle_part, LAST) + (cross + jnp.transpose(cross))
        )
        gram_ref[m] = gram + jnp.where(eye & jnp.logical_not(keep_rows), 1.0, 0.0)

    lane = lax.broadcasted_iota(jnp.int32, (1, kept), 1)
    def eliminate(tile, first, below):
        here = pl.ds(first, PANEL)
        stop = first + PANEL
        for m in range(count):
            for half in range(kept // LANES):
                span = slice(half * LANES, (half + 1) * LANES)
                rows_ref[half, pl.ds(m, PANEL, stride=SUB), :] = gram_ref[m, here, span]
        factor_panel(rows_ref, first, tile)
        for m in range(count):
            solved = jnp.concatenate(
                [
                    rows_ref[half, pl.ds(m, PANEL, stride=SUB), :]
                    for half in range(kept // LANES)
                ],
                axis=1,
            )
            inverse_ref[m, here, :] = jnp.where(lane < stop, solved, 0.0)
            if below.start == kept:
                continue
            high, middle, low = in_parts(solved)
            one = jnp.concatenate([high, high, middle, middle, high, low], axis=0)[:, below]
            two = jnp.concatenate([high, middle, high, middle, low, high], axis=0)
            change = dot(one, two, FIRST)
            kept_part = jnp.where((lane >= first) & (lane < stop), 0.0, gram_ref[m, below, :])
            gram_ref[m, below, :] = kept_part - change

    for tile in range(kept // LANES):
        if second and late:
            for first in range(tile * LANES, (tile + 1) * LANES, PANEL):
                stop = first + PANEL
                eliminate(tile, first, slice(stop - stop % LANES, kept))
        else:

            @pl.loop(0, LANES // PANEL)
            def _(panel, tile=tile):
                first = pl.multiple_of(tile * LANES + panel * PANEL, PANEL)
                eliminate(tile, first, slice(tile * LANES, kept))

    square_ref[...] = jnp.zeros_like(square_ref)

    @pl.loop(0, count, unroll=min(UNROLL, count))
    def _(m):
        inverse_high, inverse_middle, _ = in_parts(inverse_ref[m])
        sample_high, sample_middle, _ = in_parts(sample_ref[m])
        solved = dot(inverse_high, sample_high, PLAIN) + (
            dot(inverse_high, sample_middle, PLAIN) + dot(inverse_middle, sample_high, PLAIN)
        )
        solved = solved * math.sqrt(width)
        basis = solved.astype(jnp.bfloat16)
        coef = dot(basis, two_ref[m], PLAIN)
        square_ref[...] += jnp.sum(coef * coef, axis=0, keepdims=True)
        if second:
            for s in range(2):
                span = slice(s * width, (s + 1) * width)
                turned = jnp.transpose(solved[:, span])
                send[m, s] = jnp.where(is_even, turned, coef[:, span]).astype(jnp.bfloat16)
                keep[m, s] = jnp.where(is_even, coef[:, span], turned).astype(jnp.bfloat16)
        else:
            send[m] = jnp.where(is_even, coef, solved).astype(jnp.bfloat16)
            keep[m] = jnp.where(is_even, solved, coef).astype(jnp.bfloat16)

    norm_ref[0] = jnp.sum(square_ref[...])
    if second:
        if extras:
            extras[0][0] = send[0, 1]
    else:
        at = jnp.where(is_even, count - 1, 0) if late else jnp.where(is_even, 0, count - 1)
        extras[0][0] = send[at] if late else keep[at]


def pair_update(second, late, table, partner_sizes, operands, sketch_turned):
    kept, double = sketch_turned.shape
    width = double // 2
    sectors = table.shape[1] // lax.axis_size("block")
    half = sectors // 2
    early, next_early = chunk_sizes(half)
    part = next_early if second else early
    count = half - part if late else part
    block = (2, width, kept) if second else (kept, double)
    extra = [(1, kept, double)]
    if second:
        extra = [(1, width, kept)] if not late or next_early == 0 else []
    left_shape = (count + 1, kept, double) if second else (count + 1, 2, width, width)
    vmem = pl.BlockSpec(memory_space=pltpu.VMEM)
    smem = pl.BlockSpec(memory_space=pltpu.SMEM)
    anywhere = pl.BlockSpec(memory_space=pl.ANY)

    def kernel(*refs):
        pair_kernel(second, late, sectors, refs)

    return pl.pallas_call(
        kernel,
        out_shape=[
            jax.ShapeDtypeStruct((count, *block), jnp.bfloat16),
            jax.ShapeDtypeStruct((count, *block), jnp.bfloat16),
            jax.ShapeDtypeStruct((1,), jnp.float32),
            *(jax.ShapeDtypeStruct(shape, jnp.bfloat16) for shape in extra),
        ],
        in_specs=[smem] * 2 + [anywhere] * len(operands) + [vmem],
        out_specs=[vmem, vmem, smem] + [vmem] * len(extra),
        scratch_shapes=[
            pltpu.VMEM(left_shape, jnp.bfloat16),
            pltpu.VMEM(left_shape, jnp.bfloat16),
            pltpu.VMEM((count, double, double), jnp.bfloat16),
            pltpu.VMEM((count, kept, double), jnp.float32),
            pltpu.VMEM((count, kept, kept), jnp.float32),
            pltpu.VMEM((count, kept, kept), jnp.float32),
            pltpu.VMEM((kept // LANES, PANEL * SUB, LANES), jnp.float32),
            pltpu.VMEM((1, double), jnp.float32),
            pltpu.SemaphoreType.DMA((8,)),
        ],
        compiler_params=pltpu.CompilerParams(vmem_limit_bytes=32 * 2**20),
        cost_estimate=pl.CostEstimate(
            flops=(count + 12) * 50 * kept * double * double,
            bytes_accessed=8 * count * kept * double * 2,
            transcendentals=0,
        ),
    )(table, partner_sizes, *operands, sketch_turned)


def place_kernel(half, target, norm_refs, refs):
    _, early = chunk_sizes(half)
    late, sectors = half - early, 2 * half
    keep_late, returned_late, lower = refs[:3]
    even_line = [(keep_late, early, late), (returned_late, half, late)]
    odd_line = [(returned_late, early, late), (keep_late, half, late)]
    if early:
        keep_early, returned_early = refs[3:5]
        even_line += [(keep_early, 0, early), (returned_early, sectors - early, early)]
        odd_line += [(returned_early, 0, early), (keep_early, sectors - early, early)]
    lower_line = [(whole(lower), sectors, 1)]
    out, buffer, in_semaphores, out_semaphores = refs[-4:]
    site = out.at[0]
    zero_line = [(plane(ref, 0), start, size) for ref, start, size in odd_line]
    one_line = [(plane(ref, 1), start, size) for ref, start, size in odd_line]
    odd = cut(zero_line, 0, sectors, plane(site, 0))
    odd += cut(one_line + lower_line, 1, sectors, plane(site, 1))
    parts = even_line
    is_even = lax.rem(lax.axis_index("chain"), 2) == 0

    @pl.when(jnp.logical_not(is_even))
    def _():
        run_copies(odd, out_semaphores)

    @pl.when(is_even)
    def _():
        norms, from_left, direct = norm_refs
        rows = (1, buffer.shape[-1])
        norm_even = jnp.full(rows, from_left[0] + direct[0], jnp.float32)
        norm_odd = jnp.full(rows, norms[1] + from_left[1], jnp.float32)
        scale_even = jnp.sqrt(target / norm_even)
        scale = scale_even * jnp.sqrt(target / (scale_even * scale_even * norm_odd))
        coming, going, filled = [], [], 0
        for index, (source, start, size) in enumerate(parts):
            room = buffer.at[pl.ds(filled, size)]
            coming.append(pltpu.make_async_copy(source, room, in_semaphores.at[index]))
            going.append(
                pltpu.make_async_copy(room, out.at[0, pl.ds(start, size)], out_semaphores.at[index])
            )
            filled += size
        for copy in coming:
            copy.start()
        filled = 0
        for index, (source, start, size) in enumerate(parts):
            coming[index].wait()

            @pl.loop(filled, filled + size)
            def _(sector):
                for s in range(2):
                    scaled = buffer[sector, s].astype(jnp.float32) * scale
                    buffer[sector, s] = scaled.astype(jnp.bfloat16)

            going[index].start()
            filled += size
        for copy in going:
            copy.wait()


def place(half, target, norms, operands, site):
    anywhere = pl.BlockSpec(memory_space=pl.ANY)
    rows = 2 * half

    def kernel(*refs):
        place_kernel(half, target, refs[:3], refs[3:])

    return pl.pallas_call(
        kernel,
        out_shape=jax.ShapeDtypeStruct(site.shape, site.dtype),
        in_specs=[pl.BlockSpec(memory_space=pltpu.SMEM)] * 3 + [anywhere] * len(operands),
        out_specs=anywhere,
        scratch_shapes=[
            pltpu.VMEM((rows, *site.shape[2:]), site.dtype),
            pltpu.SemaphoreType.DMA((4,)),
            pltpu.SemaphoreType.DMA((9,)),
        ],
        compiler_params=pltpu.CompilerParams(vmem_limit_bytes=16 * 2**20),
        cost_estimate=pl.CostEstimate(
            flops=0, bytes_accessed=2 * rows * site.size // site.shape[1] * 2, transcendentals=0
        ),
    )(*norms, *operands)


def move(value, target_of):
    sites, parts = lax.axis_size("chain"), lax.axis_size("block")
    pairs = []
    for site in range(sites):
        for part in range(parts):
            target = target_of(site, part)
            if target is not None and 0 <= target[1] < parts:
                pairs.append((site * parts + part, (target[0] % sites) * parts + target[1]))
    return lax.ppermute(value, ("chain", "block"), pairs)


def by_parity(even_target, odd_target):
    return lambda c, b: even_target(c, b) if c % 2 == 0 else odd_target(c, b)


def nowhere(c, b):
    return None


def joined(*parts):
    return jnp.concatenate(parts, axis=0)


def body(site_tensors, sketch, bond_sizes, kept_ranks, couplings):
    sectors = site_tensors.shape[1]
    half = sectors // 2
    early, next_early = chunk_sizes(half)
    width = site_tensors.shape[-1]
    kept = sketch.shape[1]
    parts = lax.axis_size("block")
    is_even = lax.axis_index("chain") % 2 == 0
    own = site_tensors[0]
    sketch_turned = jnp.transpose(sketch)

    terms = jnp.pad(couplings[0], ((0, 0), (0, bond_sizes.shape[2] - couplings.shape[2])))
    table = joined(
        bond_sizes[0].astype(jnp.float32), kept_ranks[0].astype(jnp.float32), terms
    )

    def pick(even_value, odd_value):
        return jnp.where(is_even, even_value, odd_value)

    def update(second, late, *operands):
        return pair_update(
            second, late, table, partner_sizes, operands, sketch_turned
        )

    across = by_parity(lambda c, b: (c + 1, b), lambda c, b: (c - 1, b))
    got_early = move(pick(own[sectors - early - 1 :], own[: early + 1]), across)
    partner_sizes = move(bond_sizes, across)
    edge = move(
        pick(own[-1:], own[:1]), by_parity(lambda c, b: (c, b + 1), lambda c, b: (c, b - 1))
    )
    corner = move(own[-1:, 1], by_parity(nowhere, lambda c, b: (c - 1, b + 1)))
    sent = pick(own[half - 1 : sectors - early - 1], own[early + 1 : half + 1])
    own_early = pick(own[: early + 1], own[sectors - early - 1 :])
    own_late = pick(own[early - 1 : half + 1], own[half - 1 : sectors - early + 1])
    sent, got_early = lax.optimization_barrier((sent, got_early))
    got_late = move(sent, across)
    send_early, keep_early, norm_early, halo_early = update(
        False, False, own_early, got_early, got_early, edge, corner
    )

    along = by_parity(lambda c, b: (c + 2, b), lambda c, b: (c - 2, b))
    far = move(
        halo_early, by_parity(lambda c, b: (c - 1, b - 1), lambda c, b: (c + 1, b + 1))
    )
    carried_early = move(send_early, along)
    send_late, keep_late, norm_late, halo_late = update(
        False, True, own_late, got_early, got_late, edge, corner
    )
    norm_even = norm_early + norm_late
    carried_late = move(send_late, along)
    near = move(halo_late, across)

    back = by_parity(lambda c, b: (c - 1, b), lambda c, b: (c + 1, b))
    norm_odd = 0.0
    first_parts = ()
    if next_early:
        send_early, kept_early, norm_early, lower_first = update(
            True, False, keep_early, keep_early, carried_early, carried_early, far, far
        )
        norm_odd = norm_early
        send_early, carried_late = lax.optimization_barrier((send_early, carried_late))
        returned_early = move(send_early, back)
        first_parts = (kept_early, returned_early)
    send_late, kept_late, norm_late, *lower = update(
        True, True, keep_early, keep_late, carried_early, carried_late, far, near
    )
    if next_early == 0:
        lower_first = lower[0]
    lower_above = move(lower_first, by_parity(lambda c, b: (c - 1, b - 1), nowhere))
    if next_early:
        send_late, returned_early, lower_above = lax.optimization_barrier(
            (send_late, returned_early, lower_above)
        )
        first_parts = (kept_early, returned_early)
    returned_late = move(send_late, back)

    norms = lax.psum(joined(norm_even, norm_odd + norm_late), "block")
    hops = {1: 2, 3: -1}
    passed = move(norms, lambda c, b: (c + hops[c % 4], b) if c % 2 else None)
    direct = move(norms, lambda c, b: (c + 2, b) if c % 4 == 0 else None)
    mine = (lax.axis_index("chain") % 4 == 2) & (jnp.arange(2) == 0)
    hops_on = {3: -1, 2: 2}
    from_left = move(
        passed + jnp.where(mine, norms, 0.0),
        lambda c, b: (c + hops_on[c % 4], b) if c % 4 in hops_on else None,
    )
    target = float(sectors * parts * kept * width)
    norms = (norms, from_left, direct)

    ready = (kept_late, returned_late, lower_above, *first_parts)
    return place(half, target, norms, ready, site_tensors)


def solution(mesh):
    placed = (
        P("chain", "block", None, None, None),
        P(),
        P("chain", None, None),
        P("chain", None, None),
        P("chain", None, None),
    )
    return jax.shard_map(
        body,
        mesh=mesh,
        in_specs=placed,
        out_specs=P("chain", "block", None, None, None),
        check_vma=False,
    )
```

```python
import math

import jax
import jax.numpy as jnp
from jax import lax
from jax.experimental import pallas as pl
from jax.experimental.pallas import tpu as pltpu
from jax.sharding import PartitionSpec as P

tau_step = 0.5
SUB = 8
LANES = 128
PANEL = 32
PART = 8
UNROLL = 2
FIRST = (((0,), (0,)), ((), ()))
LAST = (((1,), (1,)), ((), ()))
PLAIN = (((1,), (0,)), ((), ()))


def gate_terms(hopping, ising_term, field_term):
    rotation = 0.5 * tau_step * hopping
    middle_scale = jnp.exp(0.25 * tau_step * ising_term)
    weight_empty = jnp.exp(-tau_step * (0.25 * ising_term - 0.5 * field_term))
    weight_full = jnp.exp(-tau_step * (0.25 * ising_term + 0.5 * field_term))
    grown, shrunk = jnp.exp(rotation), jnp.exp(-rotation)
    weight_stay = middle_scale * (0.5 * (grown + shrunk))
    weight_swap = -middle_scale * (0.5 * (grown - shrunk))
    return weight_empty, weight_stay, weight_swap, weight_full


def dot(left, right, dims):
    return lax.dot_general(left, right, dims, preferred_element_type=jnp.float32)


def spread(row, lane_index):
    return jnp.take_along_axis(row, lane_index, axis=1)


def refined_reciprocal(value):
    guess = pltpu.reciprocal(value, approx=True)
    return guess * (2.0 - value * guess)


def factor_panel(rows_ref, first, tile):
    lanes = rows_ref.shape[0] * LANES
    lane = lax.broadcasted_iota(jnp.int32, (SUB, lanes), 1)
    zero = jnp.zeros((SUB, LANES), jnp.int32)
    mine = slice(tile * LANES, (tile + 1) * LANES)
    stop = first + PANEL

    def load(index):
        at = slice(index * SUB, (index + 1) * SUB)
        return jnp.concatenate([rows_ref[half, at, :] for half in range(lanes // LANES)], axis=1)

    def wide(value):
        return jnp.concatenate([value] * (lanes // LANES), axis=1)

    def store(index, value):
        at = slice(index * SUB, (index + 1) * SUB)
        for half in range(lanes // LANES):
            rows_ref[half, at, :] = value[:, half * LANES : (half + 1) * LANES]

    for start in range(0, PANEL, PART):
        rows = [load(start + i) for i in range(PART)]
        base = first - tile * LANES + start
        entry = [
            [spread(rows[i][:, mine], base + j + zero) if j >= i else None for j in range(PART)]
            for i in range(PART)
        ]
        later = []
        for step in range(PART):
            k = first + start + step
            inverted = refined_reciprocal(entry[step][step])
            unit = jnp.where(lane == k, 1.0, rows[step])
            for other in range(step + 1, PART):
                ratio = entry[step][other] * inverted
                for column in range(other, PART):
                    entry[other][column] = entry[other][column] - ratio * entry[step][column]
                rows[other] = jnp.where(lane == k, 0.0, rows[other]) - wide(ratio) * unit
            done = jnp.where((lane > k) & (lane < stop), 0.0, unit)
            store(start + step, done * wide(lax.rsqrt(entry[step][step])))
            hidden = jnp.where((lane > k) & (lane < first + start + PART), 0.0, unit)
            later.append(hidden * wide(inverted))
        for i in range(start + PART, PANEL):
            hide = (lane >= first + start) & (lane < first + start + PART)
            row = jnp.where(hide, 0.0, load(i))
            for step in range(PART):
                row = row - wide(spread(rows[step][:, mine], first - tile * LANES + i + zero)) * later[step]
            store(i, row)


def in_parts(value):
    high = value.astype(jnp.bfloat16)
    rest = value - high.astype(jnp.float32)
    middle = rest.astype(jnp.bfloat16)
    return high, middle, (rest - middle.astype(jnp.float32)).astype(jnp.bfloat16)


def run_copies(plan, semaphores):
    copies = [
        pltpu.make_async_copy(source, place, semaphores.at[index])
        for index, (source, place) in enumerate(plan)
    ]
    for copy in copies:
        copy.start()
    for copy in copies:
        copy.wait()


def run_by_parity(even_plan, odd_plan, semaphores):
    is_even = lax.rem(lax.axis_index("chain"), 2) == 0

    @pl.when(is_even)
    def _():
        run_copies(even_plan, semaphores)

    @pl.when(jnp.logical_not(is_even))
    def _():
        run_copies(odd_plan, semaphores)


def chunk_sizes(half):
    early = max(half // 2, 1)
    return early, early - 1


def cut(line, first, count, place):
    plan = []
    for source, start, size in line:
        low, high = max(first, start), min(first + count, start + size)
        if low < high:
            plan.append((source(low - start, high - low), place(low - first, high - low)))
    return plan


def whole(ref):
    return lambda start, size: ref.at[pl.ds(start, size)]


def plane(ref, s):
    return lambda start, size: ref.at[pl.ds(start, size), s]


def first_plans(first_of, count, half, early, operands, left, right):
    own, got_early, got_late, edge, corner = operands
    late, sectors = half - early, 2 * half
    if first_of[0] == 0:
        even_own, odd_own = (own, 0, early + 1), (own, sectors - early - 1, early + 1)
    else:
        even_own, odd_own = (own, early - 1, late + 2), (own, half - 1, late + 2)

    def plans(first, left_line, right_line, extra):
        zero_line = [(plane(ref, 0), start, size) for ref, start, size in right_line]
        one_line = [(plane(ref, 1), start, size) for ref, start, size in right_line]
        return [
            *cut([(whole(ref), start, size) for ref, start, size in left_line], first - 1, count + 1, whole(left)),
            *cut(zero_line, first, count + 1, plane(right, 0)),
            *cut(one_line + extra, first - 1, count + 1, plane(right, 1)),
        ]

    even = plans(
        first_of[0],
        [(edge, -1, 1), even_own],
        [(got_early, 0, early + 1), (got_late, early + 1, late)],
        [(whole(corner), -1, 1)],
    )
    odd = plans(
        first_of[1],
        [(got_late, half - 1, late), (got_early, sectors - early - 1, early + 1)],
        [odd_own, (edge, sectors, 1)],
        [],
    )
    return even, odd


def second_plans(first_of, count, half, early, operands, left, right):
    keep_early, keep_late, carried_early, carried_late, far, near = operands
    late, sectors = half - early, 2 * half

    def plans(first, left_line, right_line):
        return [
            *cut([(whole(ref), start, size) for ref, start, size in left_line], first - 1, count + 1, whole(left)),
            *cut([(whole(ref), start, size) for ref, start, size in right_line], first, count + 1, whole(right)),
        ]

    even = plans(
        first_of[0],
        [(far, -1, 1), (carried_early, 0, early), (carried_late, early, late)],
        [(keep_early, 0, early), (keep_late, early, late), (near, half, 1)],
    )
    odd = plans(
        first_of[1],
        [(near, half - 1, 1), (keep_late, half, late), (keep_early, sectors - early, early)],
        [(carried_late, half, late), (carried_early, sectors - early, early), (far, sectors, 1)],
    )
    return even, odd


def pair_kernel(second, late, sectors, refs):
    half = sectors // 2
    early, next_early = chunk_sizes(half)
    part = next_early if second else early
    first_of = (part, half) if late else (0, sectors - part)
    table, partner_sizes = refs[:2]
    operand_count = 6 if second else 5
    operands = refs[2 : 2 + operand_count]
    sketch_ref = refs[2 + operand_count]
    outputs = refs[3 + operand_count : -9]
    (
        left_ref,
        right_ref,
        two_ref,
        sample_ref,
        gram_ref,
        inverse_ref,
        rows_ref,
        square_ref,
        in_semaphores,
    ) = refs[-9:]
    send, keep, norm_ref, *extras = outputs
    count, kept, double = sample_ref.shape
    width = double // 2
    plans = second_plans if second else first_plans
    run_by_parity(*plans(first_of, count, half, early, operands, left_ref, right_ref), in_semaphores)

    parity = lax.rem(lax.axis_index("chain"), 2)
    is_even = parity == 0
    first = lax.axis_index("block") * sectors + jnp.where(is_even, *first_of)
    bond = parity if second else 1 - parity
    total = table.shape[1]

    def size_of(row, sector):
        return table[row, sector].astype(jnp.int32)


    def left_size(sector):
        at = jnp.clip(sector, 0, total - 1)
        return jnp.where(is_even, size_of(0, at), partner_sizes[0, 0, at])

    def middle_size(sector):
        at = jnp.clip(sector, 0, total - 1)
        size = size_of(jnp.where(is_even, 1, 0), at)
        return jnp.where(sector < total, size, 0)

    def right_size(sector):
        at = jnp.clip(sector, 0, total - 1)
        size = jnp.where(is_even, partner_sizes[0, 1, at], size_of(1, at))
        return jnp.where(sector < total, size, 0)

    row_index = lax.broadcasted_iota(jnp.int32, (kept, 1), 0)
    eye = (
        lax.broadcasted_iota(jnp.int32, (kept, kept), 0)
        == lax.broadcasted_iota(jnp.int32, (kept, kept), 1)
    )
    block_row = lax.broadcasted_iota(jnp.int32, (width, width), 0)
    block_column = lax.broadcasted_iota(jnp.int32, (width, width), 1)
    column = lax.broadcasted_iota(jnp.int32, (1, width), 1)

    def left(m, s, sector):
        if second:
            return left_ref[m, :, s * width : (s + 1) * width]
        inside = (column < middle_size(sector + s)).astype(jnp.float32).astype(jnp.bfloat16)
        return left_ref[m, s] * inside

    def right(m, s):
        if second:
            return right_ref[m, :, s * width : (s + 1) * width]
        return right_ref[m, s]

    def product(a, b):
        rounded = dot(a, b, LAST if second else PLAIN).astype(jnp.bfloat16)
        return rounded.astype(jnp.float32)

    def put(m, rows, columns, value, row_limit, column_limit):
        if not second:
            value = jnp.where(
                (block_row < row_limit) & (block_column < column_limit), value, 0.0
            )
        two_ref[m, rows, columns] = value.astype(jnp.bfloat16)

    w_empty, w_stay, w_swap, w_full = gate_terms(
        *(jnp.full((1, width), table[4 + bond, term], jnp.float32) for term in range(3))
    )

    @pl.loop(0, count, unroll=min(UNROLL, count))
    def _(m):
        sector = first + m
        below_zero, below_one = left(m, 0, sector - 1), left(m, 1, sector - 1)
        here_zero, here_one = left(m + 1, 0, sector), left(m + 1, 1, sector)
        same_zero, same_one = right(m, 0), right(m, 1)
        next_zero, next_one = right(m + 1, 0), right(m + 1, 1)
        low, high = slice(0, width), slice(width, double)
        rows_low, rows_high = left_size(sector), left_size(sector - 1)
        columns_low, columns_high = right_size(sector), right_size(sector + 1)
        put(m, low, low, w_empty * product(here_zero, same_zero), rows_low, columns_low)
        put(
            m,
            low,
            high,
            w_stay * product(here_zero, next_one) + w_swap * product(here_one, next_zero),
            rows_low,
            columns_high,
        )
        put(
            m,
            high,
            low,
            w_swap * product(below_zero, same_one) + w_stay * product(below_one, same_zero),
            rows_high,
            columns_low,
        )
        put(m, high, high, w_full * product(below_one, next_one), rows_high, columns_high)
        sample = dot(sketch_ref[...], two_ref[m], LAST)
        keep_rows = row_index < size_of(2 + bond, sector)
        sample = jnp.where(keep_rows, sample, 0.0)
        sample_ref[m] = sample
        high_part, middle_part, low_part = in_parts(sample)
        cross = dot(high_part, middle_part, LAST) + dot(high_part, low_part, LAST)
        gram = dot(high_part, high_part, LAST) + (
            dot(middle_part, middle_part, LAST) + (cross + jnp.transpose(cross))
        )
        gram_ref[m] = gram + jnp.where(eye & jnp.logical_not(keep_rows), 1.0, 0.0)

    lane = lax.broadcasted_iota(jnp.int32, (1, kept), 1)
    def eliminate(tile, first, below):
        here = pl.ds(first, PANEL)
        stop = first + PANEL
        for m in range(count):
            for half in range(kept // LANES):
                span = slice(half * LANES, (half + 1) * LANES)
                rows_ref[half, pl.ds(m, PANEL, stride=SUB), :] = gram_ref[m, here, span]
        factor_panel(rows_ref, first, tile)
        for m in range(count):
            solved = jnp.concatenate(
                [
                    rows_ref[half, pl.ds(m, PANEL, stride=SUB), :]
                    for half in range(kept // LANES)
                ],
                axis=1,
            )
            inverse_ref[m, here, :] = jnp.where(lane < stop, solved, 0.0)
            if below.start == kept:
                continue
            high, middle, low = in_parts(solved)
            one = jnp.concatenate([high, high, middle, middle, high, low], axis=0)[:, below]
            two = jnp.concatenate([high, middle, high, middle, low, high], axis=0)
            change = dot(one, two, FIRST)
            kept_part = jnp.where((lane >= first) & (lane < stop), 0.0, gram_ref[m, below, :])
            gram_ref[m, below, :] = kept_part - change

    for tile in range(kept // LANES):
        if second and late:
            for first in range(tile * LANES, (tile + 1) * LANES, PANEL):
                stop = first + PANEL
                eliminate(tile, first, slice(stop - stop % LANES, kept))
        else:

            @pl.loop(0, LANES // PANEL)
            def _(panel, tile=tile):
                first = pl.multiple_of(tile * LANES + panel * PANEL, PANEL)
                eliminate(tile, first, slice(tile * LANES, kept))

    square_ref[...] = jnp.zeros_like(square_ref)

    @pl.loop(0, count, unroll=min(UNROLL, count))
    def _(m):
        inverse_high, inverse_middle, _ = in_parts(inverse_ref[m])
        sample_high, sample_middle, _ = in_parts(sample_ref[m])
        solved = dot(inverse_high, sample_high, PLAIN) + (
            dot(inverse_high, sample_middle, PLAIN) + dot(inverse_middle, sample_high, PLAIN)
        )
        solved = solved * math.sqrt(width)
        basis = solved.astype(jnp.bfloat16)
        coef = dot(basis, two_ref[m], PLAIN)
        square_ref[...] += jnp.sum(coef * coef, axis=0, keepdims=True)
        if second:
            for s in range(2):
                span = slice(s * width, (s + 1) * width)
                turned = jnp.transpose(solved[:, span])
                send[m, s] = jnp.where(is_even, turned, coef[:, span]).astype(jnp.bfloat16)
                keep[m, s] = jnp.where(is_even, coef[:, span], turned).astype(jnp.bfloat16)
        else:
            send[m] = jnp.where(is_even, coef, solved).astype(jnp.bfloat16)
            keep[m] = jnp.where(is_even, solved, coef).astype(jnp.bfloat16)

    norm_ref[0] = jnp.sum(square_ref[...])
    if second:
        if extras:
            extras[0][0] = send[0, 1]
    else:
        at = jnp.where(is_even, count - 1, 0) if late else jnp.where(is_even, 0, count - 1)
        extras[0][0] = send[at] if late else keep[at]


def pair_update(second, late, table, partner_sizes, operands, sketch_turned):
    kept, double = sketch_turned.shape
    width = double // 2
    sectors = table.shape[1] // lax.axis_size("block")
    half = sectors // 2
    early, next_early = chunk_sizes(half)
    part = next_early if second else early
    count = half - part if late else part
    block = (2, width, kept) if second else (kept, double)
    extra = [(1, kept, double)]
    if second:
        extra = [(1, width, kept)] if not late or next_early == 0 else []
    left_shape = (count + 1, kept, double) if second else (count + 1, 2, width, width)
    vmem = pl.BlockSpec(memory_space=pltpu.VMEM)
    smem = pl.BlockSpec(memory_space=pltpu.SMEM)
    anywhere = pl.BlockSpec(memory_space=pl.ANY)

    def kernel(*refs):
        pair_kernel(second, late, sectors, refs)

    return pl.pallas_call(
        kernel,
        out_shape=[
            jax.ShapeDtypeStruct((count, *block), jnp.bfloat16),
            jax.ShapeDtypeStruct((count, *block), jnp.bfloat16),
            jax.ShapeDtypeStruct((1,), jnp.float32),
            *(jax.ShapeDtypeStruct(shape, jnp.bfloat16) for shape in extra),
        ],
        in_specs=[smem] * 2 + [anywhere] * len(operands) + [vmem],
        out_specs=[vmem, vmem, smem] + [vmem] * len(extra),
        scratch_shapes=[
            pltpu.VMEM(left_shape, jnp.bfloat16),
            pltpu.VMEM(left_shape, jnp.bfloat16),
            pltpu.VMEM((count, double, double), jnp.bfloat16),
            pltpu.VMEM((count, kept, double), jnp.float32),
            pltpu.VMEM((count, kept, kept), jnp.float32),
            pltpu.VMEM((count, kept, kept), jnp.float32),
            pltpu.VMEM((kept // LANES, PANEL * SUB, LANES), jnp.float32),
            pltpu.VMEM((1, double), jnp.float32),
            pltpu.SemaphoreType.DMA((8,)),
        ],
        compiler_params=pltpu.CompilerParams(vmem_limit_bytes=32 * 2**20),
        cost_estimate=pl.CostEstimate(
            flops=(count + 12) * 50 * kept * double * double,
            bytes_accessed=8 * count * kept * double * 2,
            transcendentals=0,
        ),
    )(table, partner_sizes, *operands, sketch_turned)


def place_kernel(last, half, target, norm_refs, refs):
    _, early = chunk_sizes(half)
    late, sectors = half - early, 2 * half
    if last:
        returned_late, _, out, buffer, in_semaphores, out_semaphores = refs
        even_line = [(returned_late, half, late)]
        odd_line = [(returned_late, early, late)]
        lower_line = []
    else:
        if early:
            keep_late, lower, keep_early, returned_early = refs[:4]
            even_line = [(keep_early, 0, early), (keep_late, early, late), (returned_early, sectors - early, early)]
            odd_line = [(returned_early, 0, early), (keep_late, half, late), (keep_early, sectors - early, early)]
        else:
            keep_late, lower = refs[:2]
            even_line, odd_line = [(keep_late, 0, late)], [(keep_late, half, late)]
        lower_line = [(whole(lower), sectors, 1)]
        out, buffer, in_semaphores, out_semaphores = refs[-4:]
    site = out.at[0]
    zero_line = [(plane(ref, 0), start, size) for ref, start, size in odd_line]
    one_line = [(plane(ref, 1), start, size) for ref, start, size in odd_line]
    odd = cut(zero_line, 0, sectors, plane(site, 0))
    odd += cut(one_line + lower_line, 1, sectors, plane(site, 1))
    parts = even_line
    is_even = lax.rem(lax.axis_index("chain"), 2) == 0

    @pl.when(jnp.logical_not(is_even))
    def _():
        run_copies(odd, out_semaphores)

    @pl.when(is_even)
    def _():
        norms, from_left, direct = norm_refs
        rows = (1, buffer.shape[-1])
        norm_even = jnp.full(rows, from_left[0] + direct[0], jnp.float32)
        norm_odd = jnp.full(rows, norms[1] + from_left[1], jnp.float32)
        scale_even = jnp.sqrt(target / norm_even)
        scale = scale_even * jnp.sqrt(target / (scale_even * scale_even * norm_odd))
        coming, going, filled = [], [], 0
        for index, (source, start, size) in enumerate(parts):
            room = buffer.at[pl.ds(filled, size)]
            coming.append(pltpu.make_async_copy(source, room, in_semaphores.at[index]))
            going.append(
                pltpu.make_async_copy(room, out.at[0, pl.ds(start, size)], out_semaphores.at[index])
            )
            filled += size
        for copy in coming:
            copy.start()
        filled = 0
        for index, (source, start, size) in enumerate(parts):
            coming[index].wait()

            @pl.loop(filled, filled + size)
            def _(sector):
                for s in range(2):
                    scaled = buffer[sector, s].astype(jnp.float32) * scale
                    buffer[sector, s] = scaled.astype(jnp.bfloat16)

            going[index].start()
            filled += size
        for copy in going:
            copy.wait()


def place(last, half, target, norms, operands, site):
    anywhere = pl.BlockSpec(memory_space=pl.ANY)
    _, early = chunk_sizes(half)
    rows = half - early if last else half + early

    def kernel(*refs):
        place_kernel(last, half, target, refs[:3], refs[3:])

    return pl.pallas_call(
        kernel,
        out_shape=jax.ShapeDtypeStruct(site.shape, site.dtype),
        in_specs=[pl.BlockSpec(memory_space=pltpu.SMEM)] * 3 + [anywhere] * len(operands),
        out_specs=anywhere,
        scratch_shapes=[
            pltpu.VMEM((rows, *site.shape[2:]), site.dtype),
            pltpu.SemaphoreType.DMA((3,)),
            pltpu.SemaphoreType.DMA((7,)),
        ],
        input_output_aliases={4: 0} if last else {},
        compiler_params=pltpu.CompilerParams(vmem_limit_bytes=16 * 2**20),
        cost_estimate=pl.CostEstimate(
            flops=0, bytes_accessed=2 * rows * site.size // site.shape[1] * 2, transcendentals=0
        ),
    )(*norms, *operands)


def move(value, target_of):
    sites, parts = lax.axis_size("chain"), lax.axis_size("block")
    pairs = []
    for site in range(sites):
        for part in range(parts):
            target = target_of(site, part)
            if target is not None and 0 <= target[1] < parts:
                pairs.append((site * parts + part, (target[0] % sites) * parts + target[1]))
    return lax.ppermute(value, ("chain", "block"), pairs)


def by_parity(even_target, odd_target):
    return lambda c, b: even_target(c, b) if c % 2 == 0 else odd_target(c, b)


def nowhere(c, b):
    return None


def joined(*parts):
    return jnp.concatenate(parts, axis=0)


def body(site_tensors, sketch, bond_sizes, kept_ranks, couplings):
    sectors = site_tensors.shape[1]
    half = sectors // 2
    early, next_early = chunk_sizes(half)
    width = site_tensors.shape[-1]
    kept = sketch.shape[1]
    parts = lax.axis_size("block")
    is_even = lax.axis_index("chain") % 2 == 0
    own = site_tensors[0]
    sketch_turned = jnp.transpose(sketch)

    terms = jnp.pad(couplings[0], ((0, 0), (0, bond_sizes.shape[2] - couplings.shape[2])))
    table = joined(
        bond_sizes[0].astype(jnp.float32), kept_ranks[0].astype(jnp.float32), terms
    )

    def pick(even_value, odd_value):
        return jnp.where(is_even, even_value, odd_value)

    def update(second, late, *operands):
        return pair_update(
            second, late, table, partner_sizes, operands, sketch_turned
        )

    across = by_parity(lambda c, b: (c + 1, b), lambda c, b: (c - 1, b))
    got_early = move(pick(own[sectors - early - 1 :], own[: early + 1]), across)
    partner_sizes = move(bond_sizes, across)
    edge = move(
        pick(own[-1:], own[:1]), by_parity(lambda c, b: (c, b + 1), lambda c, b: (c, b - 1))
    )
    corner = move(own[-1:, 1], by_parity(nowhere, lambda c, b: (c - 1, b + 1)))
    sent = pick(own[half - 1 : sectors - early - 1], own[early + 1 : half + 1])
    own_early = pick(own[: early + 1], own[sectors - early - 1 :])
    own_late = pick(own[early - 1 : half + 1], own[half - 1 : sectors - early + 1])
    sent, got_early = lax.optimization_barrier((sent, got_early))
    got_late = move(sent, across)
    send_early, keep_early, norm_early, halo_early = update(
        False, False, own_early, got_early, got_early, edge, corner
    )

    along = by_parity(lambda c, b: (c + 2, b), lambda c, b: (c - 2, b))
    far = move(
        halo_early, by_parity(lambda c, b: (c - 1, b - 1), lambda c, b: (c + 1, b + 1))
    )
    carried_early = move(send_early, along)
    send_late, keep_late, norm_late, halo_late = update(
        False, True, own_late, got_early, got_late, edge, corner
    )
    norm_even = norm_early + norm_late
    carried_late = move(send_late, along)
    near = move(halo_late, across)

    back = by_parity(lambda c, b: (c - 1, b), lambda c, b: (c + 1, b))
    norm_odd = 0.0
    first_parts = ()
    if next_early:
        send_early, kept_early, norm_early, lower_first = update(
            True, False, keep_early, keep_early, carried_early, carried_early, far, far
        )
        norm_odd = norm_early
        send_early, carried_late = lax.optimization_barrier((send_early, carried_late))
        returned_early = move(send_early, back)
        first_parts = (kept_early, returned_early)
    send_late, kept_late, norm_late, *lower = update(
        True, True, keep_early, keep_late, carried_early, carried_late, far, near
    )
    if next_early == 0:
        lower_first = lower[0]
    lower_above = move(lower_first, by_parity(lambda c, b: (c - 1, b - 1), nowhere))
    if next_early:
        send_late, returned_early, lower_above = lax.optimization_barrier(
            (send_late, returned_early, lower_above)
        )
        first_parts = (kept_early, returned_early)
    returned_late = move(send_late, back)

    norms = lax.psum(joined(norm_even, norm_odd + norm_late), "block")
    hops = {1: 2, 3: -1}
    passed = move(norms, lambda c, b: (c + hops[c % 4], b) if c % 2 else None)
    direct = move(norms, lambda c, b: (c + 2, b) if c % 4 == 0 else None)
    mine = (lax.axis_index("chain") % 4 == 2) & (jnp.arange(2) == 0)
    hops_on = {3: -1, 2: 2}
    from_left = move(
        passed + jnp.where(mine, norms, 0.0),
        lambda c, b: (c + hops_on[c % 4], b) if c % 4 in hops_on else None,
    )
    target = float(sectors * parts * kept * width)
    norms = (norms, from_left, direct)

    ready = (kept_late, lower_above, *first_parts)
    site = place(False, half, target, norms, ready, site_tensors)
    return place(True, half, target, norms, (returned_late, site), site_tensors)


def solution(mesh):
    placed = (
        P("chain", "block", None, None, None),
        P(),
        P("chain", None, None),
        P("chain", None, None),
        P("chain", None, None),
    )
    return jax.shard_map(
        body,
        mesh=mesh,
        in_specs=placed,
        out_specs=P("chain", "block", None, None, None),
        check_vma=False,
    )
```
